128 devices in a mesh: row: 8 (over z_hi, y), col: 16 (over z_lo, x, core).
Axes of the slice: x: 4, y: 4, z: 4 (z_hi: 2, z_lo: 2; z = z_hi * 2 + z_lo), core: 2. Of those that a mesh axis runs over, the one named last changes fastest.
Arguments:
- query_vectors: bfloat16 [32, 1536, 128], P('row', 'col'), may hold values from -6.5 to 6.5
- key_vectors: bfloat16 [32, 1536, 128], P('row', 'col'), may hold values from -6.5 to 6.5
- value_vectors: bfloat16 [32, 1536, 128], P('row', 'col'), may hold values from -6 to 6
- gate_logits: bfloat16 [32, 1536, 128], P('row', 'col'), may hold values from -6 to 6
- pair_bias: bfloat16 [4, 1536, 1536], P(None, 'col'), may hold values from -6 to 6
- pair_mask: int32 [32, 1536], P('row', 'col'), may hold values 0 or 1
- output_weight: bfloat16 [128, 128], replicated, may hold values from -0.5 to 0.5
- output_cotangent: bfloat16 [32, 128, 1536], P('row', 'col'), may hold values from -48 to 48
Outputs:
- query_gradient: bfloat16 [32, 1536, 128], P('row', 'col')
- key_gradient: bfloat16 [32, 1536, 128], P('row', 'col')
- value_gradient: bfloat16 [32, 1536, 128], P('row', 'col')
- gate_gradient: bfloat16 [32, 1536, 128], P('row', 'col')
- bias_gradient: float32 [4, 1536, 1536], P(None, 'col', 'row')
The draws below stay inside these ranges and needn't reach their ends.
All inputs are finite; a program needn't handle non-finite values. No bound on the sum of `pair_mask` on one device may be relied on, other than what follows from the above.
Results may differ from the reference program's by a relative error of at most 0.025.
Values may be sent and summed in bfloat16 or wider, within the bound.
No kernel may reach another device: no remote copies, remote signals or barrier semaphores. Data moves between devices by JAX's collectives and lax.ppermute only.
A program may use at most 64 MiB of HBM per device.

```python
import math
import jax
import jax.numpy as jnp
from jax import lax

HEADS = 4
HEAD_W = 32
PAIR_W = 128
N_TOK = 1536
J_TOTAL = 32


def rough_field(key, salt, scale_low, scale_high):
    noise_key, scale_key = jax.random.split(jax.random.fold_in(key, salt))
    channel_count = HEADS * HEAD_W
    entries = jax.random.normal(noise_key, (J_TOTAL, N_TOK, channel_count), jnp.float32)
    scales = jnp.exp(jax.random.uniform(scale_key, (J_TOTAL, N_TOK, 1), jnp.float32, math.log(scale_low), math.log(scale_high)))
    return jnp.clip(entries * scales, -6.0, 6.0)


def draw_query_vectors(key, part):
    entries = rough_field(key, 3, 0.5, 2.0)
    return entries.astype(jnp.bfloat16)


def draw_key_vectors(key, part):
    entries = rough_field(key, 5, 0.35, 3.5)
    return entries.astype(jnp.bfloat16)


def touch_ends(values, key, low, largest):
    longest = values.shape.index(max(values.shape))
    spots = []
    for shift in (0, 1):
        where = [jax.random.randint(jax.random.fold_in(key, axis), (), 0, length) for axis, length in enumerate(values.shape)]
        where[longest] = (where[longest] + shift) % values.shape[longest]
        spots.append(tuple(where))
    return values.at[spots[0]].set(low).at[spots[1]].set(largest)


def steps_of(own_key, extent, shards, smallest, high):
    loudness = 1.0
    for dim, parts in shards:
        draws = jax.random.uniform(jax.random.fold_in(jax.random.fold_in(own_key, 6), dim), (parts,), jnp.float32, smallest / len(shards), high / len(shards))
        loudness = loudness * jnp.repeat(jnp.exp(draws), extent[dim] // parts).reshape((-1,) + (1,) * (len(extent) - 1 - dim))
    return loudness


def bell_draw(stream_key, extent, width, limit, cuts=(), dtype=jnp.bfloat16):
    factor_of = steps_of(stream_key, extent, cuts, -0.22, 0.18) if cuts else 1.0
    array = jax.random.normal(stream_key, extent, jnp.float32) * width * factor_of
    return jnp.minimum(jnp.maximum(array, -limit), limit).astype(dtype)


def setup_inputs(seed: int = 0) -> dict:
    arg_keys = jax.random.split(jax.random.key(seed), 9)
    query_vectors = draw_query_vectors(jax.random.fold_in(arg_keys[8], 71), 0)
    key_vectors = draw_key_vectors(jax.random.fold_in(arg_keys[8], 71), 0)
    value_vectors = bell_draw(arg_keys[2], (J_TOTAL, N_TOK, HEADS * HEAD_W), 1.0, 6.0, ((0, 8), (1, 16)))
    gate_logits = bell_draw(arg_keys[3], (J_TOTAL, N_TOK, HEADS * HEAD_W), 1.0, 6.0, ((0, 8), (1, 16)))
    pair_bias = bell_draw(arg_keys[4], (HEADS, N_TOK, N_TOK), 1.0, 6.0, ((1, 16),))
    pair_mask = touch_ends((jax.random.randint(arg_keys[5], (J_TOTAL, N_TOK), 0, 8) < 7).astype(jnp.int32), jax.random.fold_in(arg_keys[5], 1), 0, 1)
    output_weight = bell_draw(arg_keys[6], (HEADS * HEAD_W, PAIR_W), (HEADS * HEAD_W) ** -0.5, 0.5)
    output_cotangent = jnp.clip(jax.random.uniform(arg_keys[7], (J_TOTAL, PAIR_W, N_TOK), jnp.float32, -48.0, 48.0) * steps_of(arg_keys[7], (J_TOTAL, PAIR_W, N_TOK), ((0, 8), (1, 16)), -0.4, 0.0), -48.0, 48.0).astype(jnp.bfloat16)
    return {"query_vectors": query_vectors, "key_vectors": key_vectors, "value_vectors": value_vectors, "gate_logits": gate_logits, "pair_bias": pair_bias, "pair_mask": pair_mask, "output_weight": output_weight, "output_cotangent": output_cotangent}


NEG_FILL = -1000000000.0

def to_heads(matrix, head_width):
    return jnp.transpose(matrix.astype(jnp.float32).reshape(matrix.shape[0], HEADS, head_width), (1, 0, 2))

def from_heads(tensor):
    return jnp.transpose(tensor, (1, 0, 2)).reshape(tensor.shape[1], tensor.shape[0] * tensor.shape[2])

def rounded(operand):
    return lax.optimization_barrier(operand.astype(jnp.bfloat16)).astype(jnp.float32)

def reference(query_vectors, key_vectors, value_vectors, gate_logits, pair_bias, pair_mask, output_weight, output_cotangent):
    head_width = query_vectors.shape[2] // HEADS
    scaling = 1.0 / math.sqrt(head_width)
    bias_full = pair_bias.astype(jnp.float32)
    highest = lax.Precision.HIGHEST

    def column(bias_total, pieces):
        query_column, key_column, value_column, gate_column, mask_column, cotangent_column = pieces
        query_heads = to_heads(query_column, head_width)
        key_heads = to_heads(key_column, head_width)
        value_heads = to_heads(value_column, head_width)
        raw_scores = jnp.einsum('hic,hkc->hik', query_heads, key_heads, precision=highest)
        scores = raw_scores * scaling + bias_full
        scores = jnp.where(mask_column[None, None, :] > 0, scores, NEG_FILL)
        row_max = lax.optimization_barrier(jnp.max(scores, axis=-1, keepdims=True))
        log_total = row_max + jnp.log(lax.optimization_barrier(jnp.sum(jnp.exp(scores - row_max), axis=-1, keepdims=True)))
        attention = jnp.exp(scores - log_total)
        attended_heads = jnp.einsum('hik,hkc->hic', attention, value_heads, precision=highest)
        attended = from_heads(attended_heads)
        gated_grad = jnp.dot(cotangent_column.T, output_weight.T, preferred_element_type=jnp.float32)
        gate_sigma = jax.nn.sigmoid(gate_column.astype(jnp.float32))
        gate_gradient = (gated_grad * attended * gate_sigma * (1.0 - gate_sigma)).astype(jnp.bfloat16)
        attended_grad = (gated_grad * gate_sigma).astype(jnp.bfloat16)
        grad_heads = to_heads(attended_grad, head_width)
        row_delta = lax.optimization_barrier(jnp.sum(grad_heads * attended_heads, axis=-1, keepdims=True))
        attention_grad = jnp.einsum('hic,hkc->hik', grad_heads, value_heads, precision=highest)
        score_grad = attention * (attention_grad - row_delta)
        score_low = rounded(score_grad)
        attention_low = rounded(attention)
        query_gradient = scaling * jnp.einsum('hik,hkc->hic', score_low, key_heads, precision=highest)
        key_gradient = scaling * jnp.einsum('hik,hic->hkc', score_low, query_heads, precision=highest)
        value_gradient = jnp.einsum('hik,hic->hkc', attention_low, grad_heads, precision=highest)
        outputs = (from_heads(query_gradient).astype(jnp.bfloat16), from_heads(key_gradient).astype(jnp.bfloat16), from_heads(value_gradient).astype(jnp.bfloat16), gate_gradient)
        return (bias_total + score_grad, outputs)
    bias_start = jnp.zeros(pair_bias.shape, jnp.float32)
    bias_total, outputs = lax.scan(column, bias_start, (query_vectors, key_vectors, value_vectors, gate_logits, pair_mask, output_cotangent))
    return (outputs[0], outputs[1], outputs[2], outputs[3], bias_total)
```

```python
import math

import jax
import jax.numpy as jnp
from jax import lax
from jax.experimental import pallas as pl
from jax.experimental.pallas import tpu as pltpu
from jax.sharding import PartitionSpec as P

HEADS = 4
NEG_FILL = -1000000000.0
LOG2E = math.log2(math.e)
CHUNK = 16


def attention_kernel(qd_ref, kv_ref, bias_ref, mask_ref, qa_ref, dkv_ref, dbias_ref, s_ref, b2_ref, acc_ref, de_ref, row_ref):
    step = pl.program_id(0)
    last = pl.num_programs(0) - 1
    rows = bias_ref.shape[0]
    queries = rows // 2
    keys = bias_ref.shape[1]
    head_width = qd_ref.shape[2] // 4
    scaling = 1.0 / math.sqrt(head_width)

    @pl.when(step == 0)
    def _():
        def fill(index, carry):
            part = pl.ds(index * CHUNK, CHUNK)
            b2_ref[part, :] = bias_ref[part, :].astype(jnp.float32) * LOG2E
            acc_ref[part, :] = jnp.zeros((CHUNK, keys), jnp.float32)
            return carry

        lax.fori_loop(0, rows // CHUNK, fill, 0)

    kv = kv_ref[...].reshape(keys, 4 * head_width)
    qd = qd_ref[0]
    lane = lax.broadcasted_iota(jnp.int32, (queries, 4 * head_width), 1)
    zero = jnp.zeros_like(qd)

    def only(part):
        return jnp.where((lane >= part * head_width) & (lane < (part + 1) * head_width), qd, zero)

    query_rows = jnp.concatenate([only(0), only(1)], axis=0)
    grad_rows = jnp.concatenate([only(2), only(3)], axis=0)
    transposed = (((1,), (1,)), ((), ()))
    s_ref[...] = lax.dot_general(query_rows, kv, transposed, preferred_element_type=jnp.float32)
    cap = jnp.where(mask_ref[0] > 0.5, 1e30, NEG_FILL * LOG2E)

    def soften(index, carry):
        part = pl.ds(index * CHUNK, CHUNK)
        scores = jnp.minimum(s_ref[part, :] * (scaling * LOG2E) + b2_ref[part, :], cap)
        weights = jnp.exp2(scores - jnp.max(scores, axis=1, keepdims=True))
        row_ref[part, :] = jnp.broadcast_to(jnp.sum(weights, axis=1, keepdims=True), (CHUNK, 128))
        de_ref[pl.ds(rows + index * CHUNK, CHUNK), :] = weights.astype(jnp.bfloat16)
        return carry

    lax.fori_loop(0, rows // CHUNK, soften, 0)
    weights_low = de_ref[rows:, :]
    inverse = 1.0 / row_ref[...]
    attended = jnp.dot(weights_low, kv, preferred_element_type=jnp.float32) * inverse
    grad_wide = grad_rows.astype(jnp.float32)
    delta = jnp.sum(grad_wide * attended, axis=1, keepdims=True)
    row_ref[...] = delta * inverse
    grad_scaled = (grad_wide * inverse).astype(jnp.bfloat16)
    s_ref[...] = lax.dot_general(grad_scaled, kv, transposed, preferred_element_type=jnp.float32)

    def backward(index, carry):
        part = pl.ds(index * CHUNK, CHUNK)
        weights = de_ref[pl.ds(rows + index * CHUNK, CHUNK), :].astype(jnp.float32)
        score_grad = weights * (s_ref[part, :] - row_ref[part, :1])
        acc_ref[part, :] += score_grad
        de_ref[part, :] = score_grad.astype(jnp.bfloat16)
        return carry

    lax.fori_loop(0, rows // CHUNK, backward, 0)
    query_part = jnp.dot(de_ref[:rows, :], kv, preferred_element_type=jnp.float32) * scaling
    merged = jnp.where(
        lane < 2 * head_width,
        jnp.where(lane < head_width, query_part[:queries], query_part[queries:]),
        jnp.where(lane < 3 * head_width, attended[:queries], attended[queries:]),
    )
    qa_ref[0] = merged.astype(jnp.bfloat16)
    sides = jnp.concatenate([query_rows, grad_scaled], axis=0)
    key_value = lax.dot_general(
        sides, de_ref[...], (((0,), (0,)), ((), ())), preferred_element_type=jnp.float32
    )
    dkv_ref[...] = key_value.T.astype(jnp.bfloat16).reshape(dkv_ref.shape)

    @pl.when(step == last)
    def _():
        width = dbias_ref.shape[2]
        for piece in range(dbias_ref.shape[0]):
            dbias_ref[piece] = acc_ref[:, piece * width : (piece + 1) * width].astype(jnp.bfloat16)


def attend(query_grad, key_value, bias, mask, row_count):
    columns, queries, lanes = query_grad.shape
    groups = key_value.shape[0]
    keys = bias.shape[1]
    rows = bias.shape[0]
    width = keys // row_count
    work = columns * rows * keys
    return pl.pallas_call(
        attention_kernel,
        grid=(columns,),
        in_specs=[
            pl.BlockSpec((1, queries, lanes), lambda j: (j, 0, 0)),
            pl.BlockSpec((groups, 1, queries, lanes), lambda j: (0, j, 0, 0)),
            pl.BlockSpec((rows, keys), lambda j: (0, 0)),
            pl.BlockSpec((1, 1, keys), lambda j: (j, 0, 0)),
        ],
        out_specs=[
            pl.BlockSpec((1, queries, lanes), lambda j: (j, 0, 0)),
            pl.BlockSpec((groups, 1, queries, lanes), lambda j: (0, j, 0, 0)),
            pl.BlockSpec((row_count, rows, width), lambda j: (0, 0, 0)),
        ],
        out_shape=[
            jax.ShapeDtypeStruct((columns, queries, lanes), jnp.bfloat16),
            jax.ShapeDtypeStruct((groups, columns, queries, lanes), jnp.bfloat16),
            jax.ShapeDtypeStruct((row_count, rows, width), jnp.bfloat16),
        ],
        scratch_shapes=[
            pltpu.VMEM((rows, keys), jnp.float32),
            pltpu.VMEM((rows, keys), jnp.float32),
            pltpu.VMEM((rows, keys), jnp.float32),
            pltpu.VMEM((2 * rows, keys), jnp.bfloat16),
            pltpu.VMEM((rows, 128), jnp.float32),
        ],
        compiler_params=pltpu.CompilerParams(vmem_limit_bytes=48 * 1024 * 1024),
        cost_estimate=pl.CostEstimate(flops=12 * 128 * work, bytes_accessed=16 * 2**20, transcendentals=work),
        name="attention_both",
    )(query_grad, key_value, bias, mask)


def local(
    query_vectors,
    key_vectors,
    value_vectors,
    gate_logits,
    pair_bias,
    pair_mask,
    output_weight,
    output_cotangent,
):
    columns, tokens, channels = query_vectors.shape
    half = channels // 2
    devices = lax.axis_size("col")
    row_count = lax.axis_size("row")
    chips = devices // 2
    core = lax.axis_index("col") % 2
    scaling = 1.0 / math.sqrt(channels // HEADS)
    swap = [(index, index ^ 1) for index in range(devices)]
    chip_groups = [[2 * chip + side for chip in range(chips)] for side in range(2)]
    keys = pair_bias.shape[2]

    def mine_other(array, axis):
        size = array.shape[axis] // 2
        low = lax.slice_in_dim(array, 0, size, axis=axis)
        high = lax.slice_in_dim(array, size, 2 * size, axis=axis)
        return jnp.where(core == 0, low, high), jnp.where(core == 0, high, low)

    def in_order(mine, other, axis):
        return jnp.where(
            core == 0,
            jnp.concatenate([mine, other], axis=axis),
            jnp.concatenate([other, mine], axis=axis),
        )

    def swapped(array):
        return lax.ppermute(array, "col", swap)

    bias_mine, bias_other = mine_other(pair_bias, 0)
    bias_pair = in_order(bias_mine, swapped(bias_other), 1).reshape(-1, keys)

    key_mine, key_other = mine_other(key_vectors, 2)
    value_mine, value_other = mine_other(value_vectors, 2)
    kv_mine = jnp.concatenate([key_mine, value_mine], axis=2)
    kv_other = swapped(jnp.concatenate([key_other, value_other], axis=2))
    mask_low = pair_mask.astype(jnp.bfloat16)
    kv_chip = in_order(kv_mine, kv_other, 1)
    mask_chip = in_order(mask_low, swapped(mask_low), 1)
    mask_rows = jnp.pad(mask_chip.reshape(-1, channels), ((0, 2), (0, 0)))
    payload = jnp.concatenate([kv_chip.reshape(-1, channels), mask_rows], axis=0)
    payload = jnp.broadcast_to(payload[None], (chips,) + payload.shape)
    gathered = lax.all_to_all(payload, "col", 0, 0, tiled=True, axis_index_groups=chip_groups)
    key_value = gathered[:, : columns * 2 * tokens].reshape(chips, columns, 2 * tokens, channels)
    mask_all = gathered[:, columns * 2 * tokens : -2].reshape(chips, columns, 2 * tokens)
    mask_all = jnp.transpose(mask_all, (1, 0, 2)).reshape(columns, 1, keys).astype(jnp.float32)

    regrouped = lax.all_to_all(output_cotangent, "col", split_axis=2, concat_axis=1, tiled=True)
    gated_grad = jnp.einsum(
        "jdi,ed->jie", regrouped, output_weight, preferred_element_type=jnp.float32
    )
    gate_sigma = jax.nn.sigmoid(gate_logits.astype(jnp.float32))
    attended_grad = (gated_grad * gate_sigma).astype(jnp.bfloat16)
    query_mine, query_other = mine_other(query_vectors, 2)
    grad_mine, grad_other = mine_other(attended_grad, 2)
    qd_mine = jnp.concatenate([query_mine, grad_mine], axis=2)
    qd_other = swapped(jnp.concatenate([query_other, grad_other], axis=2))
    query_grad = in_order(qd_mine, qd_other, 1)

    query_attended, kv_grads, bias_grads = attend(query_grad, key_value, bias_pair, mask_all, row_count)

    kv_parts = lax.all_to_all(kv_grads, "col", 0, 0, tiled=True, axis_index_groups=chip_groups)
    kv_sum = jnp.sum(kv_parts.astype(jnp.float32), axis=0).astype(jnp.bfloat16)
    kv_own, kv_away = mine_other(kv_sum, 1)
    kv_back = swapped(kv_away)
    key_gradient = in_order(kv_own[..., :half], kv_back[..., :half], 2)
    key_gradient = (key_gradient.astype(jnp.float32) * scaling).astype(jnp.bfloat16)
    value_gradient = in_order(kv_own[..., half:], kv_back[..., half:], 2)

    qa_own, qa_away = mine_other(query_attended, 1)
    qa_back = swapped(qa_away)
    query_gradient = in_order(qa_own[..., :half], qa_back[..., :half], 2)
    attended = in_order(qa_own[..., half:], qa_back[..., half:], 2).astype(jnp.float32)
    gate_gradient = (gated_grad * attended * gate_sigma * (1.0 - gate_sigma)).astype(jnp.bfloat16)

    bias_parts = lax.all_to_all(bias_grads, "row", 0, 0, tiled=True)
    bias_sum = jnp.sum(bias_parts.astype(jnp.float32), axis=0).astype(jnp.bfloat16)
    bias_sum = bias_sum.reshape(2, 2 * tokens, keys // row_count)
    bias_own, bias_away = mine_other(bias_sum, 1)
    bias_gradient = in_order(bias_own, swapped(bias_away), 0).astype(jnp.float32)
    return (query_gradient, key_gradient, value_gradient, gate_gradient, bias_gradient)


def solution(mesh):
    placed = (
        P("row", "col", None),
        P("row", "col", None),
        P("row", "col", None),
        P("row", "col", None),
        P(None, "col", None),
        P("row", "col"),
        P(),
        P("row", "col", None),
    )
    return jax.shard_map(
        local,
        mesh=mesh,
        in_specs=placed,
        out_specs=(
            P("row", "col", None),
            P("row", "col", None),
            P("row", "col", None),
            P("row", "col", None),
            P(None, "col", "row"),
        ),
        check_vma=False,
    )
```

```python
import math

import jax
import jax.numpy as jnp
from jax import lax
from jax.experimental import pallas as pl
from jax.experimental.pallas import tpu as pltpu
from jax.sharding import PartitionSpec as P

HEADS = 4
NEG_FILL = -1000000000.0
LOG2E = math.log2(math.e)
CHUNK = 16
UNROLL = 12


def attention_kernel(qd_ref, kv_ref, bias_ref, mask_ref, qa_ref, dkv_ref, dbias_ref, s_ref, b2_ref, acc_ref, dp_ref, de_ref, row_ref):
    step = pl.program_id(0)
    last = pl.num_programs(0) - 1
    rows = bias_ref.shape[0]
    queries = rows // 2
    keys = bias_ref.shape[1]
    head_width = qd_ref.shape[2] // 4
    scaling = 1.0 / math.sqrt(head_width)

    @pl.when(step == 0)
    def _():
        def fill(index, carry):
            part = pl.ds(index * CHUNK, CHUNK)
            b2_ref[part, :] = bias_ref[part, :].astype(jnp.float32) * LOG2E
            acc_ref[part, :] = jnp.zeros((CHUNK, keys), jnp.float32)
            return carry

        lax.fori_loop(0, rows // CHUNK, fill, 0)

    kv = kv_ref[:, pl.ds(step * queries, queries), :].reshape(keys, 4 * head_width)
    qd = qd_ref[0]
    lane = lax.broadcasted_iota(jnp.int32, (queries, 4 * head_width), 1)
    zero = jnp.zeros_like(qd)

    def only(part):
        return jnp.where((lane >= part * head_width) & (lane < (part + 1) * head_width), qd, zero)

    transposed = (((1,), (1,)), ((), ()))
    cap = jnp.where(mask_ref[0] > 0.5, 1e30, NEG_FILL * LOG2E)
    query_rows = [only(0), only(1)]
    grad_rows = [only(2), only(3)]

    def scores_of(head):
        s_ref[head * queries : (head + 1) * queries, :] = lax.dot_general(
            query_rows[head], kv, transposed, preferred_element_type=jnp.float32
        )

    def soften(head):
        def one(index, carry):
            start = head * queries + index * CHUNK
            part = pl.ds(start, CHUNK)
            scores = jnp.minimum(s_ref[part, :] * (scaling * LOG2E) + b2_ref[part, :], cap)
            weights = jnp.exp2(scores - jnp.max(scores, axis=1, keepdims=True))
            row_ref[part, :] = jnp.broadcast_to(jnp.sum(weights, axis=1, keepdims=True), (CHUNK, 128))
            de_ref[pl.ds(rows + start, CHUNK), :] = weights.astype(jnp.bfloat16)
            return carry

        lax.fori_loop(0, queries // CHUNK, one, 0, unroll=UNROLL)

    def cotangents(head):
        part = slice(head * queries, (head + 1) * queries)
        weights_low = de_ref[rows + head * queries : rows + (head + 1) * queries, :]
        inverse = 1.0 / row_ref[part, :]
        attended = jnp.dot(weights_low, kv, preferred_element_type=jnp.float32) * inverse
        grad_wide = grad_rows[head].astype(jnp.float32)
        delta = jnp.sum(grad_wide * attended, axis=1, keepdims=True)
        row_ref[part, :] = delta * inverse
        grad_scaled = (grad_wide * inverse).astype(jnp.bfloat16)
        dp_ref[part, :] = lax.dot_general(grad_scaled, kv, transposed, preferred_element_type=jnp.float32)
        return attended, grad_scaled

    def backward(head):
        def one(index, carry):
            start = head * queries + index * CHUNK
            part = pl.ds(start, CHUNK)
            weights = de_ref[pl.ds(rows + start, CHUNK), :].astype(jnp.float32)
            score_grad = weights * (dp_ref[part, :] - row_ref[part, :1])
            acc_ref[part, :] += score_grad
            de_ref[part, :] = score_grad.astype(jnp.bfloat16)
            return carry

        lax.fori_loop(0, queries // CHUNK, one, 0, unroll=UNROLL)

    def query_of(head):
        return jnp.dot(
            de_ref[head * queries : (head + 1) * queries, :], kv, preferred_element_type=jnp.float32
        ) * scaling

    scores_of(0)
    scores_of(1)
    soften(0)
    att0, sc0 = cotangents(0)
    soften(1)
    att1, sc1 = cotangents(1)
    backward(0)
    q0 = query_of(0)
    backward(1)
    q1 = query_of(1)
    merged = jnp.where(
        lane < 2 * head_width,
        jnp.where(lane < head_width, q0, q1),
        jnp.where(lane < 3 * head_width, att0, att1),
    )
    qa_ref[0] = merged.astype(jnp.bfloat16)
    sides = jnp.concatenate(query_rows + [sc0, sc1], axis=0)
    key_value = lax.dot_general(
        sides, de_ref[...], (((0,), (0,)), ((), ())), preferred_element_type=jnp.float32
    )
    dkv_ref[...] = key_value.T.astype(jnp.bfloat16).reshape(dkv_ref.shape)

    @pl.when(step == last)
    def _():
        width = dbias_ref.shape[2]
        for piece in range(dbias_ref.shape[0]):
            dbias_ref[piece] = acc_ref[:, piece * width : (piece + 1) * width].astype(jnp.bfloat16)


def pack_kernel(cotangent_ref, packed_ref):
    width = cotangent_ref.shape[2] // packed_ref.shape[0]
    rows = packed_ref.shape[1]
    whole = cotangent_ref[...].astype(jnp.float32).reshape(rows, cotangent_ref.shape[2])
    filler = jnp.zeros((rows, packed_ref.shape[2] - width), jnp.float32)
    for piece in range(packed_ref.shape[0]):
        part = whole[:, piece * width : (piece + 1) * width]
        packed_ref[piece] = jnp.concatenate([part, filler], axis=1).astype(jnp.bfloat16)


def pack(cotangent, pieces):
    return pl.pallas_call(
        pack_kernel,
        out_shape=jax.ShapeDtypeStruct((pieces, cotangent.shape[0] * cotangent.shape[1], 128), jnp.bfloat16),
        name="pack_cotangent",
    )(cotangent)


def project_kernel(packed_ref, weight_ref, gate_ref, grad_ref, slope_ref):
    pieces, rows, lanes = packed_ref.shape
    columns, tokens, channels = gate_ref.shape
    whole = packed_ref[...].astype(jnp.float32).reshape(pieces, columns, rows // columns, lanes)
    for column in range(columns):
        part = whole[:, column].reshape(channels, lanes).astype(jnp.bfloat16)
        gated = jnp.dot(weight_ref[...], part, preferred_element_type=jnp.float32).T[:tokens]
        sigma = jax.nn.sigmoid(gate_ref[column].astype(jnp.float32))
        grad = gated * sigma
        grad_ref[column] = grad.astype(jnp.bfloat16)
        slope_ref[column] = grad * (1.0 - sigma)


def project(packed, weight, gate):
    return pl.pallas_call(
        project_kernel,
        out_shape=[
            jax.ShapeDtypeStruct(gate.shape, jnp.bfloat16),
            jax.ShapeDtypeStruct(gate.shape, jnp.float32),
        ],
        name="project_cotangent",
    )(packed, weight, gate)


def attend(query_grad, key_value, bias, mask, row_count):
    columns, queries, lanes = query_grad.shape
    groups = key_value.shape[0]
    keys = bias.shape[1]
    rows = bias.shape[0]
    width = keys // row_count
    work = columns * rows * keys
    return pl.pallas_call(
        attention_kernel,
        grid=(columns,),
        in_specs=[
            pl.BlockSpec((1, queries, lanes), lambda j: (j, 0, 0)),
            pl.BlockSpec((groups,) + key_value.shape[1:], lambda j: (0, 0, 0)),
            pl.BlockSpec((rows, keys), lambda j: (0, 0)),
            pl.BlockSpec((1, 1, keys), lambda j: (j, 0, 0)),
        ],
        out_specs=[
            pl.BlockSpec((1, queries, lanes), lambda j: (j, 0, 0)),
            pl.BlockSpec((groups, 1, queries, lanes), lambda j: (0, j, 0, 0)),
            pl.BlockSpec((row_count, rows, width), lambda j: (0, 0, 0)),
        ],
        out_shape=[
            jax.ShapeDtypeStruct((columns, queries, lanes), jnp.bfloat16),
            jax.ShapeDtypeStruct((groups, columns, queries, lanes), jnp.bfloat16),
            jax.ShapeDtypeStruct((row_count, rows, width), jnp.bfloat16),
        ],
        scratch_shapes=[
            pltpu.VMEM((rows, keys), jnp.float32),
            pltpu.VMEM((rows, keys), jnp.float32),
            pltpu.VMEM((rows, keys), jnp.float32),
            pltpu.VMEM((rows, keys), jnp.float32),
            pltpu.VMEM((2 * rows, keys), jnp.bfloat16),
            pltpu.VMEM((rows, 128), jnp.float32),
        ],
        compiler_params=pltpu.CompilerParams(vmem_limit_bytes=48 * 1024 * 1024),
        cost_estimate=pl.CostEstimate(flops=12 * 128 * work, bytes_accessed=16 * 2**20, transcendentals=work),
        name="attention_both",
    )(query_grad, key_value, bias, mask)


def local(
    query_vectors,
    key_vectors,
    value_vectors,
    gate_logits,
    pair_bias,
    pair_mask,
    output_weight,
    output_cotangent,
):
    columns, tokens, channels = query_vectors.shape
    half = channels // 2
    devices = lax.axis_size("col")
    row_count = lax.axis_size("row")
    chips = devices // 2
    core = lax.axis_index("col") % 2
    scaling = 1.0 / math.sqrt(channels // HEADS)
    swap = [(index, index ^ 1) for index in range(devices)]
    chip_groups = [[2 * chip + side for chip in range(chips)] for side in range(2)]
    keys = pair_bias.shape[2]

    def mine_other(array, axis):
        size = array.shape[axis] // 2
        low = lax.slice_in_dim(array, 0, size, axis=axis)
        high = lax.slice_in_dim(array, size, 2 * size, axis=axis)
        return jnp.where(core == 0, low, high), jnp.where(core == 0, high, low)

    def in_order(mine, other, axis):
        return jnp.where(
            core == 0,
            jnp.concatenate([mine, other], axis=axis),
            jnp.concatenate([other, mine], axis=axis),
        )

    def swapped(array):
        return lax.ppermute(array, "col", swap)

    bias_mine, bias_other = mine_other(pair_bias, 0)
    bias_pair = in_order(bias_mine, swapped(bias_other), 1).reshape(-1, keys)

    key_mine, key_other = mine_other(key_vectors, 2)
    value_mine, value_other = mine_other(value_vectors, 2)
    kv_mine = jnp.concatenate([key_mine, value_mine], axis=2)
    kv_other = swapped(jnp.concatenate([key_other, value_other], axis=2))
    mask_low = pair_mask.astype(jnp.bfloat16)
    kv_chip = in_order(kv_mine, kv_other, 1)
    mask_chip = in_order(mask_low, swapped(mask_low), 1)
    mask_rows = jnp.pad(mask_chip.reshape(-1, channels), ((0, 2), (0, 0)))
    payload = jnp.concatenate([kv_chip.reshape(-1, channels), mask_rows], axis=0)
    payload = jnp.broadcast_to(payload[None], (chips,) + payload.shape)
    gathered = lax.all_to_all(payload, "col", 0, 0, tiled=True, axis_index_groups=chip_groups)
    mask_all = gathered[:, columns * 2 * tokens : -2].reshape(chips, columns, 2 * tokens)
    mask_all = jnp.transpose(mask_all, (1, 0, 2)).reshape(columns, 1, keys).astype(jnp.float32)

    regrouped = lax.all_to_all(pack(output_cotangent, devices), "col", 0, 0, tiled=True)
    attended_grad, gate_slope = project(regrouped, output_weight, gate_logits)
    query_mine, query_other = mine_other(query_vectors, 2)
    grad_mine, grad_other = mine_other(attended_grad, 2)
    qd_mine = jnp.concatenate([query_mine, grad_mine], axis=2)
    qd_other = swapped(jnp.concatenate([query_other, grad_other], axis=2))
    query_grad = in_order(qd_mine, qd_other, 1)

    query_attended, kv_grads, bias_grads = attend(query_grad, gathered, bias_pair, mask_all, row_count)

    kv_parts = lax.all_to_all(kv_grads, "col", 0, 0, tiled=True, axis_index_groups=chip_groups)
    kv_sum = jnp.sum(kv_parts.astype(jnp.float32), axis=0).astype(jnp.bfloat16)
    kv_own, kv_away = mine_other(kv_sum, 1)
    kv_back = swapped(kv_away)
    key_gradient = in_order(kv_own[..., :half], kv_back[..., :half], 2)
    key_gradient = (key_gradient.astype(jnp.float32) * scaling).astype(jnp.bfloat16)
    value_gradient = in_order(kv_own[..., half:], kv_back[..., half:], 2)

    qa_own, qa_away = mine_other(query_attended, 1)
    qa_back = swapped(qa_away)
    query_gradient = in_order(qa_own[..., :half], qa_back[..., :half], 2)
    attended = in_order(qa_own[..., half:], qa_back[..., half:], 2).astype(jnp.float32)
    gate_gradient = (gate_slope * attended).astype(jnp.bfloat16)

    place = lax.axis_index("row")
    high_step = row_count // 2
    bias_sum = lax.dynamic_index_in_dim(bias_grads, place, 0, keepdims=False).astype(jnp.float32)
    for high in range(2):
        for low in range(high_step):
            if high or low:
                pairs = [
                    (index, ((index // high_step + high) % 2) * high_step + (index + low) % high_step)
                    for index in range(row_count)
                ]
                target = ((place // high_step + high) % 2) * high_step + (place + low) % high_step
                part = lax.dynamic_index_in_dim(bias_grads, target, 0, keepdims=False)
                bias_sum = bias_sum + lax.ppermute(part, "row", pairs).astype(jnp.float32)
    bias_sum = bias_sum.astype(jnp.bfloat16)
    bias_sum = bias_sum.reshape(2, 2 * tokens, keys // row_count)
    bias_own, bias_away = mine_other(bias_sum, 1)
    bias_gradient = in_order(bias_own, swapped(bias_away), 0).astype(jnp.float32)
    return (query_gradient, key_gradient, value_gradient, gate_gradient, bias_gradient)


def solution(mesh):
    placed = (
        P("row", "col", None),
        P("row", "col", None),
        P("row", "col", None),
        P("row", "col", None),
        P(None, "col", None),
        P("row", "col"),
        P(),
        P("row", "col", None),
    )
    return jax.shard_map(
        local,
        mesh=mesh,
        in_specs=placed,
        out_specs=(
            P("row", "col", None),
            P("row", "col", None),
            P("row", "col", None),
            P("row", "col", None),
            P(None, "col", "row"),
        ),
        check_vma=False,
    )
```

```python
import math

import jax
import jax.numpy as jnp
from jax import lax
from jax.experimental import pallas as pl
from jax.experimental.pallas import tpu as pltpu
from jax.sharding import PartitionSpec as P

HEADS = 4
NEG_FILL = -1000000000.0
LOG2E = math.log2(math.e)
CHUNK = 16
UNROLL = 12
MASK_ROWS = 16


def attention_kernel(
    place_ref,
    qd_ref,
    own_ref,
    left_ref,
    right_ref,
    across_ref,
    left_pair_ref,
    right_pair_ref,
    left_far_ref,
    right_far_ref,
    bias_ref,
    qa_ref,
    dkv_ref,
    dbias_ref,
    kv_ref,
    cap_ref,
    s_ref,
    b2_ref,
    acc_ref,
    dp_ref,
    de_ref,
    row_ref,
):
    step = pl.program_id(0)
    last = pl.num_programs(0) - 1
    rows = bias_ref.shape[0]
    queries = rows // 2
    keys = bias_ref.shape[1]
    head_width = qd_ref.shape[2] // 4
    scaling = 1.0 / math.sqrt(head_width)

    @pl.when(step == 0)
    def _():
        def fill(index, carry):
            part = pl.ds(index * CHUNK, CHUNK)
            b2_ref[part, :] = bias_ref[part, :].astype(jnp.float32) * LOG2E
            acc_ref[part, :] = jnp.zeros((CHUNK, keys), jnp.float32)
            return carry

        lax.fori_loop(0, rows // CHUNK, fill, 0)
        height = own_ref.shape[0]
        cut = left_far_ref.shape[0]
        kv_ref[place_ref[0]] = own_ref[...]
        kv_ref[place_ref[1]] = left_ref[...]
        kv_ref[place_ref[2]] = right_ref[...]
        kv_ref[place_ref[3], :cut] = left_pair_ref[height:]
        kv_ref[place_ref[3], cut:] = right_pair_ref[height:]
        kv_ref[place_ref[4]] = across_ref[...]
        kv_ref[place_ref[5]] = left_pair_ref[:height]
        kv_ref[place_ref[6]] = right_pair_ref[:height]
        kv_ref[place_ref[7], :cut] = left_far_ref[...]
        kv_ref[place_ref[7], cut:] = right_far_ref[...]
        first = height - MASK_ROWS
        masks = kv_ref[:, first:, :].astype(jnp.float32)
        for column in range(cap_ref.shape[0]):
            pieces = []
            for group in range(masks.shape[0]):
                pieces.append(masks[group, 2 * column : 2 * column + 1, :])
                pieces.append(masks[group, 2 * column + 1 : 2 * column + 2, : queries - 128])
            cap_ref[column] = jnp.where(
                jnp.concatenate(pieces, axis=1) > 0.5, 1e30, NEG_FILL * LOG2E
            )

    kv = kv_ref[:, pl.ds(step * queries, queries), :].reshape(keys, 4 * head_width)
    qd = qd_ref[0]
    lane = lax.broadcasted_iota(jnp.int32, (queries, 4 * head_width), 1)
    zero = jnp.zeros_like(qd)

    def only(part):
        return jnp.where((lane >= part * head_width) & (lane < (part + 1) * head_width), qd, zero)

    transposed = (((1,), (1,)), ((), ()))
    cap = cap_ref[step]
    query_rows = [only(0), only(1)]
    grad_rows = [only(2), only(3)]

    def scores_of(head):
        s_ref[head * queries : (head + 1) * queries, :] = lax.dot_general(
            query_rows[head], kv, transposed, preferred_element_type=jnp.float32
        )

    def soften(head):
        def one(index, carry):
            start = head * queries + index * CHUNK
            part = pl.ds(start, CHUNK)
            scores = jnp.minimum(s_ref[part, :] * (scaling * LOG2E) + b2_ref[part, :], cap)
            weights = jnp.exp2(scores - jnp.max(scores, axis=1, keepdims=True))
            row_ref[part, :] = jnp.broadcast_to(jnp.sum(weights, axis=1, keepdims=True), (CHUNK, 128))
            de_ref[pl.ds(rows + start, CHUNK), :] = weights.astype(jnp.bfloat16)
            return carry

        lax.fori_loop(0, queries // CHUNK, one, 0, unroll=UNROLL)

    def cotangents(head):
        part = slice(head * queries, (head + 1) * queries)
        weights_low = de_ref[rows + head * queries : rows + (head + 1) * queries, :]
        inverse = 1.0 / row_ref[part, :]
        attended = jnp.dot(weights_low, kv, preferred_element_type=jnp.float32) * inverse
        grad_wide = grad_rows[head].astype(jnp.float32)
        delta = jnp.sum(grad_wide * attended, axis=1, keepdims=True)
        row_ref[part, :] = delta * inverse
        grad_scaled = (grad_wide * inverse).astype(jnp.bfloat16)
        dp_ref[part, :] = lax.dot_general(grad_scaled, kv, transposed, preferred_element_type=jnp.float32)
        return attended, grad_scaled

    def backward(head):
        def one(index, carry):
            start = head * queries + index * CHUNK
            part = pl.ds(start, CHUNK)
            weights = de_ref[pl.ds(rows + start, CHUNK), :].astype(jnp.float32)
            score_grad = weights * (dp_ref[part, :] - row_ref[part, :1])
            acc_ref[part, :] += score_grad
            de_ref[part, :] = score_grad.astype(jnp.bfloat16)
            return carry

        lax.fori_loop(0, queries // CHUNK, one, 0, unroll=UNROLL)

    def query_of(head):
        return jnp.dot(
            de_ref[head * queries : (head + 1) * queries, :], kv, preferred_element_type=jnp.float32
        ) * scaling

    scores_of(0)
    scores_of(1)
    soften(0)
    att0, sc0 = cotangents(0)
    soften(1)
    att1, sc1 = cotangents(1)
    backward(0)
    q0 = query_of(0)
    backward(1)
    q1 = query_of(1)
    merged = jnp.where(
        lane < 2 * head_width,
        jnp.where(lane < head_width, q0, q1),
        jnp.where(lane < 3 * head_width, att0, att1),
    )
    qa_ref[0] = merged.astype(jnp.bfloat16)
    sides = jnp.concatenate(query_rows + [sc0, sc1], axis=0)
    key_value = lax.dot_general(
        sides, de_ref[...], (((0,), (0,)), ((), ())), preferred_element_type=jnp.float32
    )
    dkv_ref[...] = key_value.T.astype(jnp.bfloat16).reshape(dkv_ref.shape)

    @pl.when(step == last)
    def _():
        width = dbias_ref.shape[2]
        for piece in range(dbias_ref.shape[0]):
            part = acc_ref[:, piece * width : (piece + 1) * width]
            dbias_ref[place_ref[8 + piece]] = part.astype(jnp.bfloat16)


def pack_kernel(cotangent_ref, packed_ref):
    width = cotangent_ref.shape[2] // packed_ref.shape[0]
    rows = packed_ref.shape[1]
    whole = cotangent_ref[...].astype(jnp.float32).reshape(rows, cotangent_ref.shape[2])
    filler = jnp.zeros((rows, packed_ref.shape[2] - width), jnp.float32)
    for piece in range(packed_ref.shape[0]):
        part = whole[:, piece * width : (piece + 1) * width]
        packed_ref[piece] = jnp.concatenate([part, filler], axis=1).astype(jnp.bfloat16)


def pack(cotangent, pieces):
    return pl.pallas_call(
        pack_kernel,
        out_shape=jax.ShapeDtypeStruct((pieces, cotangent.shape[0] * cotangent.shape[1], 128), jnp.bfloat16),
        name="pack_cotangent",
    )(cotangent)


def project_kernel(packed_ref, weight_ref, gate_ref, grad_ref, slope_ref):
    pieces, rows, lanes = packed_ref.shape
    columns, tokens, channels = gate_ref.shape
    whole = packed_ref[...].astype(jnp.float32).reshape(pieces, columns, rows // columns, lanes)
    for column in range(columns):
        part = whole[:, column].reshape(channels, lanes).astype(jnp.bfloat16)
        gated = jnp.dot(weight_ref[...], part, preferred_element_type=jnp.float32).T[:tokens]
        sigma = jax.nn.sigmoid(gate_ref[column].astype(jnp.float32))
        grad = gated * sigma
        grad_ref[column] = grad.astype(jnp.bfloat16)
        slope_ref[column] = grad * (1.0 - sigma)


def project(packed, weight, gate):
    return pl.pallas_call(
        project_kernel,
        out_shape=[
            jax.ShapeDtypeStruct(gate.shape, jnp.bfloat16),
            jax.ShapeDtypeStruct(gate.shape, jnp.float32),
        ],
        name="project_cotangent",
    )(packed, weight, gate)


def attend(places, query_grad, blocks, bias, chips, row_count):
    columns, queries, lanes = query_grad.shape
    rows, keys = bias.shape
    height = blocks[0].shape[0]
    width = keys // row_count
    work = columns * rows * keys

    def whole(array):
        return pl.BlockSpec(array.shape, lambda j, places: (0,) * array.ndim)

    return pl.pallas_call(
        attention_kernel,
        grid_spec=pltpu.PrefetchScalarGridSpec(
            num_scalar_prefetch=1,
            grid=(columns,),
            in_specs=[pl.BlockSpec((1, queries, lanes), lambda j, places: (j, 0, 0))]
            + [whole(block) for block in blocks]
            + [whole(bias)],
            out_specs=[
                pl.BlockSpec((1, queries, lanes), lambda j, places: (j, 0, 0)),
                pl.BlockSpec((chips, 1, queries, lanes), lambda j, places: (0, j, 0, 0)),
                pl.BlockSpec((row_count, rows, width), lambda j, places: (0, 0, 0)),
            ],
            scratch_shapes=[
                pltpu.VMEM((chips, height, lanes), jnp.bfloat16),
                pltpu.VMEM((columns, 1, keys), jnp.float32),
                pltpu.VMEM((rows, keys), jnp.float32),
                pltpu.VMEM((rows, keys), jnp.float32),
                pltpu.VMEM((rows, keys), jnp.float32),
                pltpu.VMEM((rows, keys), jnp.float32),
                pltpu.VMEM((2 * rows, keys), jnp.bfloat16),
                pltpu.VMEM((rows, 128), jnp.float32),
            ],
        ),
        out_shape=[
            jax.ShapeDtypeStruct((columns, queries, lanes), jnp.bfloat16),
            jax.ShapeDtypeStruct((chips, columns, queries, lanes), jnp.bfloat16),
            jax.ShapeDtypeStruct((row_count, rows, width), jnp.bfloat16),
        ],
        compiler_params=pltpu.CompilerParams(vmem_limit_bytes=48 * 1024 * 1024),
        cost_estimate=pl.CostEstimate(flops=12 * 128 * work, bytes_accessed=16 * 2**20, transcendentals=work),
        name="attention_both",
    )(places, query_grad, *blocks, bias)


def local(
    query_vectors,
    key_vectors,
    value_vectors,
    gate_logits,
    pair_bias,
    pair_mask,
    output_weight,
    output_cotangent,
):
    columns, tokens, channels = query_vectors.shape
    half = channels // 2
    devices = lax.axis_size("col")
    row_count = lax.axis_size("row")
    chips = devices // 2
    core = lax.axis_index("col") % 2
    scaling = 1.0 / math.sqrt(channels // HEADS)
    swap = [(index, index ^ 1) for index in range(devices)]
    chip_groups = [[2 * chip + side for chip in range(chips)] for side in range(2)]
    keys = pair_bias.shape[2]

    def mine_other(array, axis):
        size = array.shape[axis] // 2
        low = lax.slice_in_dim(array, 0, size, axis=axis)
        high = lax.slice_in_dim(array, size, 2 * size, axis=axis)
        return jnp.where(core == 0, low, high), jnp.where(core == 0, high, low)

    def in_order(mine, other, axis):
        return jnp.where(
            core == 0,
            jnp.concatenate([mine, other], axis=axis),
            jnp.concatenate([other, mine], axis=axis),
        )

    def swapped(array):
        return lax.ppermute(array, "col", swap)

    bias_mine, bias_other = mine_other(pair_bias, 0)
    bias_pair = in_order(bias_mine, swapped(bias_other), 1).reshape(-1, keys)

    key_mine, key_other = mine_other(key_vectors, 2)
    value_mine, value_other = mine_other(value_vectors, 2)
    kv_mine = jnp.concatenate([key_mine, value_mine], axis=2)
    kv_other = swapped(jnp.concatenate([key_other, value_other], axis=2))
    mask_low = pair_mask.astype(jnp.bfloat16)
    kv_chip = in_order(kv_mine, kv_other, 1)
    mask_chip = in_order(mask_low, swapped(mask_low), 1)
    mask_rows = jnp.pad(mask_chip, ((0, 0), (0, 256 - 2 * tokens))).reshape(-1, channels)
    mask_rows = jnp.pad(mask_rows, ((0, MASK_ROWS - 2 * columns), (0, 0)))
    block = jnp.concatenate([kv_chip.reshape(-1, channels), mask_rows], axis=0)
    ring = chips // 2

    def along(array, turn, side):
        pairs = []
        for index in range(devices):
            high, low = index // (2 * ring), index // 2 % ring
            target = ((high + side) % 2) * ring + (low + turn) % ring
            pairs.append((index, 2 * target + index % 2))
        return lax.ppermute(array, "col", pairs)

    cut = columns * tokens
    left, right, across = along(block, 1, 0), along(block, -1, 0), along(block, 0, 1)
    left_pair = along(jnp.concatenate([across, left[:cut]], axis=0), 1, 0)
    right_pair = along(jnp.concatenate([across, right[cut:]], axis=0), -1, 0)
    left_far = along(left_pair[:cut], 1, 0)
    right_far = along(right_pair[cut : block.shape[0]], -1, 0)
    blocks = [block, left, right, across, left_pair, right_pair, left_far, right_far]
    chip = lax.axis_index("col") // 2
    place = lax.axis_index("row")
    row_ring = row_count // 2
    places = [
        ((chip // ring + side) % 2) * ring + (chip % ring + turn) % ring
        for side in range(2)
        for turn in (0, ring - 1, 1, 2)
    ] + [
        2 * ((index % row_ring - place) % row_ring) + (index // row_ring - place // row_ring) % 2
        for index in range(row_count)
    ]
    places = jnp.stack(places).astype(jnp.int32)

    regrouped = lax.all_to_all(pack(output_cotangent, devices), "col", 0, 0, tiled=True)
    attended_grad, gate_slope = project(regrouped, output_weight, gate_logits)
    query_mine, query_other = mine_other(query_vectors, 2)
    grad_mine, grad_other = mine_other(attended_grad, 2)
    qd_mine = jnp.concatenate([query_mine, grad_mine], axis=2)
    qd_other = swapped(jnp.concatenate([query_other, grad_other], axis=2))
    query_grad = in_order(qd_mine, qd_other, 1)

    query_attended, kv_grads, bias_grads = attend(places, query_grad, blocks, bias_pair, chips, row_count)

    kv_parts = lax.all_to_all(kv_grads, "col", 0, 0, tiled=True, axis_index_groups=chip_groups)
    kv_sum = jnp.sum(kv_parts.astype(jnp.float32), axis=0).astype(jnp.bfloat16)
    kv_own, kv_away = mine_other(kv_sum, 1)
    kv_back = swapped(kv_away)
    key_gradient = in_order(kv_own[..., :half], kv_back[..., :half], 2)
    key_gradient = (key_gradient.astype(jnp.float32) * scaling).astype(jnp.bfloat16)
    value_gradient = in_order(kv_own[..., half:], kv_back[..., half:], 2)

    qa_own, qa_away = mine_other(query_attended, 1)
    qa_back = swapped(qa_away)
    query_gradient = in_order(qa_own[..., :half], qa_back[..., :half], 2)
    attended = in_order(qa_own[..., half:], qa_back[..., half:], 2).astype(jnp.float32)
    gate_gradient = (gate_slope * attended).astype(jnp.bfloat16)

    def along_row(array, turn, side):
        pairs = []
        for index in range(row_count):
            high, low = index // row_ring, index % row_ring
            pairs.append((index, ((high + side) % 2) * row_ring + (low + turn) % row_ring))
        return lax.ppermute(array, "row", pairs)

    def added(*parts):
        return sum(part.astype(jnp.float32) for part in parts)

    from_left = along_row(bias_grads[4], 1, 0)
    from_right = along_row(bias_grads[5], -1, 0)
    onward = jnp.stack([added(bias_grads[2], from_left).astype(jnp.bfloat16), bias_grads[3]])
    backward = jnp.stack([bias_grads[6], added(bias_grads[7], from_right).astype(jnp.bfloat16)])
    from_left = along_row(onward, 1, 0)
    from_right = along_row(backward, -1, 0)
    bias_away = added(bias_grads[1], from_left[1], from_right[1]).astype(jnp.bfloat16)
    bias_sum = added(bias_grads[0], from_left[0], from_right[0], along_row(bias_away, 0, 1))
    bias_sum = bias_sum.astype(jnp.bfloat16)
    bias_sum = bias_sum.reshape(2, 2 * tokens, keys // row_count)
    bias_own, bias_away = mine_other(bias_sum, 1)
    bias_gradient = in_order(bias_own, swapped(bias_away), 0).astype(jnp.float32)
    return (query_gradient, key_gradient, value_gradient, gate_gradient, bias_gradient)


def solution(mesh):
    placed = (
        P("row", "col", None),
        P("row", "col", None),
        P("row", "col", None),
        P("row", "col", None),
        P(None, "col", None),
        P("row", "col"),
        P(),
        P("row", "col", None),
    )
    return jax.shard_map(
        local,
        mesh=mesh,
        in_specs=placed,
        out_specs=(
            P("row", "col", None),
            P("row", "col", None),
            P("row", "col", None),
            P("row", "col", None),
            P(None, "col", "row"),
        ),
        check_vma=False,
    )
```

```python
import math

import jax
import jax.numpy as jnp
from jax import lax
from jax.experimental import pallas as pl
from jax.experimental.pallas import tpu as pltpu
from jax.sharding import PartitionSpec as P

HEADS = 4
NEG_FILL = -1000000000.0
LOG2E = math.log2(math.e)
CHUNK = 16
UNROLL = 12
MASK_ROWS = 16
PIECES = 8


def attention_kernel(
    place_ref,
    qd_mine_ref,
    qd_other_ref,
    own_ref,
    left_ref,
    right_ref,
    across_ref,
    left_pair_ref,
    right_pair_ref,
    left_far_ref,
    right_far_ref,
    bias_ref,
    qa_own_ref,
    qa_away_ref,
    dkv_ref,
    right_out_ref,
    left_out_ref,
    rest_out_ref,
    kv_ref,
    cap_ref,
    s_ref,
    b2_ref,
    acc_ref,
    dp_ref,
    de_ref,
    row_ref,
    dbias_ref,
):
    step = pl.program_id(0)
    last = pl.num_programs(0) - 1
    rows = bias_ref.shape[0]
    queries = rows // 2
    keys = bias_ref.shape[1]
    head_width = qd_mine_ref.shape[2] // 4
    core = place_ref[8 + PIECES]
    scaling = 1.0 / math.sqrt(head_width)

    @pl.when(step == 0)
    def _():
        def fill(index, carry):
            part = pl.ds(index * CHUNK, CHUNK)
            b2_ref[part, :] = bias_ref[part, :].astype(jnp.float32) * LOG2E
            acc_ref[part, :] = jnp.zeros((CHUNK, keys), jnp.float32)
            return carry

        lax.fori_loop(0, rows // CHUNK, fill, 0)
        kv_ref[place_ref[0]] = own_ref[...]
        kv_ref[place_ref[1]] = left_ref[...]
        kv_ref[place_ref[2]] = right_ref[...]
        kv_ref[place_ref[3], 0] = left_pair_ref[2]
        kv_ref[place_ref[3], 1] = right_pair_ref[2]
        kv_ref[place_ref[4]] = across_ref[...]
        kv_ref[place_ref[5]] = left_pair_ref[:2]
        kv_ref[place_ref[6]] = right_pair_ref[:2]
        kv_ref[place_ref[7], 0] = left_far_ref[...]
        kv_ref[place_ref[7], 1] = right_far_ref[...]
        first = own_ref.shape[1] - MASK_ROWS
        masks = kv_ref[:, :, first:, :].astype(jnp.float32)
        for column in range(cap_ref.shape[0]):
            pieces = []
            for group in range(masks.shape[0]):
                for side in range(2):
                    pieces.append(masks[group, side, column : column + 1, : queries // 2])
            cap_ref[column] = jnp.where(
                jnp.concatenate(pieces, axis=1) > 0.5, 1e30, NEG_FILL * LOG2E
            )

    half = queries // 2
    kv = kv_ref[:, :, pl.ds(step * half, half), :].reshape(keys, 4 * head_width)
    qd_mine = qd_mine_ref[0]
    qd_other = qd_other_ref[0]
    qd = jnp.concatenate(
        [jnp.where(core == 0, qd_mine, qd_other), jnp.where(core == 0, qd_other, qd_mine)], axis=0
    )
    lane = lax.broadcasted_iota(jnp.int32, (queries, 4 * head_width), 1)
    zero = jnp.zeros_like(qd)

    def only(part):
        return jnp.where((lane >= part * head_width) & (lane < (part + 1) * head_width), qd, zero)

    transposed = (((1,), (1,)), ((), ()))
    cap = cap_ref[step]
    query_rows = [only(0), only(1)]
    grad_rows = [only(2), only(3)]

    def scores_of(head):
        s_ref[head * queries : (head + 1) * queries, :] = lax.dot_general(
            query_rows[head], kv, transposed, preferred_element_type=jnp.float32
        )

    def soften(head):
        def one(index, carry):
            start = head * queries + index * CHUNK
            part = pl.ds(start, CHUNK)
            scores = jnp.minimum(s_ref[part, :] * (scaling * LOG2E) + b2_ref[part, :], cap)
            weights = jnp.exp2(scores - jnp.max(scores, axis=1, keepdims=True))
            row_ref[part, :] = jnp.broadcast_to(jnp.sum(weights, axis=1, keepdims=True), (CHUNK, 128))
            de_ref[pl.ds(rows + start, CHUNK), :] = weights.astype(jnp.bfloat16)
            return carry

        lax.fori_loop(0, queries // CHUNK, one, 0, unroll=UNROLL)

    def cotangents(head):
        part = slice(head * queries, (head + 1) * queries)
        weights_low = de_ref[rows + head * queries : rows + (head + 1) * queries, :]
        inverse = 1.0 / row_ref[part, :]
        attended = jnp.dot(weights_low, kv, preferred_element_type=jnp.float32) * inverse
        grad_wide = grad_rows[head].astype(jnp.float32)
        delta = jnp.sum(grad_wide * attended, axis=1, keepdims=True)
        row_ref[part, :] = delta * inverse
        grad_scaled = (grad_wide * inverse).astype(jnp.bfloat16)
        dp_ref[part, :] = lax.dot_general(grad_scaled, kv, transposed, preferred_element_type=jnp.float32)
        return attended, grad_scaled

    def backward(head):
        def one(index, carry):
            start = head * queries + index * CHUNK
            part = pl.ds(start, CHUNK)
            weights = de_ref[pl.ds(rows + start, CHUNK), :].astype(jnp.float32)
            score_grad = weights * (dp_ref[part, :] - row_ref[part, :1])
            acc_ref[part, :] += score_grad
            de_ref[part, :] = score_grad.astype(jnp.bfloat16)
            return carry

        lax.fori_loop(0, queries // CHUNK, one, 0, unroll=UNROLL)

    def query_of(head):
        return jnp.dot(
            de_ref[head * queries : (head + 1) * queries, :], kv, preferred_element_type=jnp.float32
        ) * scaling

    scores_of(0)
    scores_of(1)
    soften(0)
    att0, sc0 = cotangents(0)
    soften(1)
    att1, sc1 = cotangents(1)
    backward(0)
    q0 = query_of(0)
    backward(1)
    q1 = query_of(1)
    merged = jnp.where(
        lane < 2 * head_width,
        jnp.where(lane < head_width, q0, q1),
        jnp.where(lane < 3 * head_width, att0, att1),
    )
    qa_own_ref[0] = jnp.where(core == 0, merged[:half], merged[half:]).astype(jnp.bfloat16)
    qa_away_ref[0] = jnp.where(core == 0, merged[half:], merged[:half]).astype(jnp.bfloat16)
    sides = jnp.concatenate(query_rows + [sc0, sc1], axis=0)
    key_value = lax.dot_general(
        sides, de_ref[...], (((0,), (0,)), ((), ())), preferred_element_type=jnp.float32
    )
    dkv_ref[...] = key_value.T.astype(jnp.bfloat16).reshape(dkv_ref.shape)

    @pl.when(step == last)
    def _():
        width = dbias_ref.shape[3]
        for piece in range(PIECES):
            for head in range(2):
                for side in range(2):
                    start = head * queries + side * half
                    part = acc_ref[start : start + half, piece * width : (piece + 1) * width]
                    target = 2 * place_ref[8 + piece] + (side + core) % 2
                    dbias_ref[target, head] = part.astype(jnp.bfloat16)
        right_out_ref[...] = dbias_ref[8:10]
        left_out_ref[...] = dbias_ref[10:12]
        rest_out_ref[:8] = dbias_ref[:8]
        rest_out_ref[8:] = dbias_ref[12:]


def prepare_kernel(core_ref, key_ref, value_ref, mask_ref, mine_ref, other_ref):
    columns, tokens, channels = key_ref.shape
    half = channels // 2
    core = core_ref[0]
    filler = jnp.zeros((MASK_ROWS - columns, channels), jnp.float32)
    mask = mask_ref[...].astype(jnp.float32)
    mask = jnp.concatenate([mask, jnp.zeros((columns, channels - tokens), jnp.float32)], axis=1)
    mask = jnp.concatenate([mask, filler], axis=0).astype(jnp.bfloat16)
    for column in range(columns):
        key = key_ref[column]
        value = value_ref[column]
        low = jnp.concatenate([key[:, :half], value[:, :half]], axis=1)
        high = jnp.concatenate([key[:, half:], value[:, half:]], axis=1)
        part = slice(column * tokens, (column + 1) * tokens)
        mine_ref[part, :] = jnp.where(core == 0, low, high)
        other_ref[part, :] = jnp.where(core == 0, high, low)
    mine_ref[columns * tokens :, :] = mask
    other_ref[columns * tokens :, :] = mask


def prepare(core, key, value, mask):
    columns, tokens, channels = key.shape
    out = jax.ShapeDtypeStruct((columns * tokens + MASK_ROWS, channels), jnp.bfloat16)
    vmem = pl.BlockSpec(memory_space=pltpu.VMEM)
    return pl.pallas_call(
        prepare_kernel,
        in_specs=[pl.BlockSpec(memory_space=pltpu.SMEM), vmem, vmem, vmem],
        out_shape=[out, out],
        name="prepare_key_value",
    )(core, key, value, mask)


def pack_kernel(cotangent_ref, packed_ref):
    width = cotangent_ref.shape[2] // packed_ref.shape[0]
    rows = packed_ref.shape[1]
    whole = cotangent_ref[...].astype(jnp.float32).reshape(rows, cotangent_ref.shape[2])
    filler = jnp.zeros((rows, packed_ref.shape[2] - width), jnp.float32)
    for piece in range(packed_ref.shape[0]):
        part = whole[:, piece * width : (piece + 1) * width]
        packed_ref[piece] = jnp.concatenate([part, filler], axis=1).astype(jnp.bfloat16)


def pack(cotangent, pieces):
    return pl.pallas_call(
        pack_kernel,
        out_shape=jax.ShapeDtypeStruct((pieces, cotangent.shape[0] * cotangent.shape[1], 128), jnp.bfloat16),
        name="pack_cotangent",
    )(cotangent)


def project_kernel(core_ref, packed_ref, weight_ref, gate_ref, query_ref, mine_ref, other_ref, slope_ref):
    pieces, rows, lanes = packed_ref.shape
    columns, tokens, channels = gate_ref.shape
    half = channels // 2
    core = core_ref[0]
    whole = packed_ref[...].astype(jnp.float32).reshape(pieces, columns, rows // columns, lanes)
    for column in range(columns):
        part = whole[:, column].reshape(channels, lanes).astype(jnp.bfloat16)
        gated = jnp.dot(weight_ref[...], part, preferred_element_type=jnp.float32).T[:tokens]
        sigma = jax.nn.sigmoid(gate_ref[column].astype(jnp.float32))
        grad = gated * sigma
        slope_ref[column] = grad * (1.0 - sigma)
        grad = grad.astype(jnp.bfloat16)
        query = query_ref[column]
        low = jnp.concatenate([query[:, :half], grad[:, :half]], axis=1)
        high = jnp.concatenate([query[:, half:], grad[:, half:]], axis=1)
        mine_ref[column] = jnp.where(core == 0, low, high)
        other_ref[column] = jnp.where(core == 0, high, low)


def project(core, packed, weight, gate, query):
    vmem = pl.BlockSpec(memory_space=pltpu.VMEM)
    return pl.pallas_call(
        project_kernel,
        in_specs=[pl.BlockSpec(memory_space=pltpu.SMEM)] + [vmem] * 4,
        out_shape=[
            jax.ShapeDtypeStruct(gate.shape, jnp.bfloat16),
            jax.ShapeDtypeStruct(gate.shape, jnp.bfloat16),
            jax.ShapeDtypeStruct(gate.shape, jnp.float32),
        ],
        name="project_cotangent",
    )(core, packed, weight, gate, query)


def total_kernel(parts_ref, key_ref, value_ref):
    half = key_ref.shape[2] // 2
    scaling = 1.0 / math.sqrt(key_ref.shape[2] // HEADS)
    for column in range(key_ref.shape[0]):
        sums = [
            jnp.sum(parts_ref[:, side, column].astype(jnp.float32), axis=0) for side in range(2)
        ]
        key = jnp.concatenate([part[:, :half] for part in sums], axis=1) * scaling
        key_ref[column] = key.astype(jnp.bfloat16)
        value = jnp.concatenate([part[:, half:] for part in sums], axis=1)
        value_ref[column] = value.astype(jnp.bfloat16)


def total(parts, like):
    out = jax.ShapeDtypeStruct(like.shape, jnp.bfloat16)
    return pl.pallas_call(total_kernel, out_shape=[out, out], name="total_key_value")(parts)


def attend(places, mine, other, blocks, bias, chips, row_count):
    columns, tokens, lanes = mine.shape
    rows, keys = bias.shape
    width = keys // row_count
    work = columns * rows * keys

    def whole(shape):
        return pl.BlockSpec(shape, lambda j, places: (0,) * len(shape))

    column_spec = pl.BlockSpec((1, tokens, lanes), lambda j, places: (j, 0, 0))
    piece = (2, tokens, width)
    return pl.pallas_call(
        attention_kernel,
        grid_spec=pltpu.PrefetchScalarGridSpec(
            num_scalar_prefetch=1,
            grid=(columns,),
            in_specs=[column_spec, column_spec]
            + [whole(block.shape) for block in blocks]
            + [whole(bias.shape)],
            out_specs=[
                column_spec,
                column_spec,
                pl.BlockSpec((chips, 2, 1, tokens, lanes), lambda j, places: (0, 0, j, 0, 0)),
                whole((2,) + piece),
                whole((2,) + piece),
                whole((12,) + piece),
            ],
            scratch_shapes=[
                pltpu.VMEM((chips,) + blocks[0].shape, jnp.bfloat16),
                pltpu.VMEM((columns, 1, keys), jnp.float32),
                pltpu.VMEM((rows, keys), jnp.float32),
                pltpu.VMEM((rows, keys), jnp.float32),
                pltpu.VMEM((rows, keys), jnp.float32),
                pltpu.VMEM((rows, keys), jnp.float32),
                pltpu.VMEM((2 * rows, keys), jnp.bfloat16),
                pltpu.VMEM((rows, 128), jnp.float32),
                pltpu.VMEM((16,) + piece, jnp.bfloat16),
            ],
        ),
        out_shape=[
            jax.ShapeDtypeStruct(mine.shape, jnp.bfloat16),
            jax.ShapeDtypeStruct(mine.shape, jnp.bfloat16),
            jax.ShapeDtypeStruct((chips, 2, columns, tokens, lanes), jnp.bfloat16),
            jax.ShapeDtypeStruct((2,) + piece, jnp.bfloat16),
            jax.ShapeDtypeStruct((2,) + piece, jnp.bfloat16),
            jax.ShapeDtypeStruct((12,) + piece, jnp.bfloat16),
        ],
        compiler_params=pltpu.CompilerParams(vmem_limit_bytes=48 * 1024 * 1024),
        cost_estimate=pl.CostEstimate(flops=12 * 128 * work, bytes_accessed=16 * 2**20, transcendentals=work),
        name="attention_both",
    )(places, mine, other, *blocks, bias)


def local(
    query_vectors,
    key_vectors,
    value_vectors,
    gate_logits,
    pair_bias,
    pair_mask,
    output_weight,
    output_cotangent,
):
    columns, tokens, channels = query_vectors.shape
    half = channels // 2
    devices = lax.axis_size("col")
    row_count = lax.axis_size("row")
    chips = devices // 2
    core = lax.axis_index("col") % 2
    scaling = 1.0 / math.sqrt(channels // HEADS)
    swap = [(index, index ^ 1) for index in range(devices)]
    chip_groups = [[2 * chip + side for chip in range(chips)] for side in range(2)]
    keys = pair_bias.shape[2]

    def mine_other(array, axis):
        size = array.shape[axis] // 2
        low = lax.slice_in_dim(array, 0, size, axis=axis)
        high = lax.slice_in_dim(array, size, 2 * size, axis=axis)
        return jnp.where(core == 0, low, high), jnp.where(core == 0, high, low)

    def in_order(mine, other, axis):
        return jnp.where(
            core == 0,
            jnp.concatenate([mine, other], axis=axis),
            jnp.concatenate([other, mine], axis=axis),
        )

    def swapped(array):
        return lax.ppermute(array, "col", swap)

    bias_mine, bias_other = mine_other(pair_bias, 0)
    bias_pair = in_order(bias_mine, swapped(bias_other), 1).reshape(-1, keys)

    core_word = core.astype(jnp.int32).reshape(1)
    kv_mine, kv_away = prepare(core_word, key_vectors, value_vectors, pair_mask)
    block = in_order(kv_mine[None], swapped(kv_away)[None], 0)
    ring = chips // 2

    def along(array, turn, side):
        pairs = []
        for index in range(devices):
            high, low = index // (2 * ring), index // 2 % ring
            target = ((high + side) % 2) * ring + (low + turn) % ring
            pairs.append((index, 2 * target + index % 2))
        return lax.ppermute(array, "col", pairs)

    block, output_cotangent = lax.optimization_barrier((block, output_cotangent))
    left, right, across = along(block, 1, 0), along(block, -1, 0), along(block, 0, 1)
    left_pair = along(jnp.concatenate([across, left[:1]], axis=0), 1, 0)
    right_pair = along(jnp.concatenate([across, right[1:]], axis=0), -1, 0)
    left_far = along(left_pair[0], 1, 0)
    right_far = along(right_pair[1], -1, 0)
    blocks = [block, left, right, across, left_pair, right_pair, left_far, right_far]
    chip = lax.axis_index("col") // 2
    place = lax.axis_index("row")
    row_ring = row_count // 2
    places = [
        ((chip // ring + side) % 2) * ring + (chip % ring + turn) % ring
        for side in range(2)
        for turn in (0, ring - 1, 1, 2)
    ] + [
        2 * ((index % row_ring - place) % row_ring) + (index // row_ring - place // row_ring) % 2
        for index in range(row_count)
    ]
    places.append(core)
    places = jnp.stack(places).astype(jnp.int32)

    regrouped = lax.all_to_all(pack(output_cotangent, devices), "col", 0, 0, tiled=True)
    qd_mine, qd_away, gate_slope = project(core_word, regrouped, output_weight, gate_logits, query_vectors)

    qa_own, qa_away, kv_grads, bias_right, bias_left, bias_rest = attend(
        places, qd_mine, swapped(qd_away), blocks, bias_pair, chips, row_count
    )

    kv_parts = lax.all_to_all(
        kv_grads.reshape((devices,) + kv_grads.shape[2:]), "col", 0, 0, tiled=True
    )
    key_gradient, value_gradient = total(kv_parts.reshape(kv_grads.shape), key_vectors)

    qa_back = swapped(qa_away)
    query_gradient = in_order(qa_own[..., :half], qa_back[..., :half], 2)
    attended = in_order(qa_own[..., half:], qa_back[..., half:], 2).astype(jnp.float32)
    gate_gradient = (gate_slope * attended).astype(jnp.bfloat16)

    def along_row(array, turn, side):
        pairs = []
        for index in range(row_count):
            high, low = index // row_ring, index % row_ring
            pairs.append((index, ((high + side) % 2) * row_ring + (low + turn) % row_ring))
        return lax.ppermute(array, "row", pairs)

    def added(*parts):
        return sum(part.astype(jnp.float32) for part in parts)

    from_left = along_row(bias_right, 1, 0)
    from_right = along_row(bias_left, -1, 0)
    onward = jnp.concatenate([added(bias_rest[4:6], from_left).astype(jnp.bfloat16), bias_rest[6:8]])
    backward = jnp.concatenate([bias_rest[8:10], added(bias_rest[10:], from_right).astype(jnp.bfloat16)])
    sums = added(bias_rest[:4], along_row(onward, 1, 0), along_row(backward, -1, 0))
    low_sums = sums.astype(jnp.bfloat16)
    diagonal = []
    for index in range(row_count * devices):
        up = (index // devices + row_ring) % row_count
        diagonal.append((index, up * devices + (index % devices ^ 1)))
    bias_own = added(sums[0], along_row(low_sums[2], 0, 1))
    bias_away = added(swapped(low_sums[1]), lax.ppermute(low_sums[3], ("row", "col"), diagonal))
    bias_gradient = in_order(bias_own, bias_away, 0)
    return (query_gradient, key_gradient, value_gradient, gate_gradient, bias_gradient)


def solution(mesh):
    placed = (
        P("row", "col", None),
        P("row", "col", None),
        P("row", "col", None),
        P("row", "col", None),
        P(None, "col", None),
        P("row", "col"),
        P(),
        P("row", "col", None),
    )
    return jax.shard_map(
        local,
        mesh=mesh,
        in_specs=placed,
        out_specs=(
            P("row", "col", None),
            P("row", "col", None),
            P("row", "col", None),
            P("row", "col", None),
            P(None, "col", "row"),
        ),
        check_vma=False,
    )
```

```python
import math

import jax
import jax.numpy as jnp
from jax import lax
from jax.experimental import pallas as pl
from jax.experimental.pallas import tpu as pltpu
from jax.sharding import PartitionSpec as P

HEADS = 4
NEG_FILL = -1000000000.0
LOG2E = math.log2(math.e)
CHUNK = 16
UNROLL = 12
MASK_ROWS = 16
PIECES = 8


def attention_kernel(
    place_ref,
    qd_mine_ref,
    qd_other_ref,
    own_ref,
    left_ref,
    right_ref,
    across_ref,
    left_pair_ref,
    right_pair_ref,
    left_far_ref,
    right_far_ref,
    bias_ref,
    qa_own_ref,
    qa_away_ref,
    right_out_ref,
    left_out_ref,
    rest_out_ref,
    dbias_ref,
    kv_ref,
    cap_ref,
    s_ref,
    b2_ref,
    acc_ref,
    dp_ref,
    de_ref,
    row_ref,
    dkv_ref,
):
    step = pl.program_id(0)
    last = pl.num_programs(0) - 1
    rows = bias_ref.shape[0]
    queries = rows // 2
    keys = bias_ref.shape[1]
    head_width = qd_mine_ref.shape[2] // 4
    core = place_ref[8 + PIECES]
    scaling = 1.0 / math.sqrt(head_width)

    @pl.when(step == 0)
    def _():
        def fill(index, carry):
            part = pl.ds(index * CHUNK, CHUNK)
            b2_ref[part, :] = bias_ref[part, :].astype(jnp.float32) * LOG2E
            acc_ref[part, :] = jnp.zeros((CHUNK, keys), jnp.float32)
            return carry

        lax.fori_loop(0, rows // CHUNK, fill, 0)
        kv_ref[place_ref[0]] = own_ref[...]
        kv_ref[place_ref[1]] = left_ref[...]
        kv_ref[place_ref[2]] = right_ref[...]
        kv_ref[place_ref[3], 0] = left_pair_ref[2]
        kv_ref[place_ref[3], 1] = right_pair_ref[2]
        kv_ref[place_ref[4]] = across_ref[...]
        kv_ref[place_ref[5]] = left_pair_ref[:2]
        kv_ref[place_ref[6]] = right_pair_ref[:2]
        kv_ref[place_ref[7], 0] = left_far_ref[...]
        kv_ref[place_ref[7], 1] = right_far_ref[...]
        first = own_ref.shape[1] - MASK_ROWS
        masks = kv_ref[:, :, first:, :].astype(jnp.float32)
        for column in range(cap_ref.shape[0]):
            pieces = []
            for group in range(masks.shape[0]):
                for side in range(2):
                    pieces.append(masks[group, side, column : column + 1, : queries // 2])
            cap_ref[column] = jnp.where(
                jnp.concatenate(pieces, axis=1) > 0.5, 1e30, NEG_FILL * LOG2E
            )

    half = queries // 2
    kv = kv_ref[:, :, pl.ds(step * half, half), :].reshape(keys, 4 * head_width)
    qd_mine = qd_mine_ref[0]
    qd_other = qd_other_ref[0]
    qd = jnp.concatenate(
        [jnp.where(core == 0, qd_mine, qd_other), jnp.where(core == 0, qd_other, qd_mine)], axis=0
    )
    lane = lax.broadcasted_iota(jnp.int32, (queries, 4 * head_width), 1)
    zero = jnp.zeros_like(qd)

    def only(part):
        return jnp.where((lane >= part * head_width) & (lane < (part + 1) * head_width), qd, zero)

    transposed = (((1,), (1,)), ((), ()))
    cap = cap_ref[step]
    query_rows = [only(0), only(1)]
    grad_rows = [only(2), only(3)]

    def scores_of(head):
        s_ref[head * queries : (head + 1) * queries, :] = lax.dot_general(
            query_rows[head], kv, transposed, preferred_element_type=jnp.float32
        )

    def soften(head):
        def one(index, carry):
            start = head * queries + index * CHUNK
            part = pl.ds(start, CHUNK)
            scores = jnp.minimum(s_ref[part, :] * (scaling * LOG2E) + b2_ref[part, :], cap)
            weights = jnp.exp2(scores - jnp.max(scores, axis=1, keepdims=True))
            row_ref[part, :] = jnp.broadcast_to(jnp.sum(weights, axis=1, keepdims=True), (CHUNK, 128))
            de_ref[pl.ds(rows + start, CHUNK), :] = weights.astype(jnp.bfloat16)
            return carry

        lax.fori_loop(0, queries // CHUNK, one, 0, unroll=UNROLL)

    def cotangents(head):
        part = slice(head * queries, (head + 1) * queries)
        weights_low = de_ref[rows + head * queries : rows + (head + 1) * queries, :]
        inverse = 1.0 / row_ref[part, :]
        attended = jnp.dot(weights_low, kv, preferred_element_type=jnp.float32) * inverse
        grad_wide = grad_rows[head].astype(jnp.float32)
        delta = jnp.sum(grad_wide * attended, axis=1, keepdims=True)
        row_ref[part, :] = delta * inverse
        grad_scaled = (grad_wide * inverse).astype(jnp.bfloat16)
        dp_ref[part, :] = lax.dot_general(grad_scaled, kv, transposed, preferred_element_type=jnp.float32)
        return attended, grad_scaled

    def backward(head):
        def one(index, carry):
            start = head * queries + index * CHUNK
            part = pl.ds(start, CHUNK)
            weights = de_ref[pl.ds(rows + start, CHUNK), :].astype(jnp.float32)
            score_grad = weights * (dp_ref[part, :] - row_ref[part, :1])
            acc_ref[part, :] += score_grad
            de_ref[part, :] = score_grad.astype(jnp.bfloat16)
            return carry

        lax.fori_loop(0, queries // CHUNK, one, 0, unroll=UNROLL)

    def query_of(head):
        return jnp.dot(
            de_ref[head * queries : (head + 1) * queries, :], kv, preferred_element_type=jnp.float32
        ) * scaling

    scores_of(0)
    scores_of(1)
    soften(0)
    att0, sc0 = cotangents(0)
    soften(1)
    att1, sc1 = cotangents(1)
    backward(0)
    q0 = query_of(0)
    backward(1)
    q1 = query_of(1)
    merged = jnp.where(
        lane < 2 * head_width,
        jnp.where(lane < head_width, q0, q1),
        jnp.where(lane < 3 * head_width, att0, att1),
    )
    qa_own_ref[0] = jnp.where(core == 0, merged[:half], merged[half:]).astype(jnp.bfloat16)
    qa_away_ref[0] = jnp.where(core == 0, merged[half:], merged[:half]).astype(jnp.bfloat16)
    sides = jnp.concatenate(query_rows + [sc0, sc1], axis=0)
    key_value = lax.dot_general(
        sides, de_ref[...], (((0,), (0,)), ((), ())), preferred_element_type=jnp.float32
    )
    key_value = key_value.T.astype(jnp.bfloat16)
    for group in range(PIECES):
        for side in range(2):
            start = group * queries + side * half
            target = 2 * place_ref[8 + group] + (side + core) % 2
            dkv_ref[target, step] = key_value[start : start + half]

    @pl.when(step == last)
    def _():
        width = dbias_ref.shape[4]
        for piece in range(PIECES):
            for head in range(2):
                for side in range(2):
                    start = head * queries + side * half
                    part = acc_ref[start : start + half, piece * width : (piece + 1) * width]
                    dbias_ref[piece, (side + core) % 2, head] = part.astype(jnp.bfloat16)
        right_out_ref[...] = dkv_ref[12]
        left_out_ref[...] = dkv_ref[13]
        rest_out_ref[:12] = dkv_ref[:12]
        rest_out_ref[12:] = dkv_ref[14:]


def prepare_kernel(core_ref, key_ref, value_ref, mask_ref, mine_ref, other_ref):
    columns, tokens, channels = key_ref.shape
    half = channels // 2
    core = core_ref[0]
    filler = jnp.zeros((MASK_ROWS - columns, channels), jnp.float32)
    mask = mask_ref[...].astype(jnp.float32)
    mask = jnp.concatenate([mask, jnp.zeros((columns, channels - tokens), jnp.float32)], axis=1)
    mask = jnp.concatenate([mask, filler], axis=0).astype(jnp.bfloat16)
    for column in range(columns):
        key = key_ref[column]
        value = value_ref[column]
        low = jnp.concatenate([key[:, :half], value[:, :half]], axis=1)
        high = jnp.concatenate([key[:, half:], value[:, half:]], axis=1)
        part = slice(column * tokens, (column + 1) * tokens)
        mine_ref[part, :] = jnp.where(core == 0, low, high)
        other_ref[part, :] = jnp.where(core == 0, high, low)
    mine_ref[columns * tokens :, :] = mask
    other_ref[columns * tokens :, :] = mask


def prepare(core, key, value, mask):
    columns, tokens, channels = key.shape
    out = jax.ShapeDtypeStruct((columns * tokens + MASK_ROWS, channels), jnp.bfloat16)
    vmem = pl.BlockSpec(memory_space=pltpu.VMEM)
    return pl.pallas_call(
        prepare_kernel,
        in_specs=[pl.BlockSpec(memory_space=pltpu.SMEM), vmem, vmem, vmem],
        out_shape=[out, out],
        name="prepare_key_value",
    )(core, key, value, mask)


def pack_kernel(cotangent_ref, packed_ref):
    width = cotangent_ref.shape[2] // packed_ref.shape[0]
    rows = packed_ref.shape[1]
    whole = cotangent_ref[...].astype(jnp.float32).reshape(rows, cotangent_ref.shape[2])
    filler = jnp.zeros((rows, packed_ref.shape[2] - width), jnp.float32)
    for piece in range(packed_ref.shape[0]):
        part = whole[:, piece * width : (piece + 1) * width]
        packed_ref[piece] = jnp.concatenate([part, filler], axis=1).astype(jnp.bfloat16)


def pack(cotangent, pieces):
    return pl.pallas_call(
        pack_kernel,
        out_shape=jax.ShapeDtypeStruct((pieces, cotangent.shape[0] * cotangent.shape[1], 128), jnp.bfloat16),
        name="pack_cotangent",
    )(cotangent)


def project_kernel(core_ref, packed_ref, weight_ref, gate_ref, query_ref, mine_ref, other_ref, slope_ref):
    pieces, rows, lanes = packed_ref.shape
    columns, tokens, channels = gate_ref.shape
    half = channels // 2
    core = core_ref[0]
    whole = packed_ref[...].astype(jnp.float32).reshape(pieces, columns, rows // columns, lanes)
    for column in range(columns):
        part = whole[:, column].reshape(channels, lanes).astype(jnp.bfloat16)
        gated = jnp.dot(weight_ref[...], part, preferred_element_type=jnp.float32).T[:tokens]
        sigma = jax.nn.sigmoid(gate_ref[column].astype(jnp.float32))
        grad = gated * sigma
        slope_ref[column] = grad * (1.0 - sigma)
        grad = grad.astype(jnp.bfloat16)
        query = query_ref[column]
        low = jnp.concatenate([query[:, :half], grad[:, :half]], axis=1)
        high = jnp.concatenate([query[:, half:], grad[:, half:]], axis=1)
        mine_ref[column] = jnp.where(core == 0, low, high)
        other_ref[column] = jnp.where(core == 0, high, low)


def project(core, packed, weight, gate, query):
    vmem = pl.BlockSpec(memory_space=pltpu.VMEM)
    return pl.pallas_call(
        project_kernel,
        in_specs=[pl.BlockSpec(memory_space=pltpu.SMEM)] + [vmem] * 4,
        out_shape=[
            jax.ShapeDtypeStruct(gate.shape, jnp.bfloat16),
            jax.ShapeDtypeStruct(gate.shape, jnp.bfloat16),
            jax.ShapeDtypeStruct(gate.shape, jnp.float32),
        ],
        name="project_cotangent",
    )(core, packed, weight, gate, query)


def attend(places, mine, other, blocks, bias, chips, row_count):
    columns, tokens, lanes = mine.shape
    rows, keys = bias.shape
    width = keys // row_count
    work = columns * rows * keys

    def whole(shape):
        return pl.BlockSpec(shape, lambda j, places: (0,) * len(shape))

    column_spec = pl.BlockSpec((1, tokens, lanes), lambda j, places: (j, 0, 0))
    piece = (2, tokens, width)
    return pl.pallas_call(
        attention_kernel,
        grid_spec=pltpu.PrefetchScalarGridSpec(
            num_scalar_prefetch=1,
            grid=(columns,),
            in_specs=[column_spec, column_spec]
            + [whole(block.shape) for block in blocks]
            + [whole(bias.shape)],
            out_specs=[
                column_spec,
                column_spec,
                whole(mine.shape),
                whole(mine.shape),
                whole((14,) + mine.shape),
                whole((row_count, 2) + piece),
            ],
            scratch_shapes=[
                pltpu.VMEM((chips,) + blocks[0].shape, jnp.bfloat16),
                pltpu.VMEM((columns, 1, keys), jnp.float32),
                pltpu.VMEM((rows, keys), jnp.float32),
                pltpu.VMEM((rows, keys), jnp.float32),
                pltpu.VMEM((rows, keys), jnp.float32),
                pltpu.VMEM((rows, keys), jnp.float32),
                pltpu.VMEM((2 * rows, keys), jnp.bfloat16),
                pltpu.VMEM((rows, 128), jnp.float32),
                pltpu.VMEM((16,) + mine.shape, jnp.bfloat16),
            ],
        ),
        out_shape=[
            jax.ShapeDtypeStruct(mine.shape, jnp.bfloat16),
            jax.ShapeDtypeStruct(mine.shape, jnp.bfloat16),
            jax.ShapeDtypeStruct(mine.shape, jnp.bfloat16),
            jax.ShapeDtypeStruct(mine.shape, jnp.bfloat16),
            jax.ShapeDtypeStruct((14,) + mine.shape, jnp.bfloat16),
            jax.ShapeDtypeStruct((row_count, 2) + piece, jnp.bfloat16),
        ],
        compiler_params=pltpu.CompilerParams(vmem_limit_bytes=48 * 1024 * 1024),
        cost_estimate=pl.CostEstimate(flops=12 * 128 * work, bytes_accessed=16 * 2**20, transcendentals=work),
        name="attention_both",
    )(places, mine, other, *blocks, bias)


def local(
    query_vectors,
    key_vectors,
    value_vectors,
    gate_logits,
    pair_bias,
    pair_mask,
    output_weight,
    output_cotangent,
):
    columns, tokens, channels = query_vectors.shape
    half = channels // 2
    devices = lax.axis_size("col")
    row_count = lax.axis_size("row")
    chips = devices // 2
    core = lax.axis_index("col") % 2
    scaling = 1.0 / math.sqrt(channels // HEADS)
    swap = [(index, index ^ 1) for index in range(devices)]
    chip_groups = [[2 * chip + side for chip in range(chips)] for side in range(2)]
    keys = pair_bias.shape[2]

    def mine_other(array, axis):
        size = array.shape[axis] // 2
        low = lax.slice_in_dim(array, 0, size, axis=axis)
        high = lax.slice_in_dim(array, size, 2 * size, axis=axis)
        return jnp.where(core == 0, low, high), jnp.where(core == 0, high, low)

    def in_order(mine, other, axis):
        return jnp.where(
            core == 0,
            jnp.concatenate([mine, other], axis=axis),
            jnp.concatenate([other, mine], axis=axis),
        )

    def swapped(array):
        return lax.ppermute(array, "col", swap)

    bias_mine, bias_other = mine_other(pair_bias, 0)
    bias_pair = in_order(bias_mine, swapped(bias_other), 1).reshape(-1, keys)

    core_word = core.astype(jnp.int32).reshape(1)
    kv_mine, kv_away = prepare(core_word, key_vectors, value_vectors, pair_mask)
    kv_away, output_cotangent = lax.optimization_barrier((kv_away, output_cotangent))
    packed = pack(output_cotangent, devices)
    block = in_order(kv_mine[None], swapped(kv_away)[None], 0)
    ring = chips // 2

    def along(array, turn, side):
        pairs = []
        for index in range(devices):
            high, low = index // (2 * ring), index // 2 % ring
            target = ((high + side) % 2) * ring + (low + turn) % ring
            pairs.append((index, 2 * target + index % 2))
        return lax.ppermute(array, "col", pairs)

    left, right, across = along(block, 1, 0), along(block, -1, 0), along(block, 0, 1)
    regrouped = lax.all_to_all(packed, "col", 0, 0, tiled=True)
    left, right, across, regrouped = lax.optimization_barrier((left, right, across, regrouped))
    left_pair = along(jnp.concatenate([across, left[:1]], axis=0), 1, 0)
    right_pair = along(jnp.concatenate([across, right[1:]], axis=0), -1, 0)
    left_far = along(left_pair[0], 1, 0)
    right_far = along(right_pair[1], -1, 0)
    blocks = [block, left, right, across, left_pair, right_pair, left_far, right_far]
    chip = lax.axis_index("col") // 2
    places = [
        ((chip // ring + side) % 2) * ring + (chip % ring + turn) % ring
        for side in range(2)
        for turn in (0, ring - 1, 1, 2)
    ] + [
        ring * ((index // ring - chip // ring) % 2) + (index % ring - chip % ring) % ring
        for index in range(chips)
    ]
    places.append(core)
    places = jnp.stack(places).astype(jnp.int32)

    qd_mine, qd_away, gate_slope = project(core_word, regrouped, output_weight, gate_logits, query_vectors)

    qa_own, qa_away, kv_right, kv_left, kv_rest, bias_grads = attend(
        places, qd_mine, swapped(qd_away), blocks, bias_pair, chips, row_count
    )

    bias_parts = lax.all_to_all(bias_grads, "row", 0, 0, tiled=True)

    def added(*parts):
        return sum(part.astype(jnp.float32) for part in parts)

    def both(*parts):
        return lax.optimization_barrier(parts)

    def low(*parts):
        return added(*parts).astype(jnp.bfloat16)

    home, near, far, behind = kv_rest[:2], kv_rest[2:4], kv_rest[4:6], kv_rest[6:8]
    home_across, near_across, behind_across = kv_rest[8:10], kv_rest[10:12], kv_rest[12:]
    from_left, from_right = both(along(kv_right, 1, 0), along(kv_left, -1, 0))
    onward = jnp.concatenate([low(near_across[:1], from_left[None]), near_across[1:], far[:1]])
    backward = jnp.concatenate([behind_across[:1], low(behind_across[1:], from_right[None]), far[1:]])
    from_left, from_right = both(along(onward, 1, 0), along(backward, -1, 0))
    from_across = along(low(home_across, from_left[:2], from_right[:2]), 0, 1)
    onward = jnp.concatenate([low(near[:1], from_left[2:]), near[1:]])
    backward = jnp.concatenate([behind[:1], low(behind[1:], from_right[2:])])
    kv_sum = low(home, along(onward, 1, 0), along(backward, -1, 0), from_across)
    kv_back = swapped(kv_sum[1])
    key_gradient = in_order(kv_sum[0, ..., :half], kv_back[..., :half], 2)
    key_gradient = (key_gradient.astype(jnp.float32) * scaling).astype(jnp.bfloat16)
    value_gradient = in_order(kv_sum[0, ..., half:], kv_back[..., half:], 2)

    qa_back = swapped(qa_away)
    query_gradient = in_order(qa_own[..., :half], qa_back[..., :half], 2)
    attended = in_order(qa_own[..., half:], qa_back[..., half:], 2).astype(jnp.float32)
    gate_gradient = (gate_slope * attended).astype(jnp.bfloat16)

    bias_sum = jnp.sum(bias_parts.astype(jnp.float32), axis=0)
    bias_gradient = in_order(
        bias_sum[0], swapped(bias_sum[1].astype(jnp.bfloat16)).astype(jnp.float32), 0
    )
    return (query_gradient, key_gradient, value_gradient, gate_gradient, bias_gradient)


def solution(mesh):
    placed = (
        P("row", "col", None),
        P("row", "col", None),
        P("row", "col", None),
        P("row", "col", None),
        P(None, "col", None),
        P("row", "col"),
        P(),
        P("row", "col", None),
    )
    return jax.shard_map(
        local,
        mesh=mesh,
        in_specs=placed,
        out_specs=(
            P("row", "col", None),
            P("row", "col", None),
            P("row", "col", None),
            P("row", "col", None),
            P(None, "col", "row"),
        ),
        check_vma=False,
    )
```

```python
import math

import jax
import jax.numpy as jnp
from jax import lax
from jax.experimental import pallas as pl
from jax.experimental.pallas import tpu as pltpu
from jax.sharding import PartitionSpec as P

HEADS = 4
NEG_FILL = -1000000000.0
LOG2E = math.log2(math.e)
CHUNK = 16
UNROLL = 12
MASK_ROWS = 16
PIECES = 8


def attention_kernel(
    place_ref,
    qd_mine_ref,
    qd_other_ref,
    kv_ref,
    mask_ref,
    bias_ref,
    qa_own_ref,
    qa_away_ref,
    right_out_ref,
    left_out_ref,
    rest_out_ref,
    dbias_ref,
    cap_ref,
    s_ref,
    b2_ref,
    acc_ref,
    dp_ref,
    de_ref,
    row_ref,
    dkv_ref,
):
    step = pl.program_id(0)
    last = pl.num_programs(0) - 1
    rows = bias_ref.shape[0]
    queries = rows // 2
    keys = bias_ref.shape[1]
    head_width = qd_mine_ref.shape[2] // 4
    core = place_ref[PIECES]
    scaling = 1.0 / math.sqrt(head_width)

    @pl.when(step == 0)
    def _():
        def fill(index, carry):
            part = pl.ds(index * CHUNK, CHUNK)
            b2_ref[part, :] = bias_ref[part, :].astype(jnp.float32) * LOG2E
            acc_ref[part, :] = jnp.zeros((CHUNK, keys), jnp.float32)
            return carry

        lax.fori_loop(0, rows // CHUNK, fill, 0)
        masks = mask_ref[...].astype(jnp.float32)
        for column in range(cap_ref.shape[0]):
            pieces = [
                masks[source, column : column + 1, : queries // 2] for source in range(masks.shape[0])
            ]
            cap_ref[column] = jnp.where(
                jnp.concatenate(pieces, axis=1) > 0.5, 1e30, NEG_FILL * LOG2E
            )

    half = queries // 2
    kv = kv_ref[...].reshape(keys, 4 * head_width)
    qd_mine = qd_mine_ref[0]
    qd_other = qd_other_ref[0]
    qd = jnp.concatenate(
        [jnp.where(core == 0, qd_mine, qd_other), jnp.where(core == 0, qd_other, qd_mine)], axis=0
    )
    lane = lax.broadcasted_iota(jnp.int32, (queries, 4 * head_width), 1)
    zero = jnp.zeros_like(qd)

    def only(part):
        return jnp.where((lane >= part * head_width) & (lane < (part + 1) * head_width), qd, zero)

    transposed = (((1,), (1,)), ((), ()))
    cap = cap_ref[step]
    query_rows = [only(0), only(1)]
    grad_rows = [only(2), only(3)]

    def scores_of(head):
        s_ref[head * queries : (head + 1) * queries, :] = lax.dot_general(
            query_rows[head], kv, transposed, preferred_element_type=jnp.float32
        )

    def soften(head):
        def one(index, carry):
            start = head * queries + index * CHUNK
            part = pl.ds(start, CHUNK)
            scores = jnp.minimum(s_ref[part, :] * (scaling * LOG2E) + b2_ref[part, :], cap)
            weights = jnp.exp2(scores - jnp.max(scores, axis=1, keepdims=True))
            row_ref[part, :] = jnp.broadcast_to(jnp.sum(weights, axis=1, keepdims=True), (CHUNK, 128))
            de_ref[pl.ds(rows + start, CHUNK), :] = weights.astype(jnp.bfloat16)
            return carry

        lax.fori_loop(0, queries // CHUNK, one, 0, unroll=UNROLL)

    def cotangents(head):
        part = slice(head * queries, (head + 1) * queries)
        weights_low = de_ref[rows + head * queries : rows + (head + 1) * queries, :]
        inverse = 1.0 / row_ref[part, :]
        attended = jnp.dot(weights_low, kv, preferred_element_type=jnp.float32) * inverse
        grad_wide = grad_rows[head].astype(jnp.float32)
        delta = jnp.sum(grad_wide * attended, axis=1, keepdims=True)
        row_ref[part, :] = delta * inverse
        grad_scaled = (grad_wide * inverse).astype(jnp.bfloat16)
        dp_ref[part, :] = lax.dot_general(grad_scaled, kv, transposed, preferred_element_type=jnp.float32)
        return attended, grad_scaled

    def backward(head):
        def one(index, carry):
            start = head * queries + index * CHUNK
            part = pl.ds(start, CHUNK)
            weights = de_ref[pl.ds(rows + start, CHUNK), :].astype(jnp.float32)
            score_grad = weights * (dp_ref[part, :] - row_ref[part, :1])
            acc_ref[part, :] += score_grad
            de_ref[part, :] = score_grad.astype(jnp.bfloat16)
            return carry

        lax.fori_loop(0, queries // CHUNK, one, 0, unroll=UNROLL)

    def query_of(head):
        return jnp.dot(
            de_ref[head * queries : (head + 1) * queries, :], kv, preferred_element_type=jnp.float32
        ) * scaling

    scores_of(0)
    scores_of(1)
    soften(0)
    att0, sc0 = cotangents(0)
    soften(1)
    att1, sc1 = cotangents(1)
    backward(0)
    q0 = query_of(0)
    backward(1)
    q1 = query_of(1)
    merged = jnp.where(
        lane < 2 * head_width,
        jnp.where(lane < head_width, q0, q1),
        jnp.where(lane < 3 * head_width, att0, att1),
    )
    qa_own_ref[0] = jnp.where(core == 0, merged[:half], merged[half:]).astype(jnp.bfloat16)
    qa_away_ref[0] = jnp.where(core == 0, merged[half:], merged[:half]).astype(jnp.bfloat16)
    sides = jnp.concatenate(query_rows + [sc0, sc1], axis=0)
    key_value = lax.dot_general(
        sides, de_ref[...], (((0,), (0,)), ((), ())), preferred_element_type=jnp.float32
    )
    key_value = key_value.T.astype(jnp.bfloat16)
    for group in range(PIECES):
        for side in range(2):
            start = group * queries + side * half
            target = 2 * place_ref[group] + (side + core) % 2
            dkv_ref[target, step] = key_value[start : start + half]

    @pl.when(step == last)
    def _():
        width = dbias_ref.shape[4]
        for piece in range(PIECES):
            for head in range(2):
                for side in range(2):
                    start = head * queries + side * half
                    part = acc_ref[start : start + half, piece * width : (piece + 1) * width]
                    dbias_ref[piece, (side + core) % 2, head] = part.astype(jnp.bfloat16)
        right_out_ref[...] = dkv_ref[12]
        left_out_ref[...] = dkv_ref[13]
        rest_out_ref[:12] = dkv_ref[:12]
        rest_out_ref[12:] = dkv_ref[14:]


def prepare_kernel(key_ref, value_ref, mask_ref, cotangent_ref, packed_ref):
    columns, tokens, channels = key_ref.shape
    half = channels // 2
    devices = packed_ref.shape[0]
    pairs = columns * tokens
    rows = cotangent_ref.shape[0] * cotangent_ref.shape[1]
    mask = mask_ref[...].astype(jnp.float32)
    mask = jnp.concatenate([mask, jnp.zeros((columns, channels - tokens), jnp.float32)], axis=1)
    filler = jnp.zeros((MASK_ROWS - columns, channels), jnp.float32)
    mask = jnp.concatenate([mask, filler], axis=0).astype(jnp.bfloat16)
    for column in range(columns):
        key = key_ref[column]
        value = value_ref[column]
        sides = [
            jnp.concatenate([key[:, :half], value[:, :half]], axis=1),
            jnp.concatenate([key[:, half:], value[:, half:]], axis=1),
        ]
        for device in range(devices):
            packed_ref[device, column * tokens : (column + 1) * tokens, :] = sides[device % 2]
    cotangent = cotangent_ref[...].astype(jnp.float32).reshape(rows, cotangent_ref.shape[2])
    filler = jnp.zeros((rows, channels - tokens), jnp.float32)
    for device in range(devices):
        part = cotangent[:, device * tokens : (device + 1) * tokens]
        part = jnp.concatenate([part, filler], axis=1).astype(jnp.bfloat16)
        packed_ref[device, pairs : pairs + rows, :] = part
        packed_ref[device, pairs + rows :, :] = mask


def prepare(key, value, mask, cotangent, devices):
    columns, tokens, channels = key.shape
    rows = columns * tokens + cotangent.shape[0] * cotangent.shape[1] + MASK_ROWS
    return pl.pallas_call(
        prepare_kernel,
        out_shape=jax.ShapeDtypeStruct((devices, rows, channels), jnp.bfloat16),
        compiler_params=pltpu.CompilerParams(vmem_limit_bytes=32 * 1024 * 1024),
        name="prepare_exchange",
    )(key, value, mask, cotangent)


def project_kernel(core_ref, packed_ref, weight_ref, gate_ref, query_ref, mine_ref, other_ref, slope_ref):
    pieces, rows, lanes = packed_ref.shape
    columns, tokens, channels = gate_ref.shape
    half = channels // 2
    core = core_ref[0]
    whole = packed_ref[...].astype(jnp.float32).reshape(pieces, columns, rows // columns, lanes)
    for column in range(columns):
        part = whole[:, column].reshape(channels, lanes).astype(jnp.bfloat16)
        gated = jnp.dot(weight_ref[...], part, preferred_element_type=jnp.float32).T[:tokens]
        sigma = jax.nn.sigmoid(gate_ref[column].astype(jnp.float32))
        grad = gated * sigma
        slope_ref[column] = grad * (1.0 - sigma)
        grad = grad.astype(jnp.bfloat16)
        query = query_ref[column]
        low = jnp.concatenate([query[:, :half], grad[:, :half]], axis=1)
        high = jnp.concatenate([query[:, half:], grad[:, half:]], axis=1)
        mine_ref[column] = jnp.where(core == 0, low, high)
        other_ref[column] = jnp.where(core == 0, high, low)


def project(core, packed, weight, gate, query):
    columns, tokens, channels = gate.shape
    rows = weight.shape[0] // packed.shape[0] * columns

    def whole(array):
        return pl.BlockSpec(array.shape, lambda i: (0,) * array.ndim)

    return pl.pallas_call(
        project_kernel,
        grid=(1,),
        in_specs=[
            pl.BlockSpec(memory_space=pltpu.SMEM),
            pl.BlockSpec((packed.shape[0], rows, channels), lambda i: (0, columns * tokens // rows, 0)),
            whole(weight),
            whole(gate),
            whole(query),
        ],
        out_specs=[whole(gate)] * 3,
        out_shape=[
            jax.ShapeDtypeStruct(gate.shape, jnp.bfloat16),
            jax.ShapeDtypeStruct(gate.shape, jnp.bfloat16),
            jax.ShapeDtypeStruct(gate.shape, jnp.float32),
        ],
        name="project_cotangent",
    )(core, packed, weight, gate, query)


def attend(places, mine, other, received, bias, row_count):
    columns, tokens, lanes = mine.shape
    rows, keys = bias.shape
    width = keys // row_count
    devices = received.shape[0]
    mask_place = received.shape[1] // MASK_ROWS - 1
    work = columns * rows * keys

    def whole(shape):
        return pl.BlockSpec(shape, lambda j, places: (0,) * len(shape))

    column_spec = pl.BlockSpec((1, tokens, lanes), lambda j, places: (j, 0, 0))
    piece = (2, tokens, width)
    return pl.pallas_call(
        attention_kernel,
        grid_spec=pltpu.PrefetchScalarGridSpec(
            num_scalar_prefetch=1,
            grid=(columns,),
            in_specs=[column_spec, column_spec]
            + [
                pl.BlockSpec((devices, tokens, lanes), lambda j, places: (0, j, 0)),
                pl.BlockSpec((devices, MASK_ROWS, lanes), lambda j, places: (0, mask_place, 0)),
                whole(bias.shape),
            ],
            out_specs=[
                column_spec,
                column_spec,
                whole(mine.shape),
                whole(mine.shape),
                whole((14,) + mine.shape),
                whole((row_count, 2) + piece),
            ],
            scratch_shapes=[
                pltpu.VMEM((columns, 1, keys), jnp.float32),
                pltpu.VMEM((rows, keys), jnp.float32),
                pltpu.VMEM((rows, keys), jnp.float32),
                pltpu.VMEM((rows, keys), jnp.float32),
                pltpu.VMEM((rows, keys), jnp.float32),
                pltpu.VMEM((2 * rows, keys), jnp.bfloat16),
                pltpu.VMEM((rows, 128), jnp.float32),
                pltpu.VMEM((16,) + mine.shape, jnp.bfloat16),
            ],
        ),
        out_shape=[
            jax.ShapeDtypeStruct(mine.shape, jnp.bfloat16),
            jax.ShapeDtypeStruct(mine.shape, jnp.bfloat16),
            jax.ShapeDtypeStruct(mine.shape, jnp.bfloat16),
            jax.ShapeDtypeStruct(mine.shape, jnp.bfloat16),
            jax.ShapeDtypeStruct((14,) + mine.shape, jnp.bfloat16),
            jax.ShapeDtypeStruct((row_count, 2) + piece, jnp.bfloat16),
        ],
        compiler_params=pltpu.CompilerParams(vmem_limit_bytes=48 * 1024 * 1024),
        cost_estimate=pl.CostEstimate(flops=12 * 128 * work, bytes_accessed=16 * 2**20, transcendentals=work),
        name="attention_both",
    )(places, mine, other, received, received, bias)


def local(
    query_vectors,
    key_vectors,
    value_vectors,
    gate_logits,
    pair_bias,
    pair_mask,
    output_weight,
    output_cotangent,
):
    columns, tokens, channels = query_vectors.shape
    half = channels // 2
    devices = lax.axis_size("col")
    row_count = lax.axis_size("row")
    chips = devices // 2
    core = lax.axis_index("col") % 2
    scaling = 1.0 / math.sqrt(channels // HEADS)
    swap = [(index, index ^ 1) for index in range(devices)]
    chip_groups = [[2 * chip + side for chip in range(chips)] for side in range(2)]
    keys = pair_bias.shape[2]

    def mine_other(array, axis):
        size = array.shape[axis] // 2
        low = lax.slice_in_dim(array, 0, size, axis=axis)
        high = lax.slice_in_dim(array, size, 2 * size, axis=axis)
        return jnp.where(core == 0, low, high), jnp.where(core == 0, high, low)

    def in_order(mine, other, axis):
        return jnp.where(
            core == 0,
            jnp.concatenate([mine, other], axis=axis),
            jnp.concatenate([other, mine], axis=axis),
        )

    def swapped(array):
        return lax.ppermute(array, "col", swap)

    bias_mine, bias_other = mine_other(pair_bias, 0)
    bias_pair = in_order(bias_mine, swapped(bias_other), 1).reshape(-1, keys)

    core_word = core.astype(jnp.int32).reshape(1)
    ring = chips // 2

    def along(array, turn, side):
        pairs = []
        for index in range(devices):
            high, low = index // (2 * ring), index // 2 % ring
            target = ((high + side) % 2) * ring + (low + turn) % ring
            pairs.append((index, 2 * target + index % 2))
        return lax.ppermute(array, "col", pairs)

    packed = prepare(key_vectors, value_vectors, pair_mask, output_cotangent, devices)
    received = lax.all_to_all(packed, "col", 0, 0, tiled=True)
    chip = lax.axis_index("col") // 2
    places = [
        ring * ((index // ring - chip // ring) % 2) + (index % ring - chip % ring) % ring
        for index in range(chips)
    ]
    places.append(core)
    places = jnp.stack(places).astype(jnp.int32)

    qd_mine, qd_away, gate_slope = project(core_word, received, output_weight, gate_logits, query_vectors)

    qa_own, qa_away, kv_right, kv_left, kv_rest, bias_grads = attend(
        places, qd_mine, swapped(qd_away), received, bias_pair, row_count
    )


    def added(*parts):
        return sum(part.astype(jnp.float32) for part in parts)

    def both(*parts):
        return lax.optimization_barrier(parts)

    def low(*parts):
        return added(*parts).astype(jnp.bfloat16)

    home, near, far, behind = kv_rest[:2], kv_rest[2:4], kv_rest[4:6], kv_rest[6:8]
    home_across, near_across, behind_across = kv_rest[8:10], kv_rest[10:12], kv_rest[12:]
    from_left, from_right = both(along(kv_right, 1, 0), along(kv_left, -1, 0))
    onward = jnp.concatenate([low(near_across[:1], from_left[None]), near_across[1:], far[:1]])
    backward = jnp.concatenate([behind_across[:1], low(behind_across[1:], from_right[None]), far[1:]])
    onward, backward, bias_grads = both(onward, backward, bias_grads)
    bias_parts = lax.all_to_all(bias_grads, "row", 0, 0, tiled=True)
    from_left, from_right = both(along(onward, 1, 0), along(backward, -1, 0))
    from_across = along(low(home_across, from_left[:2], from_right[:2]), 0, 1)
    onward = jnp.concatenate([low(near[:1], from_left[2:]), near[1:]])
    backward = jnp.concatenate([behind[:1], low(behind[1:], from_right[2:])])
    kv_sum = low(home, along(onward, 1, 0), along(backward, -1, 0), from_across)
    kv_back = swapped(kv_sum[1])
    key_gradient = in_order(kv_sum[0, ..., :half], kv_back[..., :half], 2)
    key_gradient = (key_gradient.astype(jnp.float32) * scaling).astype(jnp.bfloat16)
    value_gradient = in_order(kv_sum[0, ..., half:], kv_back[..., half:], 2)

    qa_back = swapped(qa_away)
    query_gradient = in_order(qa_own[..., :half], qa_back[..., :half], 2)
    attended = in_order(qa_own[..., half:], qa_back[..., half:], 2).astype(jnp.float32)
    gate_gradient = (gate_slope * attended).astype(jnp.bfloat16)

    bias_sum = jnp.sum(bias_parts.astype(jnp.float32), axis=0)
    bias_gradient = in_order(
        bias_sum[0], swapped(bias_sum[1].astype(jnp.bfloat16)).astype(jnp.float32), 0
    )
    return (query_gradient, key_gradient, value_gradient, gate_gradient, bias_gradient)


def solution(mesh):
    placed = (
        P("row", "col", None),
        P("row", "col", None),
        P("row", "col", None),
        P("row", "col", None),
        P(None, "col", None),
        P("row", "col"),
        P(),
        P("row", "col", None),
    )
    return jax.shard_map(
        local,
        mesh=mesh,
        in_specs=placed,
        out_specs=(
            P("row", "col", None),
            P("row", "col", None),
            P("row", "col", None),
            P("row", "col", None),
            P(None, "col", "row"),
        ),
        check_vma=False,
    )
```

```python
import math

import jax
import jax.numpy as jnp
from jax import lax
from jax.experimental import pallas as pl
from jax.experimental.pallas import tpu as pltpu
from jax.sharding import PartitionSpec as P

HEADS = 4
NEG_FILL = -1000000000.0
LOG2E = math.log2(math.e)
CHUNK = 16
UNROLL = 12
MASK_ROWS = 16
PIECES = 8
VMEM_WIDE = 60 * 1024 * 1024


def attention_kernel(
    place_ref,
    qd_mine_ref,
    qd_other_ref,
    kv_ref,
    mask_ref,
    bias_ref,
    qa_own_ref,
    qa_away_ref,
    dkv_ref,
    right_out_ref,
    left_out_ref,
    rest_out_ref,
    cap_ref,
    s_ref,
    b2_ref,
    acc_ref,
    dp_ref,
    de_ref,
    row_ref,
    dbias_ref,
):
    step = pl.program_id(0)
    last = pl.num_programs(0) - 1
    rows = bias_ref.shape[0]
    queries = rows // 2
    keys = bias_ref.shape[1]
    head_width = qd_mine_ref.shape[2] // 4
    core = place_ref[PIECES]
    scaling = 1.0 / math.sqrt(head_width)

    @pl.when(step == 0)
    def _():
        def fill(index, carry):
            part = pl.ds(index * CHUNK, CHUNK)
            b2_ref[part, :] = bias_ref[part, :].astype(jnp.float32) * LOG2E
            acc_ref[part, :] = jnp.zeros((CHUNK, keys), jnp.float32)
            return carry

        lax.fori_loop(0, rows // CHUNK, fill, 0)
        masks = mask_ref[...].astype(jnp.float32)
        for column in range(cap_ref.shape[0]):
            pieces = [
                masks[source, column : column + 1, : queries // 2] for source in range(masks.shape[0])
            ]
            cap_ref[column] = jnp.where(
                jnp.concatenate(pieces, axis=1) > 0.5, 1e30, NEG_FILL * LOG2E
            )

    half = queries // 2
    kv = kv_ref[...].reshape(keys, 4 * head_width)
    qd_mine = qd_mine_ref[0]
    qd_other = qd_other_ref[0]
    qd = jnp.concatenate(
        [jnp.where(core == 0, qd_mine, qd_other), jnp.where(core == 0, qd_other, qd_mine)], axis=0
    )
    lane = lax.broadcasted_iota(jnp.int32, (queries, 4 * head_width), 1)
    zero = jnp.zeros_like(qd)

    def only(part):
        return jnp.where((lane >= part * head_width) & (lane < (part + 1) * head_width), qd, zero)

    transposed = (((1,), (1,)), ((), ()))
    cap = cap_ref[step]
    query_rows = [only(0), only(1)]
    grad_rows = [only(2), only(3)]

    def scores_of(head):
        s_ref[head * queries : (head + 1) * queries, :] = lax.dot_general(
            query_rows[head], kv, transposed, preferred_element_type=jnp.float32
        )

    def soften(head):
        def one(index, carry):
            start = head * queries + index * CHUNK
            part = pl.ds(start, CHUNK)
            scores = jnp.minimum(s_ref[part, :] * (scaling * LOG2E) + b2_ref[part, :], cap)
            weights = jnp.exp2(scores - jnp.max(scores, axis=1, keepdims=True))
            row_ref[part, :] = jnp.broadcast_to(jnp.sum(weights, axis=1, keepdims=True), (CHUNK, 128))
            de_ref[pl.ds(rows + start, CHUNK), :] = weights.astype(jnp.bfloat16)
            return carry

        lax.fori_loop(0, queries // CHUNK, one, 0, unroll=UNROLL)

    def cotangents(head):
        part = slice(head * queries, (head + 1) * queries)
        weights_low = de_ref[rows + head * queries : rows + (head + 1) * queries, :]
        inverse = 1.0 / row_ref[part, :]
        attended = jnp.dot(weights_low, kv, preferred_element_type=jnp.float32) * inverse
        grad_wide = grad_rows[head].astype(jnp.float32)
        delta = jnp.sum(grad_wide * attended, axis=1, keepdims=True)
        row_ref[part, :] = delta * inverse
        grad_scaled = (grad_wide * inverse).astype(jnp.bfloat16)
        dp_ref[part, :] = lax.dot_general(grad_scaled, kv, transposed, preferred_element_type=jnp.float32)
        return attended, grad_scaled

    def backward(head):
        def one(index, carry):
            start = head * queries + index * CHUNK
            part = pl.ds(start, CHUNK)
            weights = de_ref[pl.ds(rows + start, CHUNK), :].astype(jnp.float32)
            score_grad = weights * (dp_ref[part, :] - row_ref[part, :1])
            acc_ref[part, :] += score_grad
            de_ref[part, :] = score_grad.astype(jnp.bfloat16)
            return carry

        lax.fori_loop(0, queries // CHUNK, one, 0, unroll=UNROLL)

    def query_of(head):
        return jnp.dot(
            de_ref[head * queries : (head + 1) * queries, :], kv, preferred_element_type=jnp.float32
        ) * scaling

    scores_of(0)
    scores_of(1)
    soften(0)
    att0, sc0 = cotangents(0)
    soften(1)
    att1, sc1 = cotangents(1)
    backward(0)
    q0 = query_of(0)
    backward(1)
    q1 = query_of(1)
    merged = jnp.where(
        lane < 2 * head_width,
        jnp.where(lane < head_width, q0, q1),
        jnp.where(lane < 3 * head_width, att0, att1),
    )
    qa_own_ref[0] = jnp.where(core == 0, merged[:half], merged[half:]).astype(jnp.bfloat16)
    qa_away_ref[0] = jnp.where(core == 0, merged[half:], merged[:half]).astype(jnp.bfloat16)
    sides = jnp.concatenate(query_rows + [sc0, sc1], axis=0)
    key_value = lax.dot_general(
        sides, de_ref[...], (((0,), (0,)), ((), ())), preferred_element_type=jnp.float32
    )
    dkv_ref[...] = key_value.T.astype(jnp.bfloat16).reshape(dkv_ref.shape)

    @pl.when(step == last)
    def _():
        width = dbias_ref.shape[3]
        for piece in range(PIECES):
            for head in range(2):
                for side in range(2):
                    start = head * queries + side * half
                    part = acc_ref[start : start + half, piece * width : (piece + 1) * width]
                    target = 2 * place_ref[piece] + (side + core) % 2
                    dbias_ref[target, head] = part.astype(jnp.bfloat16)
        right_out_ref[...] = dbias_ref[8:10]
        left_out_ref[...] = dbias_ref[10:12]
        rest_out_ref[:8] = dbias_ref[:8]
        rest_out_ref[8:] = dbias_ref[12:]


def prepare_kernel(key_ref, value_ref, mask_ref, cotangent_ref, packed_ref):
    columns, tokens, channels = key_ref.shape
    half = channels // 2
    devices = packed_ref.shape[0]
    pairs = columns * tokens
    rows = cotangent_ref.shape[0] * cotangent_ref.shape[1]
    mask = mask_ref[...].astype(jnp.float32)
    mask = jnp.concatenate([mask, jnp.zeros((columns, channels - tokens), jnp.float32)], axis=1)
    filler = jnp.zeros((MASK_ROWS - columns, channels), jnp.float32)
    mask = jnp.concatenate([mask, filler], axis=0).astype(jnp.bfloat16)
    for column in range(columns):
        key = key_ref[column]
        value = value_ref[column]
        sides = [
            jnp.concatenate([key[:, :half], value[:, :half]], axis=1),
            jnp.concatenate([key[:, half:], value[:, half:]], axis=1),
        ]
        for device in range(devices):
            packed_ref[device, column * tokens : (column + 1) * tokens, :] = sides[device % 2]
    cotangent = cotangent_ref[...].astype(jnp.float32).reshape(rows, cotangent_ref.shape[2])
    filler = jnp.zeros((rows, channels - tokens), jnp.float32)
    for device in range(devices):
        part = cotangent[:, device * tokens : (device + 1) * tokens]
        part = jnp.concatenate([part, filler], axis=1).astype(jnp.bfloat16)
        packed_ref[device, pairs : pairs + rows, :] = part
        packed_ref[device, pairs + rows :, :] = mask


def prepare(key, value, mask, cotangent, devices):
    columns, tokens, channels = key.shape
    rows = columns * tokens + cotangent.shape[0] * cotangent.shape[1] + MASK_ROWS

    def whole(shape):
        return pl.BlockSpec(shape, lambda i: (0,) * len(shape))

    out = (devices, rows, channels)
    return pl.pallas_call(
        prepare_kernel,
        grid=(1,),
        in_specs=[whole(key.shape), whole(value.shape), whole(mask.shape), whole(cotangent.shape)],
        out_specs=whole(out),
        out_shape=jax.ShapeDtypeStruct(out, jnp.bfloat16),
        compiler_params=pltpu.CompilerParams(vmem_limit_bytes=VMEM_WIDE),
        name="prepare_exchange",
    )(key, value, mask, cotangent)


def project_kernel(core_ref, packed_ref, weight_ref, gate_ref, query_ref, mine_ref, other_ref, slope_ref):
    pieces, rows, lanes = packed_ref.shape
    columns, tokens, channels = gate_ref.shape
    half = channels // 2
    core = core_ref[0]
    whole = packed_ref[...].astype(jnp.float32).reshape(pieces, columns, rows // columns, lanes)
    for column in range(columns):
        part = whole[:, column].reshape(channels, lanes).astype(jnp.bfloat16)
        gated = jnp.dot(weight_ref[...], part, preferred_element_type=jnp.float32).T[:tokens]
        sigma = jax.nn.sigmoid(gate_ref[column].astype(jnp.float32))
        grad = gated * sigma
        slope_ref[column] = grad * (1.0 - sigma)
        grad = grad.astype(jnp.bfloat16)
        query = query_ref[column]
        low = jnp.concatenate([query[:, :half], grad[:, :half]], axis=1)
        high = jnp.concatenate([query[:, half:], grad[:, half:]], axis=1)
        mine_ref[column] = jnp.where(core == 0, low, high)
        other_ref[column] = jnp.where(core == 0, high, low)


def project(core, packed, weight, gate, query):
    columns, tokens, channels = gate.shape
    rows = weight.shape[0] // packed.shape[0] * columns

    def whole(array):
        return pl.BlockSpec(array.shape, lambda i: (0,) * array.ndim)

    return pl.pallas_call(
        project_kernel,
        grid=(1,),
        in_specs=[
            pl.BlockSpec(memory_space=pltpu.SMEM),
            pl.BlockSpec((packed.shape[0], rows, channels), lambda i: (0, columns * tokens // rows, 0)),
            whole(weight),
            whole(gate),
            whole(query),
        ],
        out_specs=[whole(gate)] * 3,
        out_shape=[
            jax.ShapeDtypeStruct(gate.shape, jnp.bfloat16),
            jax.ShapeDtypeStruct(gate.shape, jnp.bfloat16),
            jax.ShapeDtypeStruct(gate.shape, jnp.float32),
        ],
        compiler_params=pltpu.CompilerParams(vmem_limit_bytes=VMEM_WIDE),
        name="project_cotangent",
    )(core, packed, weight, gate, query)


def total_kernel(parts_ref, key_ref, value_ref):
    half = key_ref.shape[2] // 2
    scaling = 1.0 / math.sqrt(key_ref.shape[2] // HEADS)
    for column in range(key_ref.shape[0]):
        sums = [
            jnp.sum(parts_ref[:, side, column].astype(jnp.float32), axis=0) for side in range(2)
        ]
        key = jnp.concatenate([part[:, :half] for part in sums], axis=1) * scaling
        key_ref[column] = key.astype(jnp.bfloat16)
        value = jnp.concatenate([part[:, half:] for part in sums], axis=1)
        value_ref[column] = value.astype(jnp.bfloat16)


def total(parts, like):
    out = jax.ShapeDtypeStruct(like.shape, jnp.bfloat16)
    return pl.pallas_call(total_kernel, out_shape=[out, out], compiler_params=pltpu.CompilerParams(vmem_limit_bytes=VMEM_WIDE), name="total_key_value")(parts)


def attend(places, mine, other, received, bias, row_count):
    columns, tokens, lanes = mine.shape
    rows, keys = bias.shape
    width = keys // row_count
    devices = received.shape[0]
    mask_place = received.shape[1] // MASK_ROWS - 1
    work = columns * rows * keys

    def whole(shape):
        return pl.BlockSpec(shape, lambda j, places: (0,) * len(shape))

    column_spec = pl.BlockSpec((1, tokens, lanes), lambda j, places: (j, 0, 0))
    piece = (2, tokens, width)
    return pl.pallas_call(
        attention_kernel,
        grid_spec=pltpu.PrefetchScalarGridSpec(
            num_scalar_prefetch=1,
            grid=(columns,),
            in_specs=[column_spec, column_spec]
            + [
                pl.BlockSpec((devices, tokens, lanes), lambda j, places: (0, j, 0)),
                pl.BlockSpec((devices, MASK_ROWS, lanes), lambda j, places: (0, mask_place, 0)),
                whole(bias.shape),
            ],
            out_specs=[
                column_spec,
                column_spec,
                pl.BlockSpec((devices, 1, tokens, lanes), lambda j, places: (0, j, 0, 0)),
                whole((2,) + piece),
                whole((2,) + piece),
                whole((12,) + piece),
            ],
            scratch_shapes=[
                pltpu.VMEM((columns, 1, keys), jnp.float32),
                pltpu.VMEM((rows, keys), jnp.float32),
                pltpu.VMEM((rows, keys), jnp.float32),
                pltpu.VMEM((rows, keys), jnp.float32),
                pltpu.VMEM((rows, keys), jnp.float32),
                pltpu.VMEM((2 * rows, keys), jnp.bfloat16),
                pltpu.VMEM((rows, 128), jnp.float32),
                pltpu.VMEM((16,) + piece, jnp.bfloat16),
            ],
        ),
        out_shape=[
            jax.ShapeDtypeStruct(mine.shape, jnp.bfloat16),
            jax.ShapeDtypeStruct(mine.shape, jnp.bfloat16),
            jax.ShapeDtypeStruct((devices,) + mine.shape, jnp.bfloat16),
            jax.ShapeDtypeStruct((2,) + piece, jnp.bfloat16),
            jax.ShapeDtypeStruct((2,) + piece, jnp.bfloat16),
            jax.ShapeDtypeStruct((12,) + piece, jnp.bfloat16),
        ],
        compiler_params=pltpu.CompilerParams(vmem_limit_bytes=48 * 1024 * 1024),
        cost_estimate=pl.CostEstimate(flops=12 * 128 * work, bytes_accessed=16 * 2**20, transcendentals=work),
        name="attention_both",
    )(places, mine, other, received, received, bias)


def local(
    query_vectors,
    key_vectors,
    value_vectors,
    gate_logits,
    pair_bias,
    pair_mask,
    output_weight,
    output_cotangent,
):
    columns, tokens, channels = query_vectors.shape
    half = channels // 2
    devices = lax.axis_size("col")
    row_count = lax.axis_size("row")
    core = lax.axis_index("col") % 2
    scaling = 1.0 / math.sqrt(channels // HEADS)
    swap = [(index, index ^ 1) for index in range(devices)]
    keys = pair_bias.shape[2]

    def mine_other(array, axis):
        size = array.shape[axis] // 2
        low = lax.slice_in_dim(array, 0, size, axis=axis)
        high = lax.slice_in_dim(array, size, 2 * size, axis=axis)
        return jnp.where(core == 0, low, high), jnp.where(core == 0, high, low)

    def in_order(mine, other, axis):
        return jnp.where(
            core == 0,
            jnp.concatenate([mine, other], axis=axis),
            jnp.concatenate([other, mine], axis=axis),
        )

    def swapped(array):
        return lax.ppermute(array, "col", swap)

    bias_mine, bias_other = mine_other(pair_bias, 0)
    bias_pair = in_order(bias_mine, swapped(bias_other), 1).reshape(-1, keys)

    core_word = core.astype(jnp.int32).reshape(1)
    packed = prepare(key_vectors, value_vectors, pair_mask, output_cotangent, devices)
    received = lax.all_to_all(packed, "col", 0, 0, tiled=True)
    place = lax.axis_index("row")
    row_ring = row_count // 2
    places = [
        2 * ((index % row_ring - place) % row_ring) + (index // row_ring - place // row_ring) % 2
        for index in range(row_count)
    ]
    places.append(core)
    places = jnp.stack(places).astype(jnp.int32)

    qd_mine, qd_away, gate_slope = project(core_word, received, output_weight, gate_logits, query_vectors)

    qa_own, qa_away, kv_grads, bias_right, bias_left, bias_rest = attend(
        places, qd_mine, swapped(qd_away), received, bias_pair, row_count
    )

    qa_back = swapped(qa_away)
    query_gradient = in_order(qa_own[..., :half], qa_back[..., :half], 2)
    attended = in_order(qa_own[..., half:], qa_back[..., half:], 2).astype(jnp.float32)
    gate_gradient = (gate_slope * attended).astype(jnp.bfloat16)

    def along_row(array, turn, side):
        pairs = []
        for index in range(row_count):
            high, low = index // row_ring, index % row_ring
            pairs.append((index, ((high + side) % 2) * row_ring + (low + turn) % row_ring))
        return lax.ppermute(array, "row", pairs)

    def added(*parts):
        return sum(part.astype(jnp.float32) for part in parts)

    from_left = along_row(bias_right, 1, 0)
    from_right = along_row(bias_left, -1, 0)
    from_left, from_right, kv_grads = lax.optimization_barrier((from_left, from_right, kv_grads))
    kv_parts = lax.all_to_all(kv_grads, "col", 0, 0, tiled=True)
    kv_parts = kv_parts.reshape((devices // 2, 2) + kv_parts.shape[1:])
    key_gradient, value_gradient = total(kv_parts, key_vectors)
    onward = jnp.concatenate([added(bias_rest[4:6], from_left).astype(jnp.bfloat16), bias_rest[6:8]])
    backward = jnp.concatenate([bias_rest[8:10], added(bias_rest[10:], from_right).astype(jnp.bfloat16)])
    sums = added(bias_rest[:4], along_row(onward, 1, 0), along_row(backward, -1, 0))
    low_sums = sums.astype(jnp.bfloat16)
    diagonal = []
    for index in range(row_count * devices):
        up = (index // devices + row_ring) % row_count
        diagonal.append((index, up * devices + (index % devices ^ 1)))
    bias_own = added(sums[0], along_row(low_sums[2], 0, 1))
    bias_away = added(swapped(low_sums[1]), lax.ppermute(low_sums[3], ("row", "col"), diagonal))
    bias_gradient = in_order(bias_own, bias_away, 0)
    return (query_gradient, key_gradient, value_gradient, gate_gradient, bias_gradient)


def solution(mesh):
    placed = (
        P("row", "col", None),
        P("row", "col", None),
        P("row", "col", None),
        P("row", "col", None),
        P(None, "col", None),
        P("row", "col"),
        P(),
        P("row", "col", None),
    )
    return jax.shard_map(
        local,
        mesh=mesh,
        in_specs=placed,
        out_specs=(
            P("row", "col", None),
            P("row", "col", None),
            P("row", "col", None),
            P("row", "col", None),
            P(None, "col", "row"),
        ),
        check_vma=False,
    )
```

```python
import math

import jax
import jax.numpy as jnp
from jax import lax
from jax.experimental import pallas as pl
from jax.experimental.pallas import tpu as pltpu
from jax.sharding import PartitionSpec as P

HEADS = 4
NEG_FILL = -1000000000.0
LOG2E = math.log2(math.e)
CHUNK = 16
UNROLL = 12
MASK_ROWS = 16
PIECES = 8
VMEM_WIDE = 60 * 1024 * 1024


def attention_kernel(
    place_ref,
    qg_mine_ref,
    qg_other_ref,
    kv_ref,
    mask_ref,
    cotangent_ref,
    weight_ref,
    bias_ref,
    qa_own_ref,
    qa_away_ref,
    dkv_ref,
    right_out_ref,
    left_out_ref,
    rest_out_ref,
    gated_ref,
    cap_ref,
    s_ref,
    b2_ref,
    acc_ref,
    dp_ref,
    de_ref,
    row_ref,
    dbias_ref,
):
    step = pl.program_id(0)
    last = pl.num_programs(0) - 1
    rows = bias_ref.shape[0]
    queries = rows // 2
    keys = bias_ref.shape[1]
    head_width = qg_mine_ref.shape[2] // 4
    core = place_ref[PIECES]
    scaling = 1.0 / math.sqrt(head_width)

    @pl.when(step == 0)
    def _():
        def fill(index, carry):
            part = pl.ds(index * CHUNK, CHUNK)
            b2_ref[part, :] = bias_ref[part, :].astype(jnp.float32) * LOG2E
            acc_ref[part, :] = jnp.zeros((CHUNK, keys), jnp.float32)
            return carry

        lax.fori_loop(0, rows // CHUNK, fill, 0)
        sources, _, lanes = cotangent_ref.shape
        cotangent = cotangent_ref[...].astype(jnp.float32)
        cotangent = cotangent.reshape(sources, 2, cap_ref.shape[0], lanes // sources, lanes)
        for column in range(cotangent.shape[2]):
            for side in range(2):
                part = cotangent[:, side, column].reshape(lanes, lanes).astype(jnp.bfloat16)
                gated = jnp.dot(weight_ref[...], part, preferred_element_type=jnp.float32)
                gated_ref[column, side * queries // 2 : (side + 1) * queries // 2] = gated.T[: queries // 2]
        masks = mask_ref[...].astype(jnp.float32)
        for column in range(cap_ref.shape[0]):
            pieces = [
                masks[source, column : column + 1, : queries // 2] for source in range(masks.shape[0])
            ]
            cap_ref[column] = jnp.where(
                jnp.concatenate(pieces, axis=1) > 0.5, 1e30, NEG_FILL * LOG2E
            )

    half = queries // 2
    kv = kv_ref[...].reshape(keys, 4 * head_width)
    qg_mine = qg_mine_ref[0]
    qg_other = qg_other_ref[0]
    query_gate = jnp.concatenate(
        [jnp.where(core == 0, qg_mine, qg_other), jnp.where(core == 0, qg_other, qg_mine)], axis=0
    )
    sigma = jax.nn.sigmoid(query_gate.astype(jnp.float32))
    gated_grad = gated_ref[step] * sigma
    gate_slope = gated_grad * (1.0 - sigma)
    lane = lax.broadcasted_iota(jnp.int32, (queries, 4 * head_width), 1)
    qd = jnp.where(lane < 2 * head_width, query_gate, gated_grad.astype(jnp.bfloat16))
    zero = jnp.zeros_like(qd)

    def only(part):
        return jnp.where((lane >= part * head_width) & (lane < (part + 1) * head_width), qd, zero)

    transposed = (((1,), (1,)), ((), ()))
    cap = cap_ref[step]
    query_rows = [only(0), only(1)]
    grad_rows = [only(2), only(3)]

    def scores_of(head):
        s_ref[head * queries : (head + 1) * queries, :] = lax.dot_general(
            query_rows[head], kv, transposed, preferred_element_type=jnp.float32
        )

    def soften(head):
        def one(index, carry):
            start = head * queries + index * CHUNK
            part = pl.ds(start, CHUNK)
            scores = jnp.minimum(s_ref[part, :] * (scaling * LOG2E) + b2_ref[part, :], cap)
            weights = jnp.exp2(scores - jnp.max(scores, axis=1, keepdims=True))
            row_ref[part, :] = jnp.broadcast_to(jnp.sum(weights, axis=1, keepdims=True), (CHUNK, 128))
            de_ref[pl.ds(rows + start, CHUNK), :] = weights.astype(jnp.bfloat16)
            return carry

        lax.fori_loop(0, queries // CHUNK, one, 0, unroll=UNROLL)

    def cotangents(head):
        part = slice(head * queries, (head + 1) * queries)
        weights_low = de_ref[rows + head * queries : rows + (head + 1) * queries, :]
        inverse = 1.0 / row_ref[part, :]
        attended = jnp.dot(weights_low, kv, preferred_element_type=jnp.float32) * inverse
        grad_wide = grad_rows[head].astype(jnp.float32)
        delta = jnp.sum(grad_wide * attended, axis=1, keepdims=True)
        row_ref[part, :] = delta * inverse
        grad_scaled = (grad_wide * inverse).astype(jnp.bfloat16)
        dp_ref[part, :] = lax.dot_general(grad_scaled, kv, transposed, preferred_element_type=jnp.float32)
        return attended, grad_scaled

    def backward(head):
        def one(index, carry):
            start = head * queries + index * CHUNK
            part = pl.ds(start, CHUNK)
            weights = de_ref[pl.ds(rows + start, CHUNK), :].astype(jnp.float32)
            score_grad = weights * (dp_ref[part, :] - row_ref[part, :1])
            acc_ref[part, :] += score_grad
            de_ref[part, :] = score_grad.astype(jnp.bfloat16)
            return carry

        lax.fori_loop(0, queries // CHUNK, one, 0, unroll=UNROLL)

    def query_of(head):
        return jnp.dot(
            de_ref[head * queries : (head + 1) * queries, :], kv, preferred_element_type=jnp.float32
        ) * scaling

    scores_of(0)
    scores_of(1)
    soften(0)
    att0, sc0 = cotangents(0)
    soften(1)
    att1, sc1 = cotangents(1)
    backward(0)
    q0 = query_of(0)
    backward(1)
    q1 = query_of(1)
    merged = jnp.where(
        lane < 2 * head_width,
        jnp.where(lane < head_width, q0, q1),
        jnp.where(lane < 3 * head_width, att0, att1) * gate_slope,
    )
    qa_own_ref[0] = jnp.where(core == 0, merged[:half], merged[half:]).astype(jnp.bfloat16)
    qa_away_ref[0] = jnp.where(core == 0, merged[half:], merged[:half]).astype(jnp.bfloat16)
    sides = jnp.concatenate(query_rows + [sc0, sc1], axis=0)
    key_value = lax.dot_general(
        sides, de_ref[...], (((0,), (0,)), ((), ())), preferred_element_type=jnp.float32
    )
    dkv_ref[...] = key_value.T.astype(jnp.bfloat16).reshape(dkv_ref.shape)

    @pl.when(step == last)
    def _():
        width = dbias_ref.shape[3]
        for piece in range(PIECES):
            for head in range(2):
                for side in range(2):
                    start = head * queries + side * half
                    part = acc_ref[start : start + half, piece * width : (piece + 1) * width]
                    target = 2 * place_ref[piece] + (side + core) % 2
                    dbias_ref[target, head] = part.astype(jnp.bfloat16)
        right_out_ref[...] = dbias_ref[8:10]
        left_out_ref[...] = dbias_ref[10:12]
        rest_out_ref[:8] = dbias_ref[:8]
        rest_out_ref[8:] = dbias_ref[12:]


def prepare_kernel(key_ref, value_ref, mask_ref, cotangent_ref, packed_ref):
    columns, tokens, channels = key_ref.shape
    half = channels // 2
    devices = packed_ref.shape[0]
    pairs = columns * tokens
    rows = cotangent_ref.shape[0] * cotangent_ref.shape[1]
    mask = mask_ref[...].astype(jnp.float32)
    mask = jnp.concatenate([mask, jnp.zeros((columns, channels - tokens), jnp.float32)], axis=1)
    filler = jnp.zeros((MASK_ROWS - columns, channels), jnp.float32)
    mask = jnp.concatenate([mask, filler], axis=0).astype(jnp.bfloat16)
    for column in range(columns):
        key = key_ref[column]
        value = value_ref[column]
        sides = [
            jnp.concatenate([key[:, :half], value[:, :half]], axis=1),
            jnp.concatenate([key[:, half:], value[:, half:]], axis=1),
        ]
        for device in range(devices):
            packed_ref[device, column * tokens : (column + 1) * tokens, :] = sides[device % 2]
    cotangent = cotangent_ref[...].astype(jnp.float32).reshape(rows, cotangent_ref.shape[2])
    filler = jnp.zeros((rows, channels - tokens), jnp.float32)
    for device in range(devices):
        packed_ref[device, pairs + 2 * rows :, :] = mask
        part = cotangent[:, device * tokens : (device + 1) * tokens]
        part = jnp.concatenate([part, filler], axis=1).astype(jnp.bfloat16)
        start = pairs + device % 2 * rows
        packed_ref[device, start : start + rows, :] = part
        packed_ref[device ^ 1, start : start + rows, :] = part


def prepare(key, value, mask, cotangent, devices):
    columns, tokens, channels = key.shape
    rows = columns * tokens + 2 * cotangent.shape[0] * cotangent.shape[1] + MASK_ROWS

    def whole(shape):
        return pl.BlockSpec(shape, lambda i: (0,) * len(shape))

    out = (devices, rows, channels)
    return pl.pallas_call(
        prepare_kernel,
        grid=(1,),
        in_specs=[whole(key.shape), whole(value.shape), whole(mask.shape), whole(cotangent.shape)],
        out_specs=whole(out),
        out_shape=jax.ShapeDtypeStruct(out, jnp.bfloat16),
        compiler_params=pltpu.CompilerParams(vmem_limit_bytes=VMEM_WIDE),
        name="prepare_exchange",
    )(key, value, mask, cotangent)


def attend(places, mine, other, received, weight, bias, row_count):
    columns, tokens, lanes = mine.shape
    rows, keys = bias.shape
    width = keys // row_count
    devices = received.shape[0]
    mask_place = received.shape[1] // MASK_ROWS - 1
    cotangent_rows = 2 * columns * lanes // devices
    cotangent_place = columns * tokens // cotangent_rows
    work = columns * rows * keys

    def whole(shape):
        return pl.BlockSpec(shape, lambda j, places: (0,) * len(shape))

    column_spec = pl.BlockSpec((1, tokens, lanes), lambda j, places: (j, 0, 0))
    piece = (2, tokens, width)
    return pl.pallas_call(
        attention_kernel,
        grid_spec=pltpu.PrefetchScalarGridSpec(
            num_scalar_prefetch=1,
            grid=(columns,),
            in_specs=[column_spec, column_spec]
            + [
                pl.BlockSpec((devices, tokens, lanes), lambda j, places: (0, j, 0)),
                pl.BlockSpec((devices, MASK_ROWS, lanes), lambda j, places: (0, mask_place, 0)),
                pl.BlockSpec(
                    (devices, cotangent_rows, lanes), lambda j, places: (0, cotangent_place, 0)
                ),
                whole(weight.shape),
                whole(bias.shape),
            ],
            out_specs=[
                column_spec,
                column_spec,
                pl.BlockSpec((devices, 1, tokens, lanes), lambda j, places: (0, j, 0, 0)),
                whole((2,) + piece),
                whole((2,) + piece),
                whole((12,) + piece),
            ],
            scratch_shapes=[
                pltpu.VMEM((columns, rows // 2, lanes), jnp.float32),
                pltpu.VMEM((columns, 1, keys), jnp.float32),
                pltpu.VMEM((rows, keys), jnp.float32),
                pltpu.VMEM((rows, keys), jnp.float32),
                pltpu.VMEM((rows, keys), jnp.float32),
                pltpu.VMEM((rows, keys), jnp.float32),
                pltpu.VMEM((2 * rows, keys), jnp.bfloat16),
                pltpu.VMEM((rows, 128), jnp.float32),
                pltpu.VMEM((16,) + piece, jnp.bfloat16),
            ],
        ),
        out_shape=[
            jax.ShapeDtypeStruct(mine.shape, jnp.bfloat16),
            jax.ShapeDtypeStruct(mine.shape, jnp.bfloat16),
            jax.ShapeDtypeStruct((devices,) + mine.shape, jnp.bfloat16),
            jax.ShapeDtypeStruct((2,) + piece, jnp.bfloat16),
            jax.ShapeDtypeStruct((2,) + piece, jnp.bfloat16),
            jax.ShapeDtypeStruct((12,) + piece, jnp.bfloat16),
        ],
        compiler_params=pltpu.CompilerParams(vmem_limit_bytes=48 * 1024 * 1024),
        cost_estimate=pl.CostEstimate(flops=12 * 128 * work, bytes_accessed=16 * 2**20, transcendentals=work),
        name="attention_both",
    )(places, mine, other, received, received, received, weight, bias)


def local(
    query_vectors,
    key_vectors,
    value_vectors,
    gate_logits,
    pair_bias,
    pair_mask,
    output_weight,
    output_cotangent,
):
    columns, tokens, channels = query_vectors.shape
    half = channels // 2
    devices = lax.axis_size("col")
    row_count = lax.axis_size("row")
    core = lax.axis_index("col") % 2
    scaling = 1.0 / math.sqrt(channels // HEADS)
    swap = [(index, index ^ 1) for index in range(devices)]
    keys = pair_bias.shape[2]

    def mine_other(array, axis):
        size = array.shape[axis] // 2
        low = lax.slice_in_dim(array, 0, size, axis=axis)
        high = lax.slice_in_dim(array, size, 2 * size, axis=axis)
        return jnp.where(core == 0, low, high), jnp.where(core == 0, high, low)

    def in_order(mine, other, axis):
        return jnp.where(
            core == 0,
            jnp.concatenate([mine, other], axis=axis),
            jnp.concatenate([other, mine], axis=axis),
        )

    def swapped(array):
        return lax.ppermute(array, "col", swap)

    bias_mine, bias_other = mine_other(pair_bias, 0)
    bias_pair = in_order(bias_mine, swapped(bias_other), 1).reshape(-1, keys)

    packed = prepare(key_vectors, value_vectors, pair_mask, output_cotangent, devices)
    received = lax.all_to_all(packed, "col", 0, 0, tiled=True)
    place = lax.axis_index("row")
    row_ring = row_count // 2
    places = [
        2 * ((index % row_ring - place) % row_ring) + (index // row_ring - place // row_ring) % 2
        for index in range(row_count)
    ]
    places.append(core)
    places = jnp.stack(places).astype(jnp.int32)

    query_mine, query_other = mine_other(query_vectors, 2)
    gate_mine, gate_other = mine_other(gate_logits, 2)
    qg_mine = jnp.concatenate([query_mine, gate_mine], axis=2)
    qg_other = swapped(jnp.concatenate([query_other, gate_other], axis=2))
    weight_mine, _ = mine_other(output_weight, 0)
    weight_mine = jnp.pad(weight_mine, ((half, 0), (0, 0)))

    qa_own, qa_away, kv_grads, bias_right, bias_left, bias_rest = attend(
        places, qg_mine, qg_other, received, weight_mine, bias_pair, row_count
    )

    qa_back = swapped(qa_away)
    query_gradient = in_order(qa_own[..., :half], qa_back[..., :half], 2)
    gate_gradient = in_order(qa_own[..., half:], qa_back[..., half:], 2)

    def along_row(array, turn, side):
        pairs = []
        for index in range(row_count):
            high, low = index // row_ring, index % row_ring
            pairs.append((index, ((high + side) % 2) * row_ring + (low + turn) % row_ring))
        return lax.ppermute(array, "row", pairs)

    def added(*parts):
        return sum(part.astype(jnp.float32) for part in parts)

    from_left = along_row(bias_right, 1, 0)
    from_right = along_row(bias_left, -1, 0)
    from_left, from_right, kv_grads = lax.optimization_barrier((from_left, from_right, kv_grads))
    kv_parts = lax.all_to_all(kv_grads, "col", 0, 0, tiled=True)
    kv_parts = kv_parts.reshape((devices // 2, 2) + kv_parts.shape[1:])
    kv_sum = jnp.sum(kv_parts.astype(jnp.float32), axis=0)
    key_gradient = jnp.concatenate([kv_sum[0, ..., :half], kv_sum[1, ..., :half]], axis=2) * scaling
    key_gradient = key_gradient.astype(jnp.bfloat16)
    value_gradient = jnp.concatenate([kv_sum[0, ..., half:], kv_sum[1, ..., half:]], axis=2)
    value_gradient = value_gradient.astype(jnp.bfloat16)
    onward = jnp.concatenate([added(bias_rest[4:6], from_left).astype(jnp.bfloat16), bias_rest[6:8]])
    backward = jnp.concatenate([bias_rest[8:10], added(bias_rest[10:], from_right).astype(jnp.bfloat16)])
    sums = added(bias_rest[:4], along_row(onward, 1, 0), along_row(backward, -1, 0))
    low_sums = sums.astype(jnp.bfloat16)
    diagonal = []
    for index in range(row_count * devices):
        up = (index // devices + row_ring) % row_count
        diagonal.append((index, up * devices + (index % devices ^ 1)))
    from_high, from_core, from_diagonal, key_gradient, value_gradient = lax.optimization_barrier((
        along_row(low_sums[2], 0, 1),
        swapped(low_sums[1]),
        lax.ppermute(low_sums[3], ("row", "col"), diagonal),
        key_gradient,
        value_gradient,
    ))
    bias_own = added(sums[0], from_high)
    bias_away = added(from_core, from_diagonal)
    bias_gradient = in_order(bias_own, bias_away, 0)
    return (query_gradient, key_gradient, value_gradient, gate_gradient, bias_gradient)


def solution(mesh):
    placed = (
        P("row", "col", None),
        P("row", "col", None),
        P("row", "col", None),
        P("row", "col", None),
        P(None, "col", None),
        P("row", "col"),
        P(),
        P("row", "col", None),
    )
    return jax.shard_map(
        local,
        mesh=mesh,
        in_specs=placed,
        out_specs=(
            P("row", "col", None),
            P("row", "col", None),
            P("row", "col", None),
            P("row", "col", None),
            P(None, "col", "row"),
        ),
        check_vma=False,
    )
```

```python
import functools
import math

import jax
import jax.numpy as jnp
from jax import lax
from jax.experimental import pallas as pl
from jax.experimental.pallas import tpu as pltpu
from jax.sharding import PartitionSpec as P

HEADS = 4
NEG_FILL = -1000000000.0
LOG2E = math.log2(math.e)
CHUNK = 16
UNROLL = 12
MASK_ROWS = 16
PIECES = 8
VMEM_WIDE = 60 * 1024 * 1024


def attention_kernel(head, *refs):
    place_ref, qg_mine_ref, qg_other_ref, kv_ref, mask_ref, cotangent_ref, weight_ref, bias_ref = refs[:8]
    earlier = refs[8 : 8 + 3 * head]
    qa_own_ref, qa_away_ref, dkv_ref, right_out_ref, left_out_ref, rest_out_ref = refs[8 + 3 * head :][:6]
    gated_ref, cap_ref, s_ref, b2_ref, acc_ref, dp_ref, de_ref, row_ref, dbias_ref = refs[14 + 3 * head :]
    step = pl.program_id(0)
    last = pl.num_programs(0) - 1
    queries, keys = bias_ref.shape
    half = queries // 2
    head_width = qg_mine_ref.shape[2] // 4
    core = place_ref[PIECES]
    scaling = 1.0 / math.sqrt(head_width)

    @pl.when(step == 0)
    def _():
        def fill(index, carry):
            part = pl.ds(index * CHUNK, CHUNK)
            b2_ref[part, :] = bias_ref[part, :].astype(jnp.float32) * LOG2E
            acc_ref[part, :] = jnp.zeros((CHUNK, keys), jnp.float32)
            return carry

        lax.fori_loop(0, queries // CHUNK, fill, 0)
        sources, _, lanes = cotangent_ref.shape
        cotangent = cotangent_ref[...].astype(jnp.float32)
        cotangent = cotangent.reshape(sources, 2, cap_ref.shape[0], lanes // sources, lanes)
        for column in range(cotangent.shape[2]):
            for side in range(2):
                part = cotangent[:, side, column].reshape(lanes, lanes).astype(jnp.bfloat16)
                gated = jnp.dot(weight_ref[...], part, preferred_element_type=jnp.float32)
                gated_ref[column, side * half : (side + 1) * half] = gated.T[:half]
        masks = mask_ref[...].astype(jnp.float32)
        for column in range(cap_ref.shape[0]):
            pieces = [
                masks[source, column : column + 1, :half] for source in range(masks.shape[0])
            ]
            cap_ref[column] = jnp.where(
                jnp.concatenate(pieces, axis=1) > 0.5, 1e30, NEG_FILL * LOG2E
            )

    lane = lax.broadcasted_iota(jnp.int32, (queries, 4 * head_width), 1)
    transposed = (((1,), (1,)), ((), ()))
    is_query = (lane >= head * head_width) & (lane < (head + 1) * head_width)
    is_gate = (lane >= (head + 2) * head_width) & (lane < (head + 3) * head_width)
    kvs, query_rows, grad_rows, slopes = [], [], [], []
    for unit in range(2):
        kvs.append(kv_ref[:, unit * half : (unit + 1) * half, :].reshape(keys, 4 * head_width))
        mine = qg_mine_ref[unit]
        other = qg_other_ref[unit]
        query_gate = jnp.concatenate(
            [jnp.where(core == 0, mine, other), jnp.where(core == 0, other, mine)], axis=0
        )
        sigma = jax.nn.sigmoid(query_gate.astype(jnp.float32))
        gated_grad = gated_ref[2 * step + unit] * sigma
        slopes.append(gated_grad * (1.0 - sigma))
        zero = jnp.zeros_like(query_gate)
        query_rows.append(jnp.where(is_query, query_gate, zero))
        grad_rows.append(jnp.where(is_gate, gated_grad.astype(jnp.bfloat16), zero))

    def scores_of(unit):
        s_ref[unit * queries : (unit + 1) * queries, :] = lax.dot_general(
            query_rows[unit], kvs[unit], transposed, preferred_element_type=jnp.float32
        )

    def soften(unit):
        cap = cap_ref[2 * step + unit]

        def one(index, carry):
            inner = index * CHUNK
            part = pl.ds(unit * queries + inner, CHUNK)
            scores = s_ref[part, :] * (scaling * LOG2E) + b2_ref[pl.ds(inner, CHUNK), :]
            scores = jnp.minimum(scores, cap)
            weights = jnp.exp2(scores - jnp.max(scores, axis=1, keepdims=True))
            row_ref[part, :] = jnp.broadcast_to(jnp.sum(weights, axis=1, keepdims=True), (CHUNK, 128))
            de_ref[pl.ds((2 * unit + 1) * queries + inner, CHUNK), :] = weights.astype(jnp.bfloat16)
            return carry

        lax.fori_loop(0, queries // CHUNK, one, 0, unroll=UNROLL)

    def cotangents(unit):
        part = slice(unit * queries, (unit + 1) * queries)
        weights_low = de_ref[(2 * unit + 1) * queries : (2 * unit + 2) * queries, :]
        inverse = 1.0 / row_ref[part, :]
        attended = jnp.dot(weights_low, kvs[unit], preferred_element_type=jnp.float32) * inverse
        grad_wide = grad_rows[unit].astype(jnp.float32)
        delta = jnp.sum(grad_wide * attended, axis=1, keepdims=True)
        row_ref[part, :] = delta * inverse
        grad_scaled = (grad_wide * inverse).astype(jnp.bfloat16)
        dp_ref[part, :] = lax.dot_general(
            grad_scaled, kvs[unit], transposed, preferred_element_type=jnp.float32
        )
        return attended, grad_scaled

    def backward(unit):
        def one(index, carry):
            inner = index * CHUNK
            part = pl.ds(unit * queries + inner, CHUNK)
            weights = de_ref[pl.ds((2 * unit + 1) * queries + inner, CHUNK), :].astype(jnp.float32)
            score_grad = weights * (dp_ref[part, :] - row_ref[part, :1])
            acc_ref[pl.ds(inner, CHUNK), :] += score_grad
            de_ref[pl.ds(2 * unit * queries + inner, CHUNK), :] = score_grad.astype(jnp.bfloat16)
            return carry

        lax.fori_loop(0, queries // CHUNK, one, 0, unroll=UNROLL)

    def finish(unit, attended, grad_scaled):
        low = de_ref[2 * unit * queries : (2 * unit + 1) * queries, :]
        query = jnp.dot(low, kvs[unit], preferred_element_type=jnp.float32) * scaling
        merged = jnp.where(is_query, query, jnp.where(is_gate, attended * slopes[unit], 0.0))
        own = jnp.where(core == 0, merged[:half], merged[half:])
        away = jnp.where(core == 0, merged[half:], merged[:half])
        sides = jnp.concatenate([query_rows[unit], grad_scaled], axis=0)
        key_value = lax.dot_general(
            sides,
            de_ref[2 * unit * queries : (2 * unit + 2) * queries, :],
            (((0,), (0,)), ((), ())),
            preferred_element_type=jnp.float32,
        ).T.reshape(dkv_ref.shape[0], half, 4 * head_width)
        if earlier:
            own = own + earlier[0][unit].astype(jnp.float32)
            away = away + earlier[1][unit].astype(jnp.float32)
            key_value = key_value + earlier[2][:, unit].astype(jnp.float32)
        qa_own_ref[unit] = own.astype(jnp.bfloat16)
        qa_away_ref[unit] = away.astype(jnp.bfloat16)
        dkv_ref[:, unit] = key_value.astype(jnp.bfloat16)

    scores_of(0)
    scores_of(1)
    soften(0)
    first = cotangents(0)
    soften(1)
    second = cotangents(1)
    backward(0)
    finish(0, *first)
    backward(1)
    finish(1, *second)

    @pl.when(step == last)
    def _():
        width = dbias_ref.shape[2]
        for piece in range(PIECES):
            for side in range(2):
                part = acc_ref[side * half : (side + 1) * half, piece * width : (piece + 1) * width]
                target = 2 * place_ref[piece] + (side + core) % 2
                dbias_ref[target] = part.astype(jnp.bfloat16)
        right_out_ref[...] = dbias_ref[8:10]
        left_out_ref[...] = dbias_ref[10:12]
        rest_out_ref[:8] = dbias_ref[:8]
        rest_out_ref[8:] = dbias_ref[12:]


def prepare_kernel(key_ref, value_ref, mask_ref, cotangent_ref, packed_ref):
    columns, tokens, channels = key_ref.shape
    half = channels // 2
    devices = packed_ref.shape[0]
    pairs = columns * tokens
    rows = cotangent_ref.shape[0] * cotangent_ref.shape[1]
    mask = mask_ref[...].astype(jnp.float32)
    mask = jnp.concatenate([mask, jnp.zeros((columns, channels - tokens), jnp.float32)], axis=1)
    filler = jnp.zeros((MASK_ROWS - columns, channels), jnp.float32)
    mask = jnp.concatenate([mask, filler], axis=0).astype(jnp.bfloat16)
    for column in range(columns):
        key = key_ref[column]
        value = value_ref[column]
        sides = [
            jnp.concatenate([key[:, :half], value[:, :half]], axis=1),
            jnp.concatenate([key[:, half:], value[:, half:]], axis=1),
        ]
        for device in range(devices):
            packed_ref[device, column * tokens : (column + 1) * tokens, :] = sides[device % 2]
    cotangent = cotangent_ref[...].astype(jnp.float32).reshape(rows, cotangent_ref.shape[2])
    filler = jnp.zeros((rows, channels - tokens), jnp.float32)
    for device in range(devices):
        packed_ref[device, pairs + 2 * rows :, :] = mask
        part = cotangent[:, device * tokens : (device + 1) * tokens]
        part = jnp.concatenate([part, filler], axis=1).astype(jnp.bfloat16)
        start = pairs + device % 2 * rows
        packed_ref[device, start : start + rows, :] = part
        packed_ref[device ^ 1, start : start + rows, :] = part


def prepare(key, value, mask, cotangent, devices):
    columns, tokens, channels = key.shape
    rows = columns * tokens + 2 * cotangent.shape[0] * cotangent.shape[1] + MASK_ROWS

    def whole(shape):
        return pl.BlockSpec(shape, lambda i: (0,) * len(shape))

    out = (devices, rows, channels)
    return pl.pallas_call(
        prepare_kernel,
        grid=(1,),
        in_specs=[whole(key.shape), whole(value.shape), whole(mask.shape), whole(cotangent.shape)],
        out_specs=whole(out),
        out_shape=jax.ShapeDtypeStruct(out, jnp.bfloat16),
        compiler_params=pltpu.CompilerParams(vmem_limit_bytes=VMEM_WIDE),
        name="prepare_exchange",
    )(key, value, mask, cotangent)


def attend(head, places, mine, other, received, weight, bias, row_count, earlier):
    columns, tokens, lanes = mine.shape
    queries, keys = bias.shape[0] // 2, bias.shape[1]
    width = keys // row_count
    devices = received.shape[0]
    mask_place = received.shape[1] // MASK_ROWS - 1
    cotangent_rows = 2 * columns * lanes // devices
    cotangent_place = columns * tokens // cotangent_rows
    work = columns * queries * keys

    def whole(shape):
        return pl.BlockSpec(shape, lambda j, places: (0,) * len(shape))

    column_spec = pl.BlockSpec((2, tokens, lanes), lambda j, places: (j, 0, 0))
    grad_spec = pl.BlockSpec((devices, 2, tokens, lanes), lambda j, places: (0, j, 0, 0))
    piece = (tokens, width)
    return pl.pallas_call(
        functools.partial(attention_kernel, head),
        grid_spec=pltpu.PrefetchScalarGridSpec(
            num_scalar_prefetch=1,
            grid=(columns // 2,),
            in_specs=[
                column_spec,
                column_spec,
                pl.BlockSpec((devices, 2 * tokens, lanes), lambda j, places: (0, j, 0)),
                pl.BlockSpec((devices, MASK_ROWS, lanes), lambda j, places: (0, mask_place, 0)),
                pl.BlockSpec(
                    (devices, cotangent_rows, lanes), lambda j, places: (0, cotangent_place, 0)
                ),
                whole(weight.shape),
                pl.BlockSpec((queries, keys), lambda j, places: (head, 0)),
            ]
            + [column_spec, column_spec, grad_spec][: len(earlier)],
            out_specs=[
                column_spec,
                column_spec,
                grad_spec,
                whole((2,) + piece),
                whole((2,) + piece),
                whole((12,) + piece),
            ],
            scratch_shapes=[
                pltpu.VMEM((columns, queries, lanes), jnp.float32),
                pltpu.VMEM((columns, 1, keys), jnp.float32),
                pltpu.VMEM((2 * queries, keys), jnp.float32),
                pltpu.VMEM((queries, keys), jnp.float32),
                pltpu.VMEM((queries, keys), jnp.float32),
                pltpu.VMEM((2 * queries, keys), jnp.float32),
                pltpu.VMEM((4 * queries, keys), jnp.bfloat16),
                pltpu.VMEM((2 * queries, 128), jnp.float32),
                pltpu.VMEM((16,) + piece, jnp.bfloat16),
            ],
        ),
        out_shape=[
            jax.ShapeDtypeStruct(mine.shape, jnp.bfloat16),
            jax.ShapeDtypeStruct(mine.shape, jnp.bfloat16),
            jax.ShapeDtypeStruct((devices,) + mine.shape, jnp.bfloat16),
            jax.ShapeDtypeStruct((2,) + piece, jnp.bfloat16),
            jax.ShapeDtypeStruct((2,) + piece, jnp.bfloat16),
            jax.ShapeDtypeStruct((12,) + piece, jnp.bfloat16),
        ],
        compiler_params=pltpu.CompilerParams(vmem_limit_bytes=48 * 1024 * 1024),
        cost_estimate=pl.CostEstimate(flops=12 * 128 * work, bytes_accessed=16 * 2**20, transcendentals=work),
        name="attention_head",
    )(places, mine, other, received, received, received, weight, bias, *earlier)


def local(
    query_vectors,
    key_vectors,
    value_vectors,
    gate_logits,
    pair_bias,
    pair_mask,
    output_weight,
    output_cotangent,
):
    columns, tokens, channels = query_vectors.shape
    half = channels // 2
    devices = lax.axis_size("col")
    row_count = lax.axis_size("row")
    core = lax.axis_index("col") % 2
    scaling = 1.0 / math.sqrt(channels // HEADS)
    swap = [(index, index ^ 1) for index in range(devices)]
    keys = pair_bias.shape[2]

    def mine_other(array, axis):
        size = array.shape[axis] // 2
        low = lax.slice_in_dim(array, 0, size, axis=axis)
        high = lax.slice_in_dim(array, size, 2 * size, axis=axis)
        return jnp.where(core == 0, low, high), jnp.where(core == 0, high, low)

    def in_order(mine, other, axis):
        return jnp.where(
            core == 0,
            jnp.concatenate([mine, other], axis=axis),
            jnp.concatenate([other, mine], axis=axis),
        )

    def swapped(array):
        return lax.ppermute(array, "col", swap)

    bias_mine, bias_other = mine_other(pair_bias, 0)
    bias_pair = in_order(bias_mine, swapped(bias_other), 1).reshape(-1, keys)

    packed = prepare(key_vectors, value_vectors, pair_mask, output_cotangent, devices)
    received = lax.all_to_all(packed, "col", 0, 0, tiled=True)
    place = lax.axis_index("row")
    row_ring = row_count // 2
    places = [
        2 * ((index % row_ring - place) % row_ring) + (index // row_ring - place // row_ring) % 2
        for index in range(row_count)
    ]
    places.append(core)
    places = jnp.stack(places).astype(jnp.int32)

    query_mine, query_other = mine_other(query_vectors, 2)
    gate_mine, gate_other = mine_other(gate_logits, 2)
    qg_mine = jnp.concatenate([query_mine, gate_mine], axis=2)
    qg_other = swapped(jnp.concatenate([query_other, gate_other], axis=2))
    weight_mine, _ = mine_other(output_weight, 0)
    weight_mine = jnp.pad(weight_mine, ((half, 0), (0, 0)))

    shared = (places, qg_mine, qg_other, received, weight_mine, bias_pair, row_count)
    *earlier, bias_right, bias_left, bias_rest = attend(0, *shared, ())
    (qa_own, qa_away, kv_grads, bias_right_2, bias_left_2, bias_rest_2) = attend(1, *shared, tuple(earlier))

    def along_row(array, turn, side):
        pairs = []
        for index in range(row_count):
            high, low = index // row_ring, index % row_ring
            pairs.append((index, ((high + side) % 2) * row_ring + (low + turn) % row_ring))
        return lax.ppermute(array, "row", pairs)

    def added(*parts):
        return sum(part.astype(jnp.float32) for part in parts)

    def ring_onward(rest, from_left, from_right):
        onward = jnp.concatenate([added(rest[4:6], from_left).astype(jnp.bfloat16), rest[6:8]])
        backward = jnp.concatenate([rest[8:10], added(rest[10:], from_right).astype(jnp.bfloat16)])
        return along_row(onward, 1, 0), along_row(backward, -1, 0)

    from_left, from_right = along_row(bias_right, 1, 0), along_row(bias_left, -1, 0)
    second = (bias_right_2, bias_left_2, bias_rest_2, kv_grads, qa_own, qa_away)
    from_left, from_right, bias_rest, second = lax.optimization_barrier(
        (from_left, from_right, bias_rest, second)
    )
    bias_right_2, bias_left_2, bias_rest_2, kv_grads, qa_own, qa_away = second
    from_left, from_right = ring_onward(bias_rest, from_left, from_right)
    sums = added(bias_rest[:4], from_left, from_right)
    from_left, from_right = along_row(bias_right_2, 1, 0), along_row(bias_left_2, -1, 0)
    from_left, from_right, kv_grads = lax.optimization_barrier((from_left, from_right, kv_grads))
    kv_parts = lax.all_to_all(kv_grads, "col", 0, 0, tiled=True)
    kv_parts = kv_parts.reshape((devices // 2, 2) + kv_parts.shape[1:])
    kv_sum = jnp.sum(kv_parts.astype(jnp.float32), axis=0)
    key_gradient = jnp.concatenate([kv_sum[0, ..., :half], kv_sum[1, ..., :half]], axis=2) * scaling
    key_gradient = key_gradient.astype(jnp.bfloat16)
    value_gradient = jnp.concatenate([kv_sum[0, ..., half:], kv_sum[1, ..., half:]], axis=2)
    value_gradient = value_gradient.astype(jnp.bfloat16)
    from_left, from_right = ring_onward(bias_rest_2, from_left, from_right)
    sums = jnp.stack([sums, added(bias_rest_2[:4], from_left, from_right)], axis=1)
    qa_back = swapped(qa_away)
    query_gradient = in_order(qa_own[..., :half], qa_back[..., :half], 2)
    gate_gradient = in_order(qa_own[..., half:], qa_back[..., half:], 2)
    low_sums = sums.astype(jnp.bfloat16)
    diagonal = []
    for index in range(row_count * devices):
        up = (index // devices + row_ring) % row_count
        diagonal.append((index, up * devices + (index % devices ^ 1)))
    from_high, from_core, from_diagonal, key_gradient, value_gradient = lax.optimization_barrier((
        along_row(low_sums[2], 0, 1),
        swapped(low_sums[1]),
        lax.ppermute(low_sums[3], ("row", "col"), diagonal),
        key_gradient,
        value_gradient,
    ))
    bias_own = added(sums[0], from_high)
    bias_away = added(from_core, from_diagonal)
    bias_gradient = in_order(bias_own, bias_away, 0)
    return (query_gradient, key_gradient, value_gradient, gate_gradient, bias_gradient)


def solution(mesh):
    placed = (
        P("row", "col", None),
        P("row", "col", None),
        P("row", "col", None),
        P("row", "col", None),
        P(None, "col", None),
        P("row", "col"),
        P(),
        P("row", "col", None),
    )
    return jax.shard_map(
        local,
        mesh=mesh,
        in_specs=placed,
        out_specs=(
            P("row", "col", None),
            P("row", "col", None),
            P("row", "col", None),
            P("row", "col", None),
            P(None, "col", "row"),
        ),
        check_vma=False,
    )
```

```python
import functools
import math

import jax
import jax.numpy as jnp
from jax import lax
from jax.experimental import pallas as pl
from jax.experimental.pallas import tpu as pltpu
from jax.sharding import PartitionSpec as P

HEADS = 4
NEG_FILL = -1000000000.0
LOG2E = math.log2(math.e)
CHUNK = 16
UNROLL = 12
MASK_ROWS = 16
PIECES = 8
VMEM_WIDE = 60 * 1024 * 1024


def attention_kernel(head, *refs):
    place_ref, qg_mine_ref, qg_other_ref, kv_ref, mask_ref, cotangent_ref, weight_ref, bias_ref = refs[:8]
    earlier = refs[8 : 8 + 3 * head]
    qa_own_ref, qa_away_ref, dkv_ref, right_out_ref, left_out_ref, rest_out_ref = refs[8 + 3 * head :][:6]
    gated_ref, cap_ref, s_ref, b2_ref, acc_ref, dp_ref, de_ref, row_ref, dbias_ref = refs[14 + 3 * head :]
    step = pl.program_id(0)
    last = pl.num_programs(0) - 1
    queries, keys = bias_ref.shape
    half = queries // 2
    head_width = qg_mine_ref.shape[2] // 4
    core = place_ref[PIECES]
    scaling = 1.0 / math.sqrt(head_width)

    @pl.when(step == 0)
    def _():
        def fill(index, carry):
            part = pl.ds(index * CHUNK, CHUNK)
            b2_ref[part, :] = bias_ref[part, :].astype(jnp.float32) * LOG2E
            acc_ref[part, :] = jnp.zeros((CHUNK, keys), jnp.float32)
            return carry

        lax.fori_loop(0, queries // CHUNK, fill, 0)
        sources, _, lanes = cotangent_ref.shape
        cotangent = cotangent_ref[...].astype(jnp.float32)
        cotangent = cotangent.reshape(sources, 2, cap_ref.shape[0], lanes // sources, lanes)
        for column in range(cotangent.shape[2]):
            for side in range(2):
                part = cotangent[:, side, column].reshape(lanes, lanes).astype(jnp.bfloat16)
                gated = jnp.dot(weight_ref[...], part, preferred_element_type=jnp.float32)
                gated_ref[column, side * half : (side + 1) * half] = gated.T[:half]
        masks = mask_ref[...].astype(jnp.float32)
        for column in range(cap_ref.shape[0]):
            pieces = [
                masks[source, column : column + 1, :half] for source in range(masks.shape[0])
            ]
            cap_ref[column] = jnp.where(
                jnp.concatenate(pieces, axis=1) > 0.5, 1e30, NEG_FILL * LOG2E
            )

    lane = lax.broadcasted_iota(jnp.int32, (queries, 4 * head_width), 1)
    transposed = (((1,), (1,)), ((), ()))
    is_query = (lane >= head * head_width) & (lane < (head + 1) * head_width)
    is_gate = (lane >= (head + 2) * head_width) & (lane < (head + 3) * head_width)
    kvs, query_rows, grad_rows, slopes = [], [], [], []
    for unit in range(2):
        kvs.append(kv_ref[:, unit * half : (unit + 1) * half, :].reshape(keys, 4 * head_width))
        mine = qg_mine_ref[unit]
        other = qg_other_ref[unit]
        query_gate = jnp.concatenate(
            [jnp.where(core == 0, mine, other), jnp.where(core == 0, other, mine)], axis=0
        )
        sigma = jax.nn.sigmoid(query_gate.astype(jnp.float32))
        gated_grad = gated_ref[2 * step + unit] * sigma
        slopes.append(gated_grad * (1.0 - sigma))
        zero = jnp.zeros_like(query_gate)
        query_rows.append(jnp.where(is_query, query_gate, zero))
        grad_rows.append(jnp.where(is_gate, gated_grad.astype(jnp.bfloat16), zero))

    def scores_of(unit):
        s_ref[unit * queries : (unit + 1) * queries, :] = lax.dot_general(
            query_rows[unit], kvs[unit], transposed, preferred_element_type=jnp.float32
        )

    def soften(unit):
        cap = cap_ref[2 * step + unit]

        def one(index, carry):
            inner = index * CHUNK
            part = pl.ds(unit * queries + inner, CHUNK)
            scores = s_ref[part, :] * (scaling * LOG2E) + b2_ref[pl.ds(inner, CHUNK), :]
            scores = jnp.minimum(scores, cap)
            weights = jnp.exp2(scores - jnp.max(scores, axis=1, keepdims=True))
            row_ref[part, :] = jnp.broadcast_to(jnp.sum(weights, axis=1, keepdims=True), (CHUNK, 128))
            de_ref[pl.ds((2 * unit + 1) * queries + inner, CHUNK), :] = weights.astype(jnp.bfloat16)
            return carry

        lax.fori_loop(0, queries // CHUNK, one, 0, unroll=UNROLL)

    def cotangents(unit):
        part = slice(unit * queries, (unit + 1) * queries)
        weights_low = de_ref[(2 * unit + 1) * queries : (2 * unit + 2) * queries, :]
        inverse = 1.0 / row_ref[part, :]
        attended = jnp.dot(weights_low, kvs[unit], preferred_element_type=jnp.float32) * inverse
        grad_wide = grad_rows[unit].astype(jnp.float32)
        delta = jnp.sum(grad_wide * attended, axis=1, keepdims=True)
        row_ref[part, :] = delta * inverse
        grad_scaled = (grad_wide * inverse).astype(jnp.bfloat16)
        dp_ref[part, :] = lax.dot_general(
            grad_scaled, kvs[unit], transposed, preferred_element_type=jnp.float32
        )
        return attended, grad_scaled

    def backward(unit):
        def one(index, carry):
            inner = index * CHUNK
            part = pl.ds(unit * queries + inner, CHUNK)
            weights = de_ref[pl.ds((2 * unit + 1) * queries + inner, CHUNK), :].astype(jnp.float32)
            score_grad = weights * (dp_ref[part, :] - row_ref[part, :1])
            acc_ref[pl.ds(inner, CHUNK), :] += score_grad
            de_ref[pl.ds(2 * unit * queries + inner, CHUNK), :] = score_grad.astype(jnp.bfloat16)
            return carry

        lax.fori_loop(0, queries // CHUNK, one, 0, unroll=UNROLL)

    def finish(unit, attended, grad_scaled):
        low = de_ref[2 * unit * queries : (2 * unit + 1) * queries, :]
        query = jnp.dot(low, kvs[unit], preferred_element_type=jnp.float32) * scaling
        merged = jnp.where(is_query, query, jnp.where(is_gate, attended * slopes[unit], 0.0))
        own = jnp.where(core == 0, merged[:half], merged[half:])
        away = jnp.where(core == 0, merged[half:], merged[:half])
        sides = jnp.concatenate([query_rows[unit], grad_scaled], axis=0)
        key_value = lax.dot_general(
            sides,
            de_ref[2 * unit * queries : (2 * unit + 2) * queries, :],
            (((0,), (0,)), ((), ())),
            preferred_element_type=jnp.float32,
        ).T.reshape(dkv_ref.shape[0], half, 4 * head_width)
        if earlier:
            own = own + earlier[0][unit].astype(jnp.float32)
            away = away + earlier[1][unit].astype(jnp.float32)
            key_value = key_value + earlier[2][:, unit].astype(jnp.float32)
        qa_own_ref[unit] = own.astype(jnp.bfloat16)
        qa_away_ref[unit] = away.astype(jnp.bfloat16)
        dkv_ref[:, unit] = key_value.astype(jnp.bfloat16)

    scores_of(0)
    scores_of(1)
    soften(0)
    first = cotangents(0)
    soften(1)
    second = cotangents(1)
    backward(0)
    finish(0, *first)
    backward(1)
    finish(1, *second)

    @pl.when(step == last)
    def _():
        width = dbias_ref.shape[2]
        for piece in range(PIECES):
            for side in range(2):
                part = acc_ref[side * half : (side + 1) * half, piece * width : (piece + 1) * width]
                target = 2 * place_ref[piece] + (side + core) % 2
                dbias_ref[target] = part.astype(jnp.bfloat16)
        right_out_ref[...] = dbias_ref[8:10]
        left_out_ref[...] = dbias_ref[10:12]
        rest_out_ref[:8] = dbias_ref[:8]
        rest_out_ref[8:] = dbias_ref[12:]


def prepare_kernel(key_ref, value_ref, mask_ref, cotangent_ref, packed_ref):
    columns, tokens, channels = key_ref.shape
    half = channels // 2
    devices = packed_ref.shape[0]
    pairs = columns * tokens
    rows = cotangent_ref.shape[0] * cotangent_ref.shape[1]
    mask = mask_ref[...].astype(jnp.float32)
    mask = jnp.concatenate([mask, jnp.zeros((columns, channels - tokens), jnp.float32)], axis=1)
    filler = jnp.zeros((MASK_ROWS - columns, channels), jnp.float32)
    mask = jnp.concatenate([mask, filler], axis=0).astype(jnp.bfloat16)
    for column in range(columns):
        key = key_ref[column]
        value = value_ref[column]
        sides = [
            jnp.concatenate([key[:, :half], value[:, :half]], axis=1),
            jnp.concatenate([key[:, half:], value[:, half:]], axis=1),
        ]
        for device in range(devices):
            packed_ref[device, column * tokens : (column + 1) * tokens, :] = sides[device % 2]
    cotangent = cotangent_ref[...].astype(jnp.float32).reshape(rows, cotangent_ref.shape[2])
    filler = jnp.zeros((rows, channels - tokens), jnp.float32)
    for device in range(devices):
        packed_ref[device, pairs + 2 * rows :, :] = mask
        part = cotangent[:, device * tokens : (device + 1) * tokens]
        part = jnp.concatenate([part, filler], axis=1).astype(jnp.bfloat16)
        start = pairs + device % 2 * rows
        packed_ref[device, start : start + rows, :] = part
        packed_ref[device ^ 1, start : start + rows, :] = part


def prepare(key, value, mask, cotangent, devices):
    columns, tokens, channels = key.shape
    rows = columns * tokens + 2 * cotangent.shape[0] * cotangent.shape[1] + MASK_ROWS

    def whole(shape):
        return pl.BlockSpec(shape, lambda i: (0,) * len(shape))

    out = (devices, rows, channels)
    return pl.pallas_call(
        prepare_kernel,
        grid=(1,),
        in_specs=[whole(key.shape), whole(value.shape), whole(mask.shape), whole(cotangent.shape)],
        out_specs=whole(out),
        out_shape=jax.ShapeDtypeStruct(out, jnp.bfloat16),
        compiler_params=pltpu.CompilerParams(vmem_limit_bytes=VMEM_WIDE),
        name="prepare_exchange",
    )(key, value, mask, cotangent)


def attend(head, places, mine, other, received, weight, bias, row_count, earlier):
    columns, tokens, lanes = mine.shape
    queries, keys = bias.shape[0] // 2, bias.shape[1]
    width = keys // row_count
    devices = received.shape[0]
    mask_place = received.shape[1] // MASK_ROWS - 1
    cotangent_rows = 2 * columns * lanes // devices
    cotangent_place = columns * tokens // cotangent_rows
    work = columns * queries * keys

    def whole(shape):
        return pl.BlockSpec(shape, lambda j, places: (0,) * len(shape))

    column_spec = pl.BlockSpec((2, tokens, lanes), lambda j, places: (j, 0, 0))
    grad_spec = pl.BlockSpec((devices, 2, tokens, lanes), lambda j, places: (0, j, 0, 0))
    piece = (tokens, width)
    return pl.pallas_call(
        functools.partial(attention_kernel, head),
        grid_spec=pltpu.PrefetchScalarGridSpec(
            num_scalar_prefetch=1,
            grid=(columns // 2,),
            in_specs=[
                column_spec,
                column_spec,
                pl.BlockSpec((devices, 2 * tokens, lanes), lambda j, places: (0, j, 0)),
                pl.BlockSpec((devices, MASK_ROWS, lanes), lambda j, places: (0, mask_place, 0)),
                pl.BlockSpec(
                    (devices, cotangent_rows, lanes), lambda j, places: (0, cotangent_place, 0)
                ),
                whole(weight.shape),
                pl.BlockSpec((queries, keys), lambda j, places: (head, 0)),
            ]
            + [column_spec, column_spec, grad_spec][: len(earlier)],
            out_specs=[
                column_spec,
                column_spec,
                grad_spec,
                whole((2,) + piece),
                whole((2,) + piece),
                whole((12,) + piece),
            ],
            scratch_shapes=[
                pltpu.VMEM((columns, queries, lanes), jnp.float32),
                pltpu.VMEM((columns, 1, keys), jnp.float32),
                pltpu.VMEM((2 * queries, keys), jnp.float32),
                pltpu.VMEM((queries, keys), jnp.float32),
                pltpu.VMEM((queries, keys), jnp.float32),
                pltpu.VMEM((2 * queries, keys), jnp.float32),
                pltpu.VMEM((4 * queries, keys), jnp.bfloat16),
                pltpu.VMEM((2 * queries, 128), jnp.float32),
                pltpu.VMEM((16,) + piece, jnp.bfloat16),
            ],
        ),
        out_shape=[
            jax.ShapeDtypeStruct(mine.shape, jnp.bfloat16),
            jax.ShapeDtypeStruct(mine.shape, jnp.bfloat16),
            jax.ShapeDtypeStruct((devices,) + mine.shape, jnp.bfloat16),
            jax.ShapeDtypeStruct((2,) + piece, jnp.bfloat16),
            jax.ShapeDtypeStruct((2,) + piece, jnp.bfloat16),
            jax.ShapeDtypeStruct((12,) + piece, jnp.bfloat16),
        ],
        compiler_params=pltpu.CompilerParams(vmem_limit_bytes=48 * 1024 * 1024),
        cost_estimate=pl.CostEstimate(flops=12 * 128 * work, bytes_accessed=16 * 2**20, transcendentals=work),
        name="attention_head",
    )(places, mine, other, received, received, received, weight, bias, *earlier)


def local(
    query_vectors,
    key_vectors,
    value_vectors,
    gate_logits,
    pair_bias,
    pair_mask,
    output_weight,
    output_cotangent,
):
    columns, tokens, channels = query_vectors.shape
    half = channels // 2
    devices = lax.axis_size("col")
    row_count = lax.axis_size("row")
    core = lax.axis_index("col") % 2
    scaling = 1.0 / math.sqrt(channels // HEADS)
    swap = [(index, index ^ 1) for index in range(devices)]
    keys = pair_bias.shape[2]

    def mine_other(array, axis):
        size = array.shape[axis] // 2
        low = lax.slice_in_dim(array, 0, size, axis=axis)
        high = lax.slice_in_dim(array, size, 2 * size, axis=axis)
        return jnp.where(core == 0, low, high), jnp.where(core == 0, high, low)

    def in_order(mine, other, axis):
        return jnp.where(
            core == 0,
            jnp.concatenate([mine, other], axis=axis),
            jnp.concatenate([other, mine], axis=axis),
        )

    def swapped(array):
        return lax.ppermute(array, "col", swap)

    bias_mine, bias_other = mine_other(pair_bias, 0)
    bias_pair = in_order(bias_mine, swapped(bias_other), 1).reshape(-1, keys)

    packed = prepare(key_vectors, value_vectors, pair_mask, output_cotangent, devices)
    received = lax.all_to_all(packed, "col", 0, 0, tiled=True)
    place = lax.axis_index("row")
    row_ring = row_count // 2
    places = [
        2 * ((index % row_ring - place) % row_ring) + (index // row_ring - place // row_ring) % 2
        for index in range(row_count)
    ]
    places.append(core)
    places = jnp.stack(places).astype(jnp.int32)

    query_mine, query_other = mine_other(query_vectors, 2)
    gate_mine, gate_other = mine_other(gate_logits, 2)
    qg_mine = jnp.concatenate([query_mine, gate_mine], axis=2)
    qg_other = swapped(jnp.concatenate([query_other, gate_other], axis=2))
    weight_mine, _ = mine_other(output_weight, 0)
    weight_mine = jnp.pad(weight_mine, ((half, 0), (0, 0)))

    shared = (places, qg_mine, qg_other, received, weight_mine, bias_pair, row_count)
    *earlier, bias_right, bias_left, bias_rest = attend(0, *shared, ())
    (qa_own, qa_away, kv_grads, bias_right_2, bias_left_2, bias_rest_2) = attend(1, *shared, tuple(earlier))

    def along_row(array, turn, side):
        pairs = []
        for index in range(row_count):
            high, low = index // row_ring, index % row_ring
            pairs.append((index, ((high + side) % 2) * row_ring + (low + turn) % row_ring))
        return lax.ppermute(array, "row", pairs)

    def added(*parts):
        return sum(part.astype(jnp.float32) for part in parts)

    def ring_onward(rest, from_left, from_right):
        onward = jnp.concatenate([added(rest[4:6], from_left).astype(jnp.bfloat16), rest[6:8]])
        backward = jnp.concatenate([rest[8:10], added(rest[10:], from_right).astype(jnp.bfloat16)])
        return along_row(onward, 1, 0), along_row(backward, -1, 0)

    from_left, from_right = along_row(bias_right, 1, 0), along_row(bias_left, -1, 0)
    second = (bias_right_2, bias_left_2, bias_rest_2, kv_grads, qa_own, qa_away)
    from_left, from_right, bias_rest, second = lax.optimization_barrier(
        (from_left, from_right, bias_rest, second)
    )
    bias_right_2, bias_left_2, bias_rest_2, kv_grads, qa_own, qa_away = second
    from_left, from_right = ring_onward(bias_rest, from_left, from_right)
    sums = added(bias_rest[:4], from_left, from_right)
    from_left, from_right = along_row(bias_right_2, 1, 0), along_row(bias_left_2, -1, 0)
    kv_parts = lax.all_to_all(kv_grads, "col", 0, 0, tiled=True)
    kv_parts = kv_parts.reshape((devices // 2, 2) + kv_parts.shape[1:])
    kv_sum = jnp.sum(kv_parts.astype(jnp.float32), axis=0)
    key_gradient = jnp.concatenate([kv_sum[0, ..., :half], kv_sum[1, ..., :half]], axis=2) * scaling
    key_gradient = key_gradient.astype(jnp.bfloat16)
    value_gradient = jnp.concatenate([kv_sum[0, ..., half:], kv_sum[1, ..., half:]], axis=2)
    value_gradient = value_gradient.astype(jnp.bfloat16)
    from_left, from_right = ring_onward(bias_rest_2, from_left, from_right)
    sums = jnp.stack([sums, added(bias_rest_2[:4], from_left, from_right)], axis=1)
    qa_back = swapped(qa_away)
    query_gradient = in_order(qa_own[..., :half], qa_back[..., :half], 2)
    gate_gradient = in_order(qa_own[..., half:], qa_back[..., half:], 2)
    low_sums = sums.astype(jnp.bfloat16)
    diagonal = []
    for index in range(row_count * devices):
        up = (index // devices + row_ring) % row_count
        diagonal.append((index, up * devices + (index % devices ^ 1)))
    from_high = along_row(low_sums[2], 0, 1)
    from_core = swapped(low_sums[1])
    from_diagonal = lax.ppermute(low_sums[3], ("row", "col"), diagonal)
    bias_own = added(sums[0], from_high)
    bias_away = added(from_core, from_diagonal)
    bias_gradient = in_order(bias_own, bias_away, 0)
    return (query_gradient, key_gradient, value_gradient, gate_gradient, bias_gradient)


def solution(mesh):
    placed = (
        P("row", "col", None),
        P("row", "col", None),
        P("row", "col", None),
        P("row", "col", None),
        P(None, "col", None),
        P("row", "col"),
        P(),
        P("row", "col", None),
    )
    return jax.shard_map(
        local,
        mesh=mesh,
        in_specs=placed,
        out_specs=(
            P("row", "col", None),
            P("row", "col", None),
            P("row", "col", None),
            P("row", "col", None),
            P(None, "col", "row"),
        ),
        check_vma=False,
    )
```

```python
import functools
import math

import jax
import jax.numpy as jnp
from jax import lax
from jax.experimental import pallas as pl
from jax.experimental.pallas import tpu as pltpu
from jax.sharding import PartitionSpec as P

HEADS = 4
NEG_FILL = -1000000000.0
LOG2E = math.log2(math.e)
CHUNK = 16
UNROLL = 12
MASK_ROWS = 16
PIECES = 8
VMEM_WIDE = 60 * 1024 * 1024


def attention_kernel(head, *refs):
    place_ref, qg_mine_ref, qg_other_ref, kv_ref, mask_ref, cotangent_ref, weight_ref, bias_ref = refs[:8]
    earlier = refs[8 : 8 + 3 * head]
    qa_own_ref, qa_away_ref, dkv_ref, right_out_ref, left_out_ref, rest_out_ref = refs[8 + 3 * head :][:6]
    gated_ref, cap_ref, s_ref, b2_ref, acc_ref, dp_ref, de_ref, row_ref, dbias_ref = refs[14 + 3 * head :]
    step = pl.program_id(0)
    last = pl.num_programs(0) - 1
    queries, keys = bias_ref.shape
    half = queries // 2
    head_width = qg_mine_ref.shape[2] // 4
    core = place_ref[PIECES]
    scaling = 1.0 / math.sqrt(head_width)

    @pl.when(step == 0)
    def _():
        def fill(index, carry):
            part = pl.ds(index * CHUNK, CHUNK)
            b2_ref[part, :] = bias_ref[part, :].astype(jnp.float32) * LOG2E
            acc_ref[part, :] = jnp.zeros((CHUNK, keys), jnp.float32)
            return carry

        lax.fori_loop(0, queries // CHUNK, fill, 0)
        sources, _, lanes = cotangent_ref.shape
        cotangent = cotangent_ref[...].astype(jnp.float32)
        cotangent = cotangent.reshape(sources, 2, cap_ref.shape[0], lanes // sources, lanes)
        for column in range(cotangent.shape[2]):
            for side in range(2):
                part = cotangent[:, side, column].reshape(lanes, lanes).astype(jnp.bfloat16)
                gated = jnp.dot(weight_ref[...], part, preferred_element_type=jnp.float32)
                gated_ref[column, side * half : (side + 1) * half] = gated.T[:half]
        masks = mask_ref[...].astype(jnp.float32)
        for column in range(cap_ref.shape[0]):
            pieces = [
                masks[source, column : column + 1, :half] for source in range(masks.shape[0])
            ]
            cap_ref[column] = jnp.where(
                jnp.concatenate(pieces, axis=1) > 0.5, 1e30, NEG_FILL * LOG2E
            )

    lane = lax.broadcasted_iota(jnp.int32, (queries, 4 * head_width), 1)
    transposed = (((1,), (1,)), ((), ()))
    is_query = (lane >= head * head_width) & (lane < (head + 1) * head_width)
    is_gate = (lane >= (head + 2) * head_width) & (lane < (head + 3) * head_width)
    kvs, query_rows, grad_rows, slopes = [], [], [], []
    for unit in range(2):
        kvs.append(kv_ref[:, unit * half : (unit + 1) * half, :].reshape(keys, 4 * head_width))
        mine = qg_mine_ref[unit]
        other = qg_other_ref[unit]
        query_gate = jnp.concatenate(
            [jnp.where(core == 0, mine, other), jnp.where(core == 0, other, mine)], axis=0
        )
        sigma = jax.nn.sigmoid(query_gate.astype(jnp.float32))
        gated_grad = gated_ref[2 * step + unit] * sigma
        slopes.append(gated_grad * (1.0 - sigma))
        zero = jnp.zeros_like(query_gate)
        query_rows.append(jnp.where(is_query, query_gate, zero))
        grad_rows.append(jnp.where(is_gate, gated_grad.astype(jnp.bfloat16), zero))

    def scores_of(unit):
        s_ref[unit * queries : (unit + 1) * queries, :] = lax.dot_general(
            query_rows[unit], kvs[unit], transposed, preferred_element_type=jnp.float32
        )

    def soften(unit):
        cap = cap_ref[2 * step + unit]

        def one(index, carry):
            inner = index * CHUNK
            part = pl.ds(unit * queries + inner, CHUNK)
            scores = s_ref[part, :] * (scaling * LOG2E) + b2_ref[pl.ds(inner, CHUNK), :]
            scores = jnp.minimum(scores, cap)
            weights = jnp.exp2(scores - jnp.max(scores, axis=1, keepdims=True))
            row_ref[part, :] = jnp.broadcast_to(jnp.sum(weights, axis=1, keepdims=True), (CHUNK, 128))
            de_ref[pl.ds((2 * unit + 1) * queries + inner, CHUNK), :] = weights.astype(jnp.bfloat16)
            return carry

        lax.fori_loop(0, queries // CHUNK, one, 0, unroll=UNROLL)

    def cotangents(unit):
        part = slice(unit * queries, (unit + 1) * queries)
        weights_low = de_ref[(2 * unit + 1) * queries : (2 * unit + 2) * queries, :]
        inverse = 1.0 / row_ref[part, :]
        attended = jnp.dot(weights_low, kvs[unit], preferred_element_type=jnp.float32) * inverse
        grad_wide = grad_rows[unit].astype(jnp.float32)
        delta = jnp.sum(grad_wide * attended, axis=1, keepdims=True)
        row_ref[part, :] = delta * inverse
        grad_scaled = (grad_wide * inverse).astype(jnp.bfloat16)
        dp_ref[part, :] = lax.dot_general(
            grad_scaled, kvs[unit], transposed, preferred_element_type=jnp.float32
        )
        return attended, grad_scaled

    def backward(unit):
        def one(index, carry):
            inner = index * CHUNK
            part = pl.ds(unit * queries + inner, CHUNK)
            weights = de_ref[pl.ds((2 * unit + 1) * queries + inner, CHUNK), :].astype(jnp.float32)
            score_grad = weights * (dp_ref[part, :] - row_ref[part, :1])
            acc_ref[pl.ds(inner, CHUNK), :] += score_grad
            de_ref[pl.ds(2 * unit * queries + inner, CHUNK), :] = score_grad.astype(jnp.bfloat16)
            return carry

        lax.fori_loop(0, queries // CHUNK, one, 0, unroll=UNROLL)

    def finish(unit, attended, grad_scaled):
        low = de_ref[2 * unit * queries : (2 * unit + 1) * queries, :]
        query = jnp.dot(low, kvs[unit], preferred_element_type=jnp.float32) * scaling
        merged = jnp.where(is_query, query, jnp.where(is_gate, attended * slopes[unit], 0.0))
        own = jnp.where(core == 0, merged[:half], merged[half:])
        away = jnp.where(core == 0, merged[half:], merged[:half])
        sides = jnp.concatenate([query_rows[unit], grad_scaled], axis=0)
        key_value = lax.dot_general(
            sides,
            de_ref[2 * unit * queries : (2 * unit + 2) * queries, :],
            (((0,), (0,)), ((), ())),
            preferred_element_type=jnp.float32,
        ).T.reshape(dkv_ref.shape[0], half, 4 * head_width)
        if earlier:
            own = own + earlier[0][unit].astype(jnp.float32)
            away = away + earlier[1][unit].astype(jnp.float32)
            key_value = key_value + earlier[2][:, unit].astype(jnp.float32)
        qa_own_ref[unit] = own.astype(jnp.bfloat16)
        qa_away_ref[unit] = away.astype(jnp.bfloat16)
        dkv_ref[:, unit] = key_value.astype(jnp.bfloat16)

    scores_of(0)
    scores_of(1)
    soften(0)
    first = cotangents(0)
    soften(1)
    second = cotangents(1)
    backward(0)
    finish(0, *first)
    backward(1)
    finish(1, *second)

    @pl.when(step == last)
    def _():
        width = dbias_ref.shape[2]
        for piece in range(PIECES):
            for side in range(2):
                part = acc_ref[side * half : (side + 1) * half, piece * width : (piece + 1) * width]
                target = 2 * place_ref[piece] + (side + core) % 2
                dbias_ref[target] = part.astype(jnp.bfloat16)
        right_out_ref[...] = dbias_ref[8:10]
        left_out_ref[...] = dbias_ref[10:12]
        rest_out_ref[:8] = dbias_ref[:8]
        rest_out_ref[8:] = dbias_ref[12:]


def prepare_kernel(key_ref, value_ref, mask_ref, cotangent_ref, packed_ref):
    columns, tokens, channels = key_ref.shape
    half = channels // 2
    devices = packed_ref.shape[0]
    pairs = columns * tokens
    rows = cotangent_ref.shape[0] * cotangent_ref.shape[1]
    mask = mask_ref[...].astype(jnp.float32)
    mask = jnp.concatenate([mask, jnp.zeros((columns, channels - tokens), jnp.float32)], axis=1)
    filler = jnp.zeros((MASK_ROWS - columns, channels), jnp.float32)
    mask = jnp.concatenate([mask, filler], axis=0).astype(jnp.bfloat16)
    for column in range(columns):
        key = key_ref[column]
        value = value_ref[column]
        sides = [
            jnp.concatenate([key[:, :half], value[:, :half]], axis=1),
            jnp.concatenate([key[:, half:], value[:, half:]], axis=1),
        ]
        for device in range(devices):
            packed_ref[device, column * tokens : (column + 1) * tokens, :] = sides[device % 2]
    cotangent = cotangent_ref[...].astype(jnp.float32).reshape(rows, cotangent_ref.shape[2])
    filler = jnp.zeros((rows, channels - tokens), jnp.float32)
    for device in range(devices):
        packed_ref[device, pairs + 2 * rows :, :] = mask
        part = cotangent[:, device * tokens : (device + 1) * tokens]
        part = jnp.concatenate([part, filler], axis=1).astype(jnp.bfloat16)
        start = pairs + device % 2 * rows
        packed_ref[device, start : start + rows, :] = part
        packed_ref[device ^ 1, start : start + rows, :] = part


def prepare(key, value, mask, cotangent, devices):
    columns, tokens, channels = key.shape
    rows = columns * tokens + 2 * cotangent.shape[0] * cotangent.shape[1] + MASK_ROWS

    def whole(shape):
        return pl.BlockSpec(shape, lambda i: (0,) * len(shape))

    out = (devices, rows, channels)
    return pl.pallas_call(
        prepare_kernel,
        grid=(1,),
        in_specs=[whole(key.shape), whole(value.shape), whole(mask.shape), whole(cotangent.shape)],
        out_specs=whole(out),
        out_shape=jax.ShapeDtypeStruct(out, jnp.bfloat16),
        compiler_params=pltpu.CompilerParams(vmem_limit_bytes=VMEM_WIDE),
        name="prepare_exchange",
    )(key, value, mask, cotangent)


def attend(head, places, mine, other, received, weight, bias, row_count, earlier):
    columns, tokens, lanes = mine.shape
    queries, keys = bias.shape[0] // 2, bias.shape[1]
    width = keys // row_count
    devices = received.shape[0]
    mask_place = received.shape[1] // MASK_ROWS - 1
    cotangent_rows = 2 * columns * lanes // devices
    cotangent_place = columns * tokens // cotangent_rows
    work = columns * queries * keys

    def whole(shape):
        return pl.BlockSpec(shape, lambda j, places: (0,) * len(shape))

    column_spec = pl.BlockSpec((2, tokens, lanes), lambda j, places: (j, 0, 0))
    grad_spec = pl.BlockSpec((devices, 2, tokens, lanes), lambda j, places: (0, j, 0, 0))
    piece = (tokens, width)
    return pl.pallas_call(
        functools.partial(attention_kernel, head),
        grid_spec=pltpu.PrefetchScalarGridSpec(
            num_scalar_prefetch=1,
            grid=(columns // 2,),
            in_specs=[
                column_spec,
                column_spec,
                pl.BlockSpec((devices, 2 * tokens, lanes), lambda j, places: (0, j, 0)),
                pl.BlockSpec((devices, MASK_ROWS, lanes), lambda j, places: (0, mask_place, 0)),
                pl.BlockSpec(
                    (devices, cotangent_rows, lanes), lambda j, places: (0, cotangent_place, 0)
                ),
                whole(weight.shape),
                pl.BlockSpec((queries, keys), lambda j, places: (head, 0)),
            ]
            + [column_spec, column_spec, grad_spec][: len(earlier)],
            out_specs=[
                column_spec,
                column_spec,
                grad_spec,
                whole((2,) + piece),
                whole((2,) + piece),
                whole((12,) + piece),
            ],
            scratch_shapes=[
                pltpu.VMEM((columns, queries, lanes), jnp.float32),
                pltpu.VMEM((columns, 1, keys), jnp.float32),
                pltpu.VMEM((2 * queries, keys), jnp.float32),
                pltpu.VMEM((queries, keys), jnp.float32),
                pltpu.VMEM((queries, keys), jnp.float32),
                pltpu.VMEM((2 * queries, keys), jnp.float32),
                pltpu.VMEM((4 * queries, keys), jnp.bfloat16),
                pltpu.VMEM((2 * queries, 128), jnp.float32),
                pltpu.VMEM((16,) + piece, jnp.bfloat16),
            ],
        ),
        out_shape=[
            jax.ShapeDtypeStruct(mine.shape, jnp.bfloat16),
            jax.ShapeDtypeStruct(mine.shape, jnp.bfloat16),
            jax.ShapeDtypeStruct((devices,) + mine.shape, jnp.bfloat16),
            jax.ShapeDtypeStruct((2,) + piece, jnp.bfloat16),
            jax.ShapeDtypeStruct((2,) + piece, jnp.bfloat16),
            jax.ShapeDtypeStruct((12,) + piece, jnp.bfloat16),
        ],
        compiler_params=pltpu.CompilerParams(vmem_limit_bytes=48 * 1024 * 1024),
        cost_estimate=pl.CostEstimate(flops=12 * 128 * work, bytes_accessed=16 * 2**20, transcendentals=work),
        name="attention_head",
    )(places, mine, other, received, received, received, weight, bias, *earlier)


def local(
    query_vectors,
    key_vectors,
    value_vectors,
    gate_logits,
    pair_bias,
    pair_mask,
    output_weight,
    output_cotangent,
):
    columns, tokens, channels = query_vectors.shape
    half = channels // 2
    devices = lax.axis_size("col")
    row_count = lax.axis_size("row")
    core = lax.axis_index("col") % 2
    scaling = 1.0 / math.sqrt(channels // HEADS)
    swap = [(index, index ^ 1) for index in range(devices)]
    keys = pair_bias.shape[2]

    def mine_other(array, axis):
        size = array.shape[axis] // 2
        low = lax.slice_in_dim(array, 0, size, axis=axis)
        high = lax.slice_in_dim(array, size, 2 * size, axis=axis)
        return jnp.where(core == 0, low, high), jnp.where(core == 0, high, low)

    def in_order(mine, other, axis):
        return jnp.where(
            core == 0,
            jnp.concatenate([mine, other], axis=axis),
            jnp.concatenate([other, mine], axis=axis),
        )

    def swapped(array):
        return lax.ppermute(array, "col", swap)

    bias_mine, bias_other = mine_other(pair_bias, 0)
    bias_pair = in_order(bias_mine, swapped(bias_other), 1).reshape(-1, keys)

    packed = prepare(key_vectors, value_vectors, pair_mask, output_cotangent, devices)
    received = lax.all_to_all(packed, "col", 0, 0, tiled=True)
    place = lax.axis_index("row")
    row_ring = row_count // 2
    places = [
        2 * ((index % row_ring - place) % row_ring) + (index // row_ring - place // row_ring) % 2
        for index in range(row_count)
    ]
    places.append(core)
    places = jnp.stack(places).astype(jnp.int32)

    query_mine, query_other = mine_other(query_vectors, 2)
    gate_mine, gate_other = mine_other(gate_logits, 2)
    qg_mine = jnp.concatenate([query_mine, gate_mine], axis=2)
    qg_other = swapped(jnp.concatenate([query_other, gate_other], axis=2))
    weight_mine, _ = mine_other(output_weight, 0)
    weight_mine = jnp.pad(weight_mine, ((half, 0), (0, 0)))

    shared = (places, qg_mine, qg_other, received, weight_mine, bias_pair, row_count)
    *earlier, bias_right, bias_left, bias_rest = attend(0, *shared, ())
    (qa_own, qa_away, kv_grads, bias_right_2, bias_left_2, bias_rest_2) = attend(1, *shared, tuple(earlier))

    def along_row(array, turn, side):
        pairs = []
        for index in range(row_count):
            high, low = index // row_ring, index % row_ring
            pairs.append((index, ((high + side) % 2) * row_ring + (low + turn) % row_ring))
        return lax.ppermute(array, "row", pairs)

    def added(*parts):
        return sum(part.astype(jnp.float32) for part in parts)

    def ring_onward(rest, from_left, from_right):
        onward = jnp.concatenate([added(rest[4:6], from_left).astype(jnp.bfloat16), rest[6:8]])
        backward = jnp.concatenate([rest[8:10], added(rest[10:], from_right).astype(jnp.bfloat16)])
        return along_row(onward, 1, 0), along_row(backward, -1, 0)

    from_left, from_right = along_row(bias_right, 1, 0), along_row(bias_left, -1, 0)
    second = (bias_right_2, bias_left_2, bias_rest_2, kv_grads, qa_own, qa_away)
    from_left, from_right, bias_rest, second = lax.optimization_barrier(
        (from_left, from_right, bias_rest, second)
    )
    bias_right_2, bias_left_2, bias_rest_2, kv_grads, qa_own, qa_away = second
    qa_back = swapped(qa_away)
    from_left, from_right, bias_right_2, bias_left_2, qa_back = lax.optimization_barrier(
        (from_left, from_right, bias_right_2, bias_left_2, qa_back)
    )
    from_left, from_right = ring_onward(bias_rest, from_left, from_right)
    sums = added(bias_rest[:4], from_left, from_right)
    from_left, from_right = along_row(bias_right_2, 1, 0), along_row(bias_left_2, -1, 0)
    kv_parts = lax.all_to_all(kv_grads, "col", 0, 0, tiled=True)
    kv_parts = kv_parts.reshape((devices // 2, 2) + kv_parts.shape[1:])
    kv_sum = jnp.sum(kv_parts.astype(jnp.float32), axis=0)
    key_gradient = jnp.concatenate([kv_sum[0, ..., :half], kv_sum[1, ..., :half]], axis=2) * scaling
    key_gradient = key_gradient.astype(jnp.bfloat16)
    value_gradient = jnp.concatenate([kv_sum[0, ..., half:], kv_sum[1, ..., half:]], axis=2)
    value_gradient = value_gradient.astype(jnp.bfloat16)
    from_left, from_right = ring_onward(bias_rest_2, from_left, from_right)
    sums = jnp.stack([sums, added(bias_rest_2[:4], from_left, from_right)], axis=1)
    query_gradient = in_order(qa_own[..., :half], qa_back[..., :half], 2)
    gate_gradient = in_order(qa_own[..., half:], qa_back[..., half:], 2)
    low_sums = sums.astype(jnp.bfloat16)
    diagonal = []
    for index in range(row_count * devices):
        up = (index // devices + row_ring) % row_count
        diagonal.append((index, up * devices + (index % devices ^ 1)))
    from_high, from_core, from_diagonal, key_gradient, value_gradient = lax.optimization_barrier((
        along_row(low_sums[2], 0, 1),
        swapped(low_sums[1]),
        lax.ppermute(low_sums[3], ("row", "col"), diagonal),
        key_gradient,
        value_gradient,
    ))
    bias_own = added(sums[0], from_high)
    bias_away = added(from_core, from_diagonal)
    bias_gradient = in_order(bias_own, bias_away, 0)
    return (query_gradient, key_gradient, value_gradient, gate_gradient, bias_gradient)


def solution(mesh):
    placed = (
        P("row", "col", None),
        P("row", "col", None),
        P("row", "col", None),
        P("row", "col", None),
        P(None, "col", None),
        P("row", "col"),
        P(),
        P("row", "col", None),
    )
    return jax.shard_map(
        local,
        mesh=mesh,
        in_specs=placed,
        out_specs=(
            P("row", "col", None),
            P("row", "col", None),
            P("row", "col", None),
            P("row", "col", None),
            P(None, "col", "row"),
        ),
        check_vma=False,
    )
```

```python
import functools
import math

import jax
import jax.numpy as jnp
from jax import lax
from jax.experimental import pallas as pl
from jax.experimental.pallas import tpu as pltpu
from jax.sharding import PartitionSpec as P

HEADS = 4
NEG_FILL = -1000000000.0
LOG2E = math.log2(math.e)
CHUNK = 16
UNROLL = 12
MASK_ROWS = 16
PIECES = 8
VMEM_WIDE = 60 * 1024 * 1024


def attention_kernel(head, *refs):
    place_ref, qg_mine_ref, qg_other_ref, kv_ref, mask_ref, cotangent_ref, weight_ref, bias_ref = refs[:8]
    earlier = refs[8 : 8 + 3 * head]
    qa_own_ref, qa_away_ref, dkv_ref, right_out_ref, left_out_ref, rest_out_ref = refs[8 + 3 * head :][:6]
    gated_ref, cap_ref, s_ref, b2_ref, acc_ref, dp_ref, de_ref, row_ref, dbias_ref = refs[14 + 3 * head :]
    step = pl.program_id(0)
    last = pl.num_programs(0) - 1
    queries, keys = bias_ref.shape
    half = queries // 2
    head_width = qg_mine_ref.shape[2] // 4
    core = place_ref[PIECES]
    scaling = 1.0 / math.sqrt(head_width)

    @pl.when(step == 0)
    def _():
        def fill(index, carry):
            part = pl.ds(index * CHUNK, CHUNK)
            b2_ref[part, :] = bias_ref[part, :].astype(jnp.float32) * LOG2E
            acc_ref[part, :] = jnp.zeros((CHUNK, keys), jnp.float32)
            return carry

        lax.fori_loop(0, queries // CHUNK, fill, 0)
        sources, _, lanes = cotangent_ref.shape
        cotangent = cotangent_ref[...].astype(jnp.float32)
        cotangent = cotangent.reshape(sources, 2, cap_ref.shape[0], lanes // sources, lanes)
        for column in range(cotangent.shape[2]):
            for side in range(2):
                part = cotangent[:, side, column].reshape(lanes, lanes).astype(jnp.bfloat16)
                gated = jnp.dot(weight_ref[...], part, preferred_element_type=jnp.float32)
                gated_ref[column, side * half : (side + 1) * half] = gated.T[:half]
        masks = mask_ref[...].astype(jnp.float32)
        for column in range(cap_ref.shape[0]):
            pieces = [
                masks[source, column : column + 1, :half] for source in range(masks.shape[0])
            ]
            cap_ref[column] = jnp.where(
                jnp.concatenate(pieces, axis=1) > 0.5, 1e30, NEG_FILL * LOG2E
            )

    lane = lax.broadcasted_iota(jnp.int32, (queries, 4 * head_width), 1)
    transposed = (((1,), (1,)), ((), ()))
    is_query = (lane >= head * head_width) & (lane < (head + 1) * head_width)
    is_gate = (lane >= (head + 2) * head_width) & (lane < (head + 3) * head_width)
    kvs, query_rows, grad_rows, slopes = [], [], [], []
    for unit in range(2):
        kvs.append(kv_ref[:, unit * half : (unit + 1) * half, :].reshape(keys, 4 * head_width))
        mine = qg_mine_ref[unit]
        other = qg_other_ref[unit]
        query_gate = jnp.concatenate(
            [jnp.where(core == 0, mine, other), jnp.where(core == 0, other, mine)], axis=0
        )
        sigma = jax.nn.sigmoid(query_gate.astype(jnp.float32))
        gated_grad = gated_ref[2 * step + unit] * sigma
        slopes.append(gated_grad * (1.0 - sigma))
        zero = jnp.zeros_like(query_gate)
        query_rows.append(jnp.where(is_query, query_gate, zero))
        grad_rows.append(jnp.where(is_gate, gated_grad.astype(jnp.bfloat16), zero))

    def scores_of(unit):
        s_ref[unit * queries : (unit + 1) * queries, :] = lax.dot_general(
            query_rows[unit], kvs[unit], transposed, preferred_element_type=jnp.float32
        )

    def soften(unit):
        cap = cap_ref[2 * step + unit]

        def one(index, carry):
            inner = index * CHUNK
            part = pl.ds(unit * queries + inner, CHUNK)
            scores = s_ref[part, :] * (scaling * LOG2E) + b2_ref[pl.ds(inner, CHUNK), :]
            scores = jnp.minimum(scores, cap)
            weights = jnp.exp2(scores - jnp.max(scores, axis=1, keepdims=True))
            row_ref[part, :] = jnp.broadcast_to(jnp.sum(weights, axis=1, keepdims=True), (CHUNK, 128))
            de_ref[pl.ds((2 * unit + 1) * queries + inner, CHUNK), :] = weights.astype(jnp.bfloat16)
            return carry

        lax.fori_loop(0, queries // CHUNK, one, 0, unroll=UNROLL)

    def cotangents(unit):
        part = slice(unit * queries, (unit + 1) * queries)
        weights_low = de_ref[(2 * unit + 1) * queries : (2 * unit + 2) * queries, :]
        inverse = 1.0 / row_ref[part, :]
        attended = jnp.dot(weights_low, kvs[unit], preferred_element_type=jnp.float32) * inverse
        grad_wide = grad_rows[unit].astype(jnp.float32)
        delta = jnp.sum(grad_wide * attended, axis=1, keepdims=True)
        row_ref[part, :] = delta * inverse
        grad_scaled = (grad_wide * inverse).astype(jnp.bfloat16)
        dp_ref[part, :] = lax.dot_general(
            grad_scaled, kvs[unit], transposed, preferred_element_type=jnp.float32
        )
        return attended, grad_scaled

    def backward(unit):
        def one(index, carry):
            inner = index * CHUNK
            part = pl.ds(unit * queries + inner, CHUNK)
            weights = de_ref[pl.ds((2 * unit + 1) * queries + inner, CHUNK), :].astype(jnp.float32)
            score_grad = weights * (dp_ref[part, :] - row_ref[part, :1])
            acc_ref[pl.ds(inner, CHUNK), :] += score_grad
            de_ref[pl.ds(2 * unit * queries + inner, CHUNK), :] = score_grad.astype(jnp.bfloat16)
            return carry

        lax.fori_loop(0, queries // CHUNK, one, 0, unroll=UNROLL)

    def finish(unit, attended, grad_scaled):
        low = de_ref[2 * unit * queries : (2 * unit + 1) * queries, :]
        query = jnp.dot(low, kvs[unit], preferred_element_type=jnp.float32) * scaling
        merged = jnp.where(is_query, query, jnp.where(is_gate, attended * slopes[unit], 0.0))
        own = jnp.where(core == 0, merged[:half], merged[half:])
        away = jnp.where(core == 0, merged[half:], merged[:half])
        sides = jnp.concatenate([query_rows[unit], grad_scaled], axis=0)
        key_value = lax.dot_general(
            sides,
            de_ref[2 * unit * queries : (2 * unit + 2) * queries, :],
            (((0,), (0,)), ((), ())),
            preferred_element_type=jnp.float32,
        )
        keys_here = key_value[head * head_width : (head + 1) * head_width]
        values_here = key_value[(head + 2) * head_width : (head + 3) * head_width]
        if earlier:
            own = own + earlier[0][unit].astype(jnp.float32)
            away = away + earlier[1][unit].astype(jnp.float32)
            passed = earlier[2][unit].astype(jnp.float32)
            key_value = jnp.concatenate(
                [passed[:head_width], keys_here, passed[head_width:], values_here], axis=0
            )
            key_value = key_value.T.reshape(dkv_ref.shape[0], half, 4 * head_width)
            dkv_ref[:, unit] = key_value.astype(jnp.bfloat16)
        else:
            dkv_ref[unit] = jnp.concatenate([keys_here, values_here], axis=0).astype(jnp.bfloat16)
        qa_own_ref[unit] = own.astype(jnp.bfloat16)
        qa_away_ref[unit] = away.astype(jnp.bfloat16)

    scores_of(0)
    scores_of(1)
    soften(0)
    first = cotangents(0)
    soften(1)
    second = cotangents(1)
    backward(0)
    finish(0, *first)
    backward(1)
    finish(1, *second)

    @pl.when(step == last)
    def _():
        width = dbias_ref.shape[2]
        for piece in range(PIECES):
            for side in range(2):
                part = acc_ref[side * half : (side + 1) * half, piece * width : (piece + 1) * width]
                target = 2 * place_ref[piece] + (side + core) % 2
                dbias_ref[target] = part.astype(jnp.bfloat16)
        right_out_ref[...] = dbias_ref[8:10]
        left_out_ref[...] = dbias_ref[10:12]
        rest_out_ref[:8] = dbias_ref[:8]
        rest_out_ref[8:] = dbias_ref[12:]


def prepare_kernel(key_ref, value_ref, mask_ref, cotangent_ref, packed_ref):
    columns, tokens, channels = key_ref.shape
    half = channels // 2
    devices = packed_ref.shape[0]
    pairs = columns * tokens
    rows = cotangent_ref.shape[0] * cotangent_ref.shape[1]
    mask = mask_ref[...].astype(jnp.float32)
    mask = jnp.concatenate([mask, jnp.zeros((columns, channels - tokens), jnp.float32)], axis=1)
    filler = jnp.zeros((MASK_ROWS - columns, channels), jnp.float32)
    mask = jnp.concatenate([mask, filler], axis=0).astype(jnp.bfloat16)
    for column in range(columns):
        key = key_ref[column]
        value = value_ref[column]
        sides = [
            jnp.concatenate([key[:, :half], value[:, :half]], axis=1),
            jnp.concatenate([key[:, half:], value[:, half:]], axis=1),
        ]
        for device in range(devices):
            packed_ref[device, column * tokens : (column + 1) * tokens, :] = sides[device % 2]
    cotangent = cotangent_ref[...].astype(jnp.float32).reshape(rows, cotangent_ref.shape[2])
    filler = jnp.zeros((rows, channels - tokens), jnp.float32)
    for device in range(devices):
        packed_ref[device, pairs + 2 * rows :, :] = mask
        part = cotangent[:, device * tokens : (device + 1) * tokens]
        part = jnp.concatenate([part, filler], axis=1).astype(jnp.bfloat16)
        start = pairs + device % 2 * rows
        packed_ref[device, start : start + rows, :] = part
        packed_ref[device ^ 1, start : start + rows, :] = part


def prepare(key, value, mask, cotangent, devices):
    columns, tokens, channels = key.shape
    rows = columns * tokens + 2 * cotangent.shape[0] * cotangent.shape[1] + MASK_ROWS

    def whole(shape):
        return pl.BlockSpec(shape, lambda i: (0,) * len(shape))

    out = (devices, rows, channels)
    return pl.pallas_call(
        prepare_kernel,
        grid=(1,),
        in_specs=[whole(key.shape), whole(value.shape), whole(mask.shape), whole(cotangent.shape)],
        out_specs=whole(out),
        out_shape=jax.ShapeDtypeStruct(out, jnp.bfloat16),
        compiler_params=pltpu.CompilerParams(vmem_limit_bytes=VMEM_WIDE),
        name="prepare_exchange",
    )(key, value, mask, cotangent)


def attend(head, places, mine, other, received, weight, bias, row_count, earlier):
    columns, tokens, lanes = mine.shape
    queries, keys = bias.shape[0] // 2, bias.shape[1]
    width = keys // row_count
    devices = received.shape[0]
    mask_place = received.shape[1] // MASK_ROWS - 1
    cotangent_rows = 2 * columns * lanes // devices
    cotangent_place = columns * tokens // cotangent_rows
    work = columns * queries * keys

    def whole(shape):
        return pl.BlockSpec(shape, lambda j, places: (0,) * len(shape))

    column_spec = pl.BlockSpec((2, tokens, lanes), lambda j, places: (j, 0, 0))
    part_spec = pl.BlockSpec((2, lanes // 2, keys), lambda j, places: (j, 0, 0))
    part_shape = (columns, lanes // 2, keys)
    if earlier:
        grad_spec = pl.BlockSpec((devices, 2, tokens, lanes), lambda j, places: (0, j, 0, 0))
        grad_shape = (devices,) + mine.shape
    else:
        grad_spec, grad_shape = part_spec, part_shape
    piece = (tokens, width)
    return pl.pallas_call(
        functools.partial(attention_kernel, head),
        grid_spec=pltpu.PrefetchScalarGridSpec(
            num_scalar_prefetch=1,
            grid=(columns // 2,),
            in_specs=[
                column_spec,
                column_spec,
                pl.BlockSpec((devices, 2 * tokens, lanes), lambda j, places: (0, j, 0)),
                pl.BlockSpec((devices, MASK_ROWS, lanes), lambda j, places: (0, mask_place, 0)),
                pl.BlockSpec(
                    (devices, cotangent_rows, lanes), lambda j, places: (0, cotangent_place, 0)
                ),
                whole(weight.shape),
                pl.BlockSpec((queries, keys), lambda j, places: (head, 0)),
            ]
            + [column_spec, column_spec, part_spec][: len(earlier)],
            out_specs=[
                column_spec,
                column_spec,
                grad_spec,
                whole((2,) + piece),
                whole((2,) + piece),
                whole((12,) + piece),
            ],
            scratch_shapes=[
                pltpu.VMEM((columns, queries, lanes), jnp.float32),
                pltpu.VMEM((columns, 1, keys), jnp.float32),
                pltpu.VMEM((2 * queries, keys), jnp.float32),
                pltpu.VMEM((queries, keys), jnp.float32),
                pltpu.VMEM((queries, keys), jnp.float32),
                pltpu.VMEM((2 * queries, keys), jnp.float32),
                pltpu.VMEM((4 * queries, keys), jnp.bfloat16),
                pltpu.VMEM((2 * queries, 128), jnp.float32),
                pltpu.VMEM((16,) + piece, jnp.bfloat16),
            ],
        ),
        out_shape=[
            jax.ShapeDtypeStruct(mine.shape, jnp.bfloat16),
            jax.ShapeDtypeStruct(mine.shape, jnp.bfloat16),
            jax.ShapeDtypeStruct(grad_shape, jnp.bfloat16),
            jax.ShapeDtypeStruct((2,) + piece, jnp.bfloat16),
            jax.ShapeDtypeStruct((2,) + piece, jnp.bfloat16),
            jax.ShapeDtypeStruct((12,) + piece, jnp.bfloat16),
        ],
        compiler_params=pltpu.CompilerParams(vmem_limit_bytes=48 * 1024 * 1024),
        cost_estimate=pl.CostEstimate(flops=12 * 128 * work, bytes_accessed=16 * 2**20, transcendentals=work),
        name="attention_head",
    )(places, mine, other, received, received, received, weight, bias, *earlier)


def local(
    query_vectors,
    key_vectors,
    value_vectors,
    gate_logits,
    pair_bias,
    pair_mask,
    output_weight,
    output_cotangent,
):
    columns, tokens, channels = query_vectors.shape
    half = channels // 2
    devices = lax.axis_size("col")
    row_count = lax.axis_size("row")
    core = lax.axis_index("col") % 2
    scaling = 1.0 / math.sqrt(channels // HEADS)
    swap = [(index, index ^ 1) for index in range(devices)]
    keys = pair_bias.shape[2]

    def mine_other(array, axis):
        size = array.shape[axis] // 2
        low = lax.slice_in_dim(array, 0, size, axis=axis)
        high = lax.slice_in_dim(array, size, 2 * size, axis=axis)
        return jnp.where(core == 0, low, high), jnp.where(core == 0, high, low)

    def in_order(mine, other, axis):
        return jnp.where(
            core == 0,
            jnp.concatenate([mine, other], axis=axis),
            jnp.concatenate([other, mine], axis=axis),
        )

    def swapped(array):
        return lax.ppermute(array, "col", swap)

    bias_mine, bias_other = mine_other(pair_bias, 0)
    bias_pair = in_order(bias_mine, swapped(bias_other), 1).reshape(-1, keys)

    packed = prepare(key_vectors, value_vectors, pair_mask, output_cotangent, devices)
    received = lax.all_to_all(packed, "col", 0, 0, tiled=True)
    place = lax.axis_index("row")
    row_ring = row_count // 2
    places = [
        2 * ((index % row_ring - place) % row_ring) + (index // row_ring - place // row_ring) % 2
        for index in range(row_count)
    ]
    places.append(core)
    places = jnp.stack(places).astype(jnp.int32)

    query_mine, query_other = mine_other(query_vectors, 2)
    gate_mine, gate_other = mine_other(gate_logits, 2)
    qg_mine = jnp.concatenate([query_mine, gate_mine], axis=2)
    qg_other = swapped(jnp.concatenate([query_other, gate_other], axis=2))
    weight_mine, _ = mine_other(output_weight, 0)
    weight_mine = jnp.pad(weight_mine, ((half, 0), (0, 0)))

    shared = (places, qg_mine, qg_other, received, weight_mine, bias_pair, row_count)
    *earlier, bias_right, bias_left, bias_rest = attend(0, *shared, ())
    (qa_own, qa_away, kv_grads, bias_right_2, bias_left_2, bias_rest_2) = attend(1, *shared, tuple(earlier))

    def along_row(array, turn, side):
        pairs = []
        for index in range(row_count):
            high, low = index // row_ring, index % row_ring
            pairs.append((index, ((high + side) % 2) * row_ring + (low + turn) % row_ring))
        return lax.ppermute(array, "row", pairs)

    def added(*parts):
        return sum(part.astype(jnp.float32) for part in parts)

    def ring_onward(rest, from_left, from_right):
        onward = jnp.concatenate([added(rest[4:6], from_left).astype(jnp.bfloat16), rest[6:8]])
        backward = jnp.concatenate([rest[8:10], added(rest[10:], from_right).astype(jnp.bfloat16)])
        return along_row(onward, 1, 0), along_row(backward, -1, 0)

    from_left, from_right = along_row(bias_right, 1, 0), along_row(bias_left, -1, 0)
    second = (bias_right_2, bias_left_2, bias_rest_2, kv_grads, qa_own, qa_away)
    from_left, from_right, bias_rest, second = lax.optimization_barrier(
        (from_left, from_right, bias_rest, second)
    )
    bias_right_2, bias_left_2, bias_rest_2, kv_grads, qa_own, qa_away = second
    qa_back = swapped(qa_away)
    from_left, from_right, bias_right_2, bias_left_2, qa_back = lax.optimization_barrier(
        (from_left, from_right, bias_right_2, bias_left_2, qa_back)
    )
    from_left, from_right = ring_onward(bias_rest, from_left, from_right)
    sums = added(bias_rest[:4], from_left, from_right)
    from_left, from_right = along_row(bias_right_2, 1, 0), along_row(bias_left_2, -1, 0)
    kv_parts = lax.all_to_all(kv_grads, "col", 0, 0, tiled=True)
    kv_parts = kv_parts.reshape((devices // 2, 2) + kv_parts.shape[1:])
    kv_sum = jnp.sum(kv_parts.astype(jnp.float32), axis=0)
    key_gradient = jnp.concatenate([kv_sum[0, ..., :half], kv_sum[1, ..., :half]], axis=2) * scaling
    key_gradient = key_gradient.astype(jnp.bfloat16)
    value_gradient = jnp.concatenate([kv_sum[0, ..., half:], kv_sum[1, ..., half:]], axis=2)
    value_gradient = value_gradient.astype(jnp.bfloat16)
    from_left, from_right = ring_onward(bias_rest_2, from_left, from_right)
    sums = jnp.stack([sums, added(bias_rest_2[:4], from_left, from_right)], axis=1)
    query_gradient = in_order(qa_own[..., :half], qa_back[..., :half], 2)
    gate_gradient = in_order(qa_own[..., half:], qa_back[..., half:], 2)
    low_sums = sums.astype(jnp.bfloat16)
    diagonal = []
    for index in range(row_count * devices):
        up = (index // devices + row_ring) % row_count
        diagonal.append((index, up * devices + (index % devices ^ 1)))
    from_high, from_core, from_diagonal, key_gradient, value_gradient = lax.optimization_barrier((
        along_row(low_sums[2], 0, 1),
        swapped(low_sums[1]),
        lax.ppermute(low_sums[3], ("row", "col"), diagonal),
        key_gradient,
        value_gradient,
    ))
    bias_own = added(sums[0], from_high)
    bias_away = added(from_core, from_diagonal)
    bias_gradient = in_order(bias_own, bias_away, 0)
    return (query_gradient, key_gradient, value_gradient, gate_gradient, bias_gradient)


def solution(mesh):
    placed = (
        P("row", "col", None),
        P("row", "col", None),
        P("row", "col", None),
        P("row", "col", None),
        P(None, "col", None),
        P("row", "col"),
        P(),
        P("row", "col", None),
    )
    return jax.shard_map(
        local,
        mesh=mesh,
        in_specs=placed,
        out_specs=(
            P("row", "col", None),
            P("row", "col", None),
            P("row", "col", None),
            P("row", "col", None),
            P(None, "col", "row"),
        ),
        check_vma=False,
    )
```

```python
import functools
import math

import jax
import jax.numpy as jnp
from jax import lax
from jax.experimental import pallas as pl
from jax.experimental.pallas import tpu as pltpu
from jax.sharding import PartitionSpec as P

HEADS = 4
NEG_FILL = -1000000000.0
LOG2E = math.log2(math.e)
CHUNK = 16
UNROLL = 12
MASK_ROWS = 16
PIECES = 8
VMEM_WIDE = 60 * 1024 * 1024


def attention_kernel(head, *refs):
    place_ref, qg_mine_ref, qg_other_ref, kv_ref, mask_ref, cotangent_ref, weight_ref, bias_ref = refs[:8]
    earlier = refs[8 : 8 + 3 * head]
    qa_own_ref, qa_away_ref, dkv_ref, right_out_ref, left_out_ref, rest_out_ref = refs[8 + 3 * head :][:6]
    gated_ref, cap_ref, s_ref, b2_ref, acc_ref, dp_ref, de_ref, row_ref, dbias_ref = refs[14 + 3 * head :]
    step = pl.program_id(0)
    last = pl.num_programs(0) - 1
    queries, keys = bias_ref.shape
    half = queries // 2
    head_width = qg_mine_ref.shape[2] // 4
    core = place_ref[PIECES]
    scaling = 1.0 / math.sqrt(head_width)

    @pl.when(step == 0)
    def _():
        def fill(index, carry):
            part = pl.ds(index * CHUNK, CHUNK)
            b2_ref[part, :] = bias_ref[part, :].astype(jnp.float32) * LOG2E
            acc_ref[part, :] = jnp.zeros((CHUNK, keys), jnp.float32)
            return carry

        lax.fori_loop(0, queries // CHUNK, fill, 0)
        sources, _, lanes = cotangent_ref.shape
        cotangent = cotangent_ref[...].astype(jnp.float32)
        cotangent = cotangent.reshape(sources, 2, cap_ref.shape[0], lanes // sources, lanes)
        for column in range(cotangent.shape[2]):
            for side in range(2):
                part = cotangent[:, side, column].reshape(lanes, lanes).astype(jnp.bfloat16)
                gated = jnp.dot(weight_ref[...], part, preferred_element_type=jnp.float32)
                gated_ref[column, side * half : (side + 1) * half] = gated.T[:half]
        masks = mask_ref[...].astype(jnp.float32)
        for column in range(cap_ref.shape[0]):
            pieces = [
                masks[source, column : column + 1, :half] for source in range(masks.shape[0])
            ]
            cap_ref[column] = jnp.where(
                jnp.concatenate(pieces, axis=1) > 0.5, 1e30, NEG_FILL * LOG2E
            )

    lane = lax.broadcasted_iota(jnp.int32, (queries, 4 * head_width), 1)
    transposed = (((1,), (1,)), ((), ()))
    is_query = (lane >= head * head_width) & (lane < (head + 1) * head_width)
    is_gate = (lane >= (head + 2) * head_width) & (lane < (head + 3) * head_width)
    kvs, query_rows, grad_rows, slopes = [], [], [], []
    for unit in range(2):
        kvs.append(kv_ref[:, unit * half : (unit + 1) * half, :].reshape(keys, 4 * head_width))
        mine = qg_mine_ref[unit]
        other = qg_other_ref[unit]
        query_gate = jnp.concatenate(
            [jnp.where(core == 0, mine, other), jnp.where(core == 0, other, mine)], axis=0
        )
        sigma = jax.nn.sigmoid(query_gate.astype(jnp.float32))
        gated_grad = gated_ref[2 * step + unit] * sigma
        slopes.append(gated_grad * (1.0 - sigma))
        zero = jnp.zeros_like(query_gate)
        query_rows.append(jnp.where(is_query, query_gate, zero))
        grad_rows.append(jnp.where(is_gate, gated_grad.astype(jnp.bfloat16), zero))

    def scores_of(unit):
        s_ref[unit * queries : (unit + 1) * queries, :] = lax.dot_general(
            query_rows[unit], kvs[unit], transposed, preferred_element_type=jnp.float32
        )

    def soften(unit):
        cap = cap_ref[2 * step + unit]

        def one(index, carry):
            inner = index * CHUNK
            part = pl.ds(unit * queries + inner, CHUNK)
            scores = s_ref[part, :] * (scaling * LOG2E) + b2_ref[pl.ds(inner, CHUNK), :]
            scores = jnp.minimum(scores, cap)
            weights = jnp.exp2(scores - jnp.max(scores, axis=1, keepdims=True))
            row_ref[part, :] = jnp.broadcast_to(jnp.sum(weights, axis=1, keepdims=True), (CHUNK, 128))
            de_ref[pl.ds((2 * unit + 1) * queries + inner, CHUNK), :] = weights.astype(jnp.bfloat16)
            return carry

        lax.fori_loop(0, queries // CHUNK, one, 0, unroll=UNROLL)

    def cotangents(unit):
        part = slice(unit * queries, (unit + 1) * queries)
        weights_low = de_ref[(2 * unit + 1) * queries : (2 * unit + 2) * queries, :]
        inverse = 1.0 / row_ref[part, :]
        attended = jnp.dot(weights_low, kvs[unit], preferred_element_type=jnp.float32) * inverse
        grad_wide = grad_rows[unit].astype(jnp.float32)
        delta = jnp.sum(grad_wide * attended, axis=1, keepdims=True)
        row_ref[part, :] = delta * inverse
        grad_scaled = (grad_wide * inverse).astype(jnp.bfloat16)
        dp_ref[part, :] = lax.dot_general(
            grad_scaled, kvs[unit], transposed, preferred_element_type=jnp.float32
        )
        return attended, grad_scaled

    def backward(unit):
        def one(index, carry):
            inner = index * CHUNK
            part = pl.ds(unit * queries + inner, CHUNK)
            weights = de_ref[pl.ds((2 * unit + 1) * queries + inner, CHUNK), :].astype(jnp.float32)
            score_grad = weights * (dp_ref[part, :] - row_ref[part, :1])
            acc_ref[pl.ds(inner, CHUNK), :] += score_grad
            de_ref[pl.ds(2 * unit * queries + inner, CHUNK), :] = score_grad.astype(jnp.bfloat16)
            return carry

        lax.fori_loop(0, queries // CHUNK, one, 0, unroll=UNROLL)

    def finish(unit, attended, grad_scaled):
        low = de_ref[2 * unit * queries : (2 * unit + 1) * queries, :]
        query = jnp.dot(low, kvs[unit], preferred_element_type=jnp.float32) * scaling
        merged = jnp.where(is_query, query, jnp.where(is_gate, attended * slopes[unit], 0.0))
        own = jnp.where(core == 0, merged[:half], merged[half:])
        away = jnp.where(core == 0, merged[half:], merged[:half])
        sides = jnp.concatenate([query_rows[unit], grad_scaled], axis=0)
        key_value = lax.dot_general(
            sides,
            de_ref[2 * unit * queries : (2 * unit + 2) * queries, :],
            (((0,), (0,)), ((), ())),
            preferred_element_type=jnp.float32,
        )
        keys_here = key_value[head * head_width : (head + 1) * head_width]
        values_here = key_value[(head + 2) * head_width : (head + 3) * head_width]
        if earlier:
            own = own + earlier[0][unit].astype(jnp.float32)
            away = away + earlier[1][unit].astype(jnp.float32)
            passed = earlier[2][unit].astype(jnp.float32)
            key_value = jnp.concatenate(
                [passed[:head_width], keys_here, passed[head_width:], values_here], axis=0
            )
            key_value = key_value.T.reshape(dkv_ref.shape[0], half, 4 * head_width)
            dkv_ref[:, unit] = key_value.astype(jnp.bfloat16)
        else:
            dkv_ref[unit] = jnp.concatenate([keys_here, values_here], axis=0).astype(jnp.bfloat16)
        qa_own_ref[unit] = own.astype(jnp.bfloat16)
        qa_away_ref[unit] = away.astype(jnp.bfloat16)

    scores_of(0)
    scores_of(1)
    soften(0)
    first = cotangents(0)
    soften(1)
    second = cotangents(1)
    backward(0)
    finish(0, *first)
    backward(1)
    finish(1, *second)

    @pl.when(step == last)
    def _():
        width = dbias_ref.shape[2]
        for piece in range(PIECES):
            for side in range(2):
                part = acc_ref[side * half : (side + 1) * half, piece * width : (piece + 1) * width]
                target = 2 * place_ref[piece] + (side + core) % 2
                dbias_ref[target] = part.astype(jnp.bfloat16)
        right_out_ref[...] = dbias_ref[8 : 8 + right_out_ref.shape[0]]
        left_out_ref[...] = dbias_ref[10:12]
        rest_out_ref[:8] = dbias_ref[:8]
        rest_out_ref[8:] = dbias_ref[12:]


def prepare_kernel(key_ref, value_ref, mask_ref, cotangent_ref, packed_ref):
    columns, tokens, channels = key_ref.shape
    half = channels // 2
    devices = packed_ref.shape[0]
    pairs = columns * tokens
    rows = cotangent_ref.shape[0] * cotangent_ref.shape[1]
    mask = mask_ref[...].astype(jnp.float32)
    mask = jnp.concatenate([mask, jnp.zeros((columns, channels - tokens), jnp.float32)], axis=1)
    filler = jnp.zeros((MASK_ROWS - columns, channels), jnp.float32)
    mask = jnp.concatenate([mask, filler], axis=0).astype(jnp.bfloat16)
    for column in range(columns):
        key = key_ref[column]
        value = value_ref[column]
        sides = [
            jnp.concatenate([key[:, :half], value[:, :half]], axis=1),
            jnp.concatenate([key[:, half:], value[:, half:]], axis=1),
        ]
        for device in range(devices):
            packed_ref[device, column * tokens : (column + 1) * tokens, :] = sides[device % 2]
    cotangent = cotangent_ref[...].astype(jnp.float32).reshape(rows, cotangent_ref.shape[2])
    filler = jnp.zeros((rows, channels - tokens), jnp.float32)
    for device in range(devices):
        packed_ref[device, pairs + 2 * rows :, :] = mask
        part = cotangent[:, device * tokens : (device + 1) * tokens]
        part = jnp.concatenate([part, filler], axis=1).astype(jnp.bfloat16)
        start = pairs + device % 2 * rows
        packed_ref[device, start : start + rows, :] = part
        packed_ref[device ^ 1, start : start + rows, :] = part


def prepare(key, value, mask, cotangent, devices):
    columns, tokens, channels = key.shape
    rows = columns * tokens + 2 * cotangent.shape[0] * cotangent.shape[1] + MASK_ROWS

    def whole(shape):
        return pl.BlockSpec(shape, lambda i: (0,) * len(shape))

    out = (devices, rows, channels)
    return pl.pallas_call(
        prepare_kernel,
        grid=(1,),
        in_specs=[whole(key.shape), whole(value.shape), whole(mask.shape), whole(cotangent.shape)],
        out_specs=whole(out),
        out_shape=jax.ShapeDtypeStruct(out, jnp.bfloat16),
        compiler_params=pltpu.CompilerParams(vmem_limit_bytes=VMEM_WIDE),
        name="prepare_exchange",
    )(key, value, mask, cotangent)


def attend(head, places, mine, other, received, weight, bias, row_count, earlier):
    columns, tokens, lanes = mine.shape
    queries, keys = bias.shape[0] // 2, bias.shape[1]
    width = keys // row_count
    devices = received.shape[0]
    mask_place = received.shape[1] // MASK_ROWS - 1
    cotangent_rows = 2 * columns * lanes // devices
    cotangent_place = columns * tokens // cotangent_rows
    work = columns * queries * keys

    def whole(shape):
        return pl.BlockSpec(shape, lambda j, places: (0,) * len(shape))

    column_spec = pl.BlockSpec((2, tokens, lanes), lambda j, places: (j, 0, 0))
    part_spec = pl.BlockSpec((2, lanes // 2, keys), lambda j, places: (j, 0, 0))
    part_shape = (columns, lanes // 2, keys)
    if earlier:
        grad_spec = pl.BlockSpec((devices, 2, tokens, lanes), lambda j, places: (0, j, 0, 0))
        grad_shape = (devices,) + mine.shape
    else:
        grad_spec, grad_shape = part_spec, part_shape
    piece = (tokens, width)
    return pl.pallas_call(
        functools.partial(attention_kernel, head),
        grid_spec=pltpu.PrefetchScalarGridSpec(
            num_scalar_prefetch=1,
            grid=(columns // 2,),
            in_specs=[
                column_spec,
                column_spec,
                pl.BlockSpec((devices, 2 * tokens, lanes), lambda j, places: (0, j, 0)),
                pl.BlockSpec((devices, MASK_ROWS, lanes), lambda j, places: (0, mask_place, 0)),
                pl.BlockSpec(
                    (devices, cotangent_rows, lanes), lambda j, places: (0, cotangent_place, 0)
                ),
                whole(weight.shape),
                pl.BlockSpec((queries, keys), lambda j, places: (head, 0)),
            ]
            + [column_spec, column_spec, part_spec][: len(earlier)],
            out_specs=[
                column_spec,
                column_spec,
                grad_spec,
                whole((2 if earlier else 4,) + piece),
                whole((2,) + piece),
                whole((12,) + piece),
            ],
            scratch_shapes=[
                pltpu.VMEM((columns, queries, lanes), jnp.float32),
                pltpu.VMEM((columns, 1, keys), jnp.float32),
                pltpu.VMEM((2 * queries, keys), jnp.float32),
                pltpu.VMEM((queries, keys), jnp.float32),
                pltpu.VMEM((queries, keys), jnp.float32),
                pltpu.VMEM((2 * queries, keys), jnp.float32),
                pltpu.VMEM((4 * queries, keys), jnp.bfloat16),
                pltpu.VMEM((2 * queries, 128), jnp.float32),
                pltpu.VMEM((16,) + piece, jnp.bfloat16),
            ],
        ),
        out_shape=[
            jax.ShapeDtypeStruct(mine.shape, jnp.bfloat16),
            jax.ShapeDtypeStruct(mine.shape, jnp.bfloat16),
            jax.ShapeDtypeStruct(grad_shape, jnp.bfloat16),
            jax.ShapeDtypeStruct((2 if earlier else 4,) + piece, jnp.bfloat16),
            jax.ShapeDtypeStruct((2,) + piece, jnp.bfloat16),
            jax.ShapeDtypeStruct((12,) + piece, jnp.bfloat16),
        ],
        compiler_params=pltpu.CompilerParams(vmem_limit_bytes=48 * 1024 * 1024),
        cost_estimate=pl.CostEstimate(flops=12 * 128 * work, bytes_accessed=16 * 2**20, transcendentals=work),
        name="attention_head",
    )(places, mine, other, received, received, received, weight, bias, *earlier)


def local(
    query_vectors,
    key_vectors,
    value_vectors,
    gate_logits,
    pair_bias,
    pair_mask,
    output_weight,
    output_cotangent,
):
    columns, tokens, channels = query_vectors.shape
    half = channels // 2
    devices = lax.axis_size("col")
    row_count = lax.axis_size("row")
    core = lax.axis_index("col") % 2
    scaling = 1.0 / math.sqrt(channels // HEADS)
    swap = [(index, index ^ 1) for index in range(devices)]
    keys = pair_bias.shape[2]

    def mine_other(array, axis):
        size = array.shape[axis] // 2
        low = lax.slice_in_dim(array, 0, size, axis=axis)
        high = lax.slice_in_dim(array, size, 2 * size, axis=axis)
        return jnp.where(core == 0, low, high), jnp.where(core == 0, high, low)

    def in_order(mine, other, axis):
        return jnp.where(
            core == 0,
            jnp.concatenate([mine, other], axis=axis),
            jnp.concatenate([other, mine], axis=axis),
        )

    def swapped(array):
        return lax.ppermute(array, "col", swap)

    bias_mine, bias_other = mine_other(pair_bias, 0)
    bias_pair = in_order(bias_mine, swapped(bias_other), 1).reshape(-1, keys)

    packed = prepare(key_vectors, value_vectors, pair_mask, output_cotangent, devices)
    received = lax.all_to_all(packed, "col", 0, 0, tiled=True)
    place = lax.axis_index("row")
    row_ring = row_count // 2
    places = [
        2 * ((index % row_ring - place) % row_ring) + (index // row_ring - place // row_ring) % 2
        for index in range(row_count)
    ]
    places.append(core)
    places = jnp.stack(places).astype(jnp.int32)

    query_mine, query_other = mine_other(query_vectors, 2)
    gate_mine, gate_other = mine_other(gate_logits, 2)
    qg_mine = jnp.concatenate([query_mine, gate_mine], axis=2)
    qg_other = swapped(jnp.concatenate([query_other, gate_other], axis=2))
    weight_mine, _ = mine_other(output_weight, 0)
    weight_mine = jnp.pad(weight_mine, ((half, 0), (0, 0)))

    shared = (places, qg_mine, qg_other, received, weight_mine, bias_pair, row_count)
    *earlier, bias_right, _, bias_rest = attend(0, *shared, ())
    (qa_own, qa_away, kv_grads, bias_right_2, bias_left_2, bias_rest_2) = attend(1, *shared, tuple(earlier))

    def along_row(array, turn, side):
        pairs = []
        for index in range(row_count):
            high, low = index // row_ring, index % row_ring
            pairs.append((index, ((high + side) % 2) * row_ring + (low + turn) % row_ring))
        return lax.ppermute(array, "row", pairs)

    def added(*parts):
        return sum(part.astype(jnp.float32) for part in parts)

    def ring_onward(rest, from_left, from_right):
        onward = jnp.concatenate([added(rest[4:6], from_left).astype(jnp.bfloat16), rest[6:8]])
        backward = jnp.concatenate([rest[8:10], added(rest[10:], from_right).astype(jnp.bfloat16)])
        return along_row(onward, 1, 0), along_row(backward, -1, 0)

    from_left = along_row(bias_right, 1, 0)
    second = (bias_right_2, bias_left_2, bias_rest_2, kv_grads, qa_own, qa_away)
    from_left, bias_rest, second = lax.optimization_barrier((from_left, bias_rest, second))
    bias_right_2, bias_left_2, bias_rest_2, kv_grads, qa_own, qa_away = second
    qa_back = swapped(qa_away)
    from_left, bias_right_2, bias_left_2, qa_back = lax.optimization_barrier(
        (from_left, bias_right_2, bias_left_2, qa_back)
    )
    onward = added(bias_rest[4:8], from_left).astype(jnp.bfloat16)
    from_left, from_right = along_row(onward, 1, 0), along_row(bias_rest[8:], -1, 0)
    sums = added(bias_rest[:4], from_left, from_right)
    from_left, from_right = along_row(bias_right_2, 1, 0), along_row(bias_left_2, -1, 0)
    kv_parts = lax.all_to_all(kv_grads, "col", 0, 0, tiled=True)
    kv_parts = kv_parts.reshape((devices // 2, 2) + kv_parts.shape[1:])
    kv_sum = jnp.sum(kv_parts.astype(jnp.float32), axis=0)
    key_gradient = jnp.concatenate([kv_sum[0, ..., :half], kv_sum[1, ..., :half]], axis=2) * scaling
    key_gradient = key_gradient.astype(jnp.bfloat16)
    value_gradient = jnp.concatenate([kv_sum[0, ..., half:], kv_sum[1, ..., half:]], axis=2)
    value_gradient = value_gradient.astype(jnp.bfloat16)
    from_left, from_right = ring_onward(bias_rest_2, from_left, from_right)
    sums = jnp.stack([sums, added(bias_rest_2[:4], from_left, from_right)], axis=1)
    query_gradient = in_order(qa_own[..., :half], qa_back[..., :half], 2)
    gate_gradient = in_order(qa_own[..., half:], qa_back[..., half:], 2)
    low_sums = sums.astype(jnp.bfloat16)
    diagonal = []
    for index in range(row_count * devices):
        up = (index // devices + row_ring) % row_count
        diagonal.append((index, up * devices + (index % devices ^ 1)))
    from_high, from_core, from_diagonal, key_gradient, value_gradient = lax.optimization_barrier((
        along_row(low_sums[2], 0, 1),
        swapped(low_sums[1]),
        lax.ppermute(low_sums[3], ("row", "col"), diagonal),
        key_gradient,
        value_gradient,
    ))
    bias_own = added(sums[0], from_high)
    bias_away = added(from_core, from_diagonal)
    bias_gradient = in_order(bias_own, bias_away, 0)
    return (query_gradient, key_gradient, value_gradient, gate_gradient, bias_gradient)


def solution(mesh):
    placed = (
        P("row", "col", None),
        P("row", "col", None),
        P("row", "col", None),
        P("row", "col", None),
        P(None, "col", None),
        P("row", "col"),
        P(),
        P("row", "col", None),
    )
    return jax.shard_map(
        local,
        mesh=mesh,
        in_specs=placed,
        out_specs=(
            P("row", "col", None),
            P("row", "col", None),
            P("row", "col", None),
            P("row", "col", None),
            P(None, "col", "row"),
        ),
        check_vma=False,
    )
```

```python
import functools
import math

import jax
import jax.numpy as jnp
from jax import lax
from jax.experimental import pallas as pl
from jax.experimental.pallas import tpu as pltpu
from jax.sharding import PartitionSpec as P

HEADS = 4
NEG_FILL = -1000000000.0
LOG2E = math.log2(math.e)
CHUNK = 16
UNROLL = 12
MASK_ROWS = 16
PIECES = 8
VMEM_WIDE = 60 * 1024 * 1024


def attention_kernel(head, *refs):
    place_ref, qg_mine_ref, qg_other_ref, kv_ref, mask_ref, cotangent_ref, weight_ref, bias_ref = refs[:8]
    earlier = refs[8 : 8 + 3 * head]
    qa_own_ref, qa_away_ref, dkv_ref, right_out_ref, left_out_ref, rest_out_ref = refs[8 + 3 * head :][:6]
    gated_ref, cap_ref, s_ref, b2_ref, acc_ref, dp_ref, de_ref, row_ref, dbias_ref = refs[14 + 3 * head :]
    step = pl.program_id(0)
    last = pl.num_programs(0) - 1
    queries, keys = bias_ref.shape
    half = queries // 2
    head_width = qg_mine_ref.shape[2] // 4
    core = place_ref[PIECES]
    scaling = 1.0 / math.sqrt(head_width)

    @pl.when(step == 0)
    def _():
        def fill(index, carry):
            part = pl.ds(index * CHUNK, CHUNK)
            b2_ref[part, :] = bias_ref[part, :].astype(jnp.float32) * LOG2E
            acc_ref[part, :] = jnp.zeros((CHUNK, keys), jnp.float32)
            return carry

        lax.fori_loop(0, queries // CHUNK, fill, 0, unroll=UNROLL)
        sources, _, lanes = cotangent_ref.shape
        cotangent = cotangent_ref[...].astype(jnp.float32)
        cotangent = cotangent.reshape(sources, 2, cap_ref.shape[0], lanes // sources, lanes)
        for column in range(cotangent.shape[2]):
            for side in range(2):
                part = cotangent[:, side, column].reshape(lanes, lanes).astype(jnp.bfloat16)
                gated = jnp.dot(weight_ref[...], part, preferred_element_type=jnp.float32)
                gated_ref[column, side * half : (side + 1) * half] = gated.T[:half]
        masks = mask_ref[...].astype(jnp.float32)
        for column in range(cap_ref.shape[0]):
            pieces = [
                masks[source, column : column + 1, :half] for source in range(masks.shape[0])
            ]
            cap_ref[column] = jnp.where(
                jnp.concatenate(pieces, axis=1) > 0.5, 1e30, NEG_FILL * LOG2E
            )

    lane = lax.broadcasted_iota(jnp.int32, (queries, 4 * head_width), 1)
    transposed = (((1,), (1,)), ((), ()))
    is_query = (lane >= head * head_width) & (lane < (head + 1) * head_width)
    is_gate = (lane >= (head + 2) * head_width) & (lane < (head + 3) * head_width)
    kvs, query_rows, grad_rows, slopes = [], [], [], []
    for unit in range(2):
        kvs.append(kv_ref[:, unit * half : (unit + 1) * half, :].reshape(keys, 4 * head_width))
        mine = qg_mine_ref[unit]
        other = qg_other_ref[unit]
        query_gate = jnp.concatenate(
            [jnp.where(core == 0, mine, other), jnp.where(core == 0, other, mine)], axis=0
        )
        sigma = jax.nn.sigmoid(query_gate.astype(jnp.float32))
        gated_grad = gated_ref[2 * step + unit] * sigma
        slopes.append(gated_grad * (1.0 - sigma))
        zero = jnp.zeros_like(query_gate)
        query_rows.append(jnp.where(is_query, query_gate, zero))
        grad_rows.append(jnp.where(is_gate, gated_grad.astype(jnp.bfloat16), zero))

    def scores_of(unit):
        s_ref[unit * queries : (unit + 1) * queries, :] = lax.dot_general(
            query_rows[unit], kvs[unit], transposed, preferred_element_type=jnp.float32
        )

    def soften(unit):
        cap = cap_ref[2 * step + unit]

        def one(index, carry):
            inner = index * CHUNK
            part = pl.ds(unit * queries + inner, CHUNK)
            scores = s_ref[part, :] * (scaling * LOG2E) + b2_ref[pl.ds(inner, CHUNK), :]
            scores = jnp.minimum(scores, cap)
            weights = jnp.exp2(scores - jnp.max(scores, axis=1, keepdims=True))
            row_ref[part, :] = jnp.broadcast_to(jnp.sum(weights, axis=1, keepdims=True), (CHUNK, 128))
            de_ref[pl.ds((2 * unit + 1) * queries + inner, CHUNK), :] = weights.astype(jnp.bfloat16)
            return carry

        lax.fori_loop(0, queries // CHUNK, one, 0, unroll=UNROLL)

    def cotangents(unit):
        part = slice(unit * queries, (unit + 1) * queries)
        weights_low = de_ref[(2 * unit + 1) * queries : (2 * unit + 2) * queries, :]
        inverse = 1.0 / row_ref[part, :]
        attended = jnp.dot(weights_low, kvs[unit], preferred_element_type=jnp.float32) * inverse
        grad_wide = grad_rows[unit].astype(jnp.float32)
        delta = jnp.sum(grad_wide * attended, axis=1, keepdims=True)
        row_ref[part, :] = delta * inverse
        grad_scaled = (grad_wide * inverse).astype(jnp.bfloat16)
        dp_ref[part, :] = lax.dot_general(
            grad_scaled, kvs[unit], transposed, preferred_element_type=jnp.float32
        )
        return attended, grad_scaled

    def backward(unit):
        def one(index, carry):
            inner = index * CHUNK
            part = pl.ds(unit * queries + inner, CHUNK)
            weights = de_ref[pl.ds((2 * unit + 1) * queries + inner, CHUNK), :].astype(jnp.float32)
            score_grad = weights * (dp_ref[part, :] - row_ref[part, :1])
            acc_ref[pl.ds(inner, CHUNK), :] += score_grad
            de_ref[pl.ds(2 * unit * queries + inner, CHUNK), :] = score_grad.astype(jnp.bfloat16)
            return carry

        lax.fori_loop(0, queries // CHUNK, one, 0, unroll=UNROLL)

    def finish(unit, attended, grad_scaled):
        low = de_ref[2 * unit * queries : (2 * unit + 1) * queries, :]
        query = jnp.dot(low, kvs[unit], preferred_element_type=jnp.float32) * scaling
        merged = jnp.where(is_query, query, jnp.where(is_gate, attended * slopes[unit], 0.0))
        own = jnp.where(core == 0, merged[:half], merged[half:])
        away = jnp.where(core == 0, merged[half:], merged[:half])
        sides = jnp.concatenate([query_rows[unit], grad_scaled], axis=0)
        key_value = lax.dot_general(
            sides,
            de_ref[2 * unit * queries : (2 * unit + 2) * queries, :],
            (((0,), (0,)), ((), ())),
            preferred_element_type=jnp.float32,
        )
        keys_here = key_value[head * head_width : (head + 1) * head_width]
        values_here = key_value[(head + 2) * head_width : (head + 3) * head_width]
        if earlier:
            own = own + earlier[0][unit].astype(jnp.float32)
            away = away + earlier[1][unit].astype(jnp.float32)
            passed = earlier[2][unit].astype(jnp.float32)
            key_value = jnp.concatenate(
                [passed[:head_width], keys_here, passed[head_width:], values_here], axis=0
            )
            key_value = key_value.T.reshape(dkv_ref.shape[0], half, 4 * head_width)
            dkv_ref[:, unit] = key_value.astype(jnp.bfloat16)
        else:
            dkv_ref[unit] = jnp.concatenate([keys_here, values_here], axis=0).astype(jnp.bfloat16)
        qa_own_ref[unit] = own.astype(jnp.bfloat16)
        qa_away_ref[unit] = away.astype(jnp.bfloat16)

    scores_of(0)
    scores_of(1)
    soften(0)
    first = cotangents(0)
    soften(1)
    second = cotangents(1)
    backward(0)
    finish(0, *first)
    backward(1)
    finish(1, *second)

    @pl.when(step == last)
    def _():
        width = dbias_ref.shape[2]
        for piece in range(PIECES):
            for side in range(2):
                part = acc_ref[side * half : (side + 1) * half, piece * width : (piece + 1) * width]
                target = 2 * place_ref[piece] + (side + core) % 2
                dbias_ref[target] = part.astype(jnp.bfloat16)
        right_out_ref[...] = dbias_ref[8 : 8 + right_out_ref.shape[0]]
        left_out_ref[...] = dbias_ref[10:12]
        rest_out_ref[:8] = dbias_ref[:8]
        rest_out_ref[8:] = dbias_ref[12:]


def prepare_kernel(key_ref, value_ref, mask_ref, cotangent_ref, packed_ref):
    columns, tokens, channels = key_ref.shape
    half = channels // 2
    devices = packed_ref.shape[0]
    pairs = columns * tokens
    rows = cotangent_ref.shape[0] * cotangent_ref.shape[1]
    mask = mask_ref[...].astype(jnp.float32)
    mask = jnp.concatenate([mask, jnp.zeros((columns, channels - tokens), jnp.float32)], axis=1)
    filler = jnp.zeros((MASK_ROWS - columns, channels), jnp.float32)
    mask = jnp.concatenate([mask, filler], axis=0).astype(jnp.bfloat16)
    for column in range(columns):
        key = key_ref[column]
        value = value_ref[column]
        sides = [
            jnp.concatenate([key[:, :half], value[:, :half]], axis=1),
            jnp.concatenate([key[:, half:], value[:, half:]], axis=1),
        ]
        for device in range(devices):
            packed_ref[device, column * tokens : (column + 1) * tokens, :] = sides[device % 2]
    cotangent = cotangent_ref[...].astype(jnp.float32).reshape(rows, cotangent_ref.shape[2])
    filler = jnp.zeros((rows, channels - tokens), jnp.float32)
    for device in range(devices):
        packed_ref[device, pairs + 2 * rows :, :] = mask
        part = cotangent[:, device * tokens : (device + 1) * tokens]
        part = jnp.concatenate([part, filler], axis=1).astype(jnp.bfloat16)
        start = pairs + device % 2 * rows
        packed_ref[device, start : start + rows, :] = part
        packed_ref[device ^ 1, start : start + rows, :] = part


def prepare(key, value, mask, cotangent, devices):
    columns, tokens, channels = key.shape
    rows = columns * tokens + 2 * cotangent.shape[0] * cotangent.shape[1] + MASK_ROWS

    def whole(shape):
        return pl.BlockSpec(shape, lambda i: (0,) * len(shape))

    out = (devices, rows, channels)
    return pl.pallas_call(
        prepare_kernel,
        grid=(1,),
        in_specs=[whole(key.shape), whole(value.shape), whole(mask.shape), whole(cotangent.shape)],
        out_specs=whole(out),
        out_shape=jax.ShapeDtypeStruct(out, jnp.bfloat16),
        compiler_params=pltpu.CompilerParams(vmem_limit_bytes=VMEM_WIDE),
        name="prepare_exchange",
    )(key, value, mask, cotangent)


def attend(head, places, mine, other, received, weight, bias, row_count, earlier):
    columns, tokens, lanes = mine.shape
    queries, keys = bias.shape[0] // 2, bias.shape[1]
    width = keys // row_count
    devices = received.shape[0]
    mask_place = received.shape[1] // MASK_ROWS - 1
    cotangent_rows = 2 * columns * lanes // devices
    cotangent_place = columns * tokens // cotangent_rows
    work = columns * queries * keys

    def whole(shape):
        return pl.BlockSpec(shape, lambda j, places: (0,) * len(shape))

    column_spec = pl.BlockSpec((2, tokens, lanes), lambda j, places: (j, 0, 0))
    part_spec = pl.BlockSpec((2, lanes // 2, keys), lambda j, places: (j, 0, 0))
    part_shape = (columns, lanes // 2, keys)
    if earlier:
        grad_spec = pl.BlockSpec((devices, 2, tokens, lanes), lambda j, places: (0, j, 0, 0))
        grad_shape = (devices,) + mine.shape
    else:
        grad_spec, grad_shape = part_spec, part_shape
    piece = (tokens, width)
    return pl.pallas_call(
        functools.partial(attention_kernel, head),
        grid_spec=pltpu.PrefetchScalarGridSpec(
            num_scalar_prefetch=1,
            grid=(columns // 2,),
            in_specs=[
                column_spec,
                column_spec,
                pl.BlockSpec((devices, 2 * tokens, lanes), lambda j, places: (0, j, 0)),
                pl.BlockSpec((devices, MASK_ROWS, lanes), lambda j, places: (0, mask_place, 0)),
                pl.BlockSpec(
                    (devices, cotangent_rows, lanes), lambda j, places: (0, cotangent_place, 0)
                ),
                whole(weight.shape),
                pl.BlockSpec((queries, keys), lambda j, places: (head, 0)),
            ]
            + [column_spec, column_spec, part_spec][: len(earlier)],
            out_specs=[
                column_spec,
                column_spec,
                grad_spec,
                whole((2 if earlier else 4,) + piece),
                whole((2,) + piece),
                whole((12,) + piece),
            ],
            scratch_shapes=[
                pltpu.VMEM((columns, queries, lanes), jnp.float32),
                pltpu.VMEM((columns, 1, keys), jnp.float32),
                pltpu.VMEM((2 * queries, keys), jnp.float32),
                pltpu.VMEM((queries, keys), jnp.float32),
                pltpu.VMEM((queries, keys), jnp.float32),
                pltpu.VMEM((2 * queries, keys), jnp.float32),
                pltpu.VMEM((4 * queries, keys), jnp.bfloat16),
                pltpu.VMEM((2 * queries, 128), jnp.float32),
                pltpu.VMEM((16,) + piece, jnp.bfloat16),
            ],
        ),
        out_shape=[
            jax.ShapeDtypeStruct(mine.shape, jnp.bfloat16),
            jax.ShapeDtypeStruct(mine.shape, jnp.bfloat16),
            jax.ShapeDtypeStruct(grad_shape, jnp.bfloat16),
            jax.ShapeDtypeStruct((2 if earlier else 4,) + piece, jnp.bfloat16),
            jax.ShapeDtypeStruct((2,) + piece, jnp.bfloat16),
            jax.ShapeDtypeStruct((12,) + piece, jnp.bfloat16),
        ],
        compiler_params=pltpu.CompilerParams(vmem_limit_bytes=48 * 1024 * 1024),
        cost_estimate=pl.CostEstimate(flops=12 * 128 * work, bytes_accessed=16 * 2**20, transcendentals=work),
        name="attention_head",
    )(places, mine, other, received, received, received, weight, bias, *earlier)


def local(
    query_vectors,
    key_vectors,
    value_vectors,
    gate_logits,
    pair_bias,
    pair_mask,
    output_weight,
    output_cotangent,
):
    columns, tokens, channels = query_vectors.shape
    half = channels // 2
    devices = lax.axis_size("col")
    row_count = lax.axis_size("row")
    core = lax.axis_index("col") % 2
    scaling = 1.0 / math.sqrt(channels // HEADS)
    swap = [(index, index ^ 1) for index in range(devices)]
    keys = pair_bias.shape[2]

    def mine_other(array, axis):
        size = array.shape[axis] // 2
        low = lax.slice_in_dim(array, 0, size, axis=axis)
        high = lax.slice_in_dim(array, size, 2 * size, axis=axis)
        return jnp.where(core == 0, low, high), jnp.where(core == 0, high, low)

    def in_order(mine, other, axis):
        return jnp.where(
            core == 0,
            jnp.concatenate([mine, other], axis=axis),
            jnp.concatenate([other, mine], axis=axis),
        )

    def swapped(array):
        return lax.ppermute(array, "col", swap)

    bias_mine, bias_other = mine_other(pair_bias, 0)
    bias_pair = in_order(bias_mine, swapped(bias_other), 1).reshape(-1, keys)

    packed = prepare(key_vectors, value_vectors, pair_mask, output_cotangent, devices)
    received = lax.all_to_all(packed, "col", 0, 0, tiled=True)
    place = lax.axis_index("row")
    row_ring = row_count // 2
    places = [
        2 * ((index % row_ring - place) % row_ring) + (index // row_ring - place // row_ring) % 2
        for index in range(row_count)
    ]
    places.append(core)
    places = jnp.stack(places).astype(jnp.int32)

    query_mine, query_other = mine_other(query_vectors, 2)
    gate_mine, gate_other = mine_other(gate_logits, 2)
    qg_mine = jnp.concatenate([query_mine, gate_mine], axis=2)
    qg_other = swapped(jnp.concatenate([query_other, gate_other], axis=2))
    weight_mine, _ = mine_other(output_weight, 0)
    weight_mine = jnp.pad(weight_mine, ((half, 0), (0, 0)))

    shared = (places, qg_mine, qg_other, received, weight_mine, bias_pair, row_count)
    *earlier, bias_right, _, bias_rest = attend(0, *shared, ())
    (qa_own, qa_away, kv_grads, bias_right_2, bias_left_2, bias_rest_2) = attend(1, *shared, tuple(earlier))

    def along_row(array, turn, side):
        pairs = []
        for index in range(row_count):
            high, low = index // row_ring, index % row_ring
            pairs.append((index, ((high + side) % 2) * row_ring + (low + turn) % row_ring))
        return lax.ppermute(array, "row", pairs)

    def added(*parts):
        return sum(part.astype(jnp.float32) for part in parts)

    def ring_onward(rest, from_left, from_right):
        onward = jnp.concatenate([added(rest[4:6], from_left).astype(jnp.bfloat16), rest[6:8]])
        backward = jnp.concatenate([rest[8:10], added(rest[10:], from_right).astype(jnp.bfloat16)])
        return along_row(onward, 1, 0), along_row(backward, -1, 0)

    from_left = along_row(bias_right, 1, 0)
    second = (bias_right_2, bias_left_2, bias_rest_2, kv_grads, qa_own, qa_away)
    from_left, bias_rest, second = lax.optimization_barrier((from_left, bias_rest, second))
    bias_right_2, bias_left_2, bias_rest_2, kv_grads, qa_own, qa_away = second
    qa_back = swapped(qa_away)
    from_left, bias_right_2, bias_left_2, qa_back = lax.optimization_barrier(
        (from_left, bias_right_2, bias_left_2, qa_back)
    )
    onward = added(bias_rest[4:8], from_left).astype(jnp.bfloat16)
    from_left, from_right = along_row(onward, 1, 0), along_row(bias_rest[8:], -1, 0)
    sums = added(bias_rest[:4], from_left, from_right)
    from_left, from_right = along_row(bias_right_2, 1, 0), along_row(bias_left_2, -1, 0)
    kv_parts = lax.all_to_all(kv_grads, "col", 0, 0, tiled=True)
    kv_parts = kv_parts.reshape((devices // 2, 2) + kv_parts.shape[1:])
    kv_sum = jnp.sum(kv_parts.astype(jnp.float32), axis=0)
    key_gradient = jnp.concatenate([kv_sum[0, ..., :half], kv_sum[1, ..., :half]], axis=2) * scaling
    key_gradient = key_gradient.astype(jnp.bfloat16)
    value_gradient = jnp.concatenate([kv_sum[0, ..., half:], kv_sum[1, ..., half:]], axis=2)
    value_gradient = value_gradient.astype(jnp.bfloat16)
    from_left, from_right = ring_onward(bias_rest_2, from_left, from_right)
    sums = jnp.stack([sums, added(bias_rest_2[:4], from_left, from_right)], axis=1)
    query_gradient = in_order(qa_own[..., :half], qa_back[..., :half], 2)
    gate_gradient = in_order(qa_own[..., half:], qa_back[..., half:], 2)
    low_sums = sums.astype(jnp.bfloat16)
    diagonal = []
    for index in range(row_count * devices):
        up = (index // devices + row_ring) % row_count
        diagonal.append((index, up * devices + (index % devices ^ 1)))
    from_high, from_core, from_diagonal, key_gradient, value_gradient = lax.optimization_barrier((
        along_row(low_sums[2], 0, 1),
        swapped(low_sums[1]),
        lax.ppermute(low_sums[3], ("row", "col"), diagonal),
        key_gradient,
        value_gradient,
    ))
    bias_own = added(sums[0], from_high)
    bias_away = added(from_core, from_diagonal)
    bias_gradient = in_order(bias_own, bias_away, 0)
    return (query_gradient, key_gradient, value_gradient, gate_gradient, bias_gradient)


def solution(mesh):
    placed = (
        P("row", "col", None),
        P("row", "col", None),
        P("row", "col", None),
        P("row", "col", None),
        P(None, "col", None),
        P("row", "col"),
        P(),
        P("row", "col", None),
    )
    return jax.shard_map(
        local,
        mesh=mesh,
        in_specs=placed,
        out_specs=(
            P("row", "col", None),
            P("row", "col", None),
            P("row", "col", None),
            P("row", "col", None),
            P(None, "col", "row"),
        ),
        check_vma=False,
    )
```
